32 devices in a mesh: group: 4 (over y, core), dp: 8 (over z, x).
Axes of the slice: x: 2, y: 2, z: 4, core: 2. Of those that a mesh axis runs over, the one named last changes fastest.
Arguments:
- pixels: bfloat16 [1, 2, 128, 49, 3072], P(None, None, ('group', 'dp')), may hold values from -6 to 6
- counts: int32 [1, 2, 32], P(None, None, ('group', 'dp')), may hold values from 1 to 4, as said below
- labels: int32 [1, 2, 128], P(None, None, ('group', 'dp')), may hold values from 0 to 999
- text: bfloat16 [1000, 512], replicated, may hold values from -0.25 to 0.25
- master: float32 [22272, 768], P('dp')
- outer_momentum: float32 [22272, 768], P('dp'), may hold values from -0.06 to 0.06
- first_moment: float32 [4, 22272, 768], P('group', 'dp')
- second_moment: float32 [4, 22272, 768], P('group', 'dp')
- eval_pixels: bfloat16 [128, 49, 3072], P(('group', 'dp')), may hold values from -6 to 6
- eval_counts: int32 [32], P(('group', 'dp')), may hold values from 1 to 4, as said below
- eval_labels: int32 [128], P(('group', 'dp')), may hold values from 0 to 999
Outputs:
- new_master: float32 [22272, 768], P('dp')
- new_outer: float32 [22272, 768], P('dp')
- new_first: float32 [4, 22272, 768], P('group', 'dp')
- new_second: float32 [4, 22272, 768], P('group', 'dp')
- clip_norms: float32 [4, 1], P('group')
- loss_sums: float32 [4, 1], P('group')
- image_counts: float32 [4, 1], P('group')
- post_grads: float32 [4, 1, 2, 768], P('group')
- eval_losses: float32 [128], P(('group', 'dp'))
The draws below stay inside these ranges and needn't reach their ends.
Inputs may be any that keep to these rules, and one draw needn't show every extreme that they name: `counts`: real images of a device in a micro-batch; slots at or past it are padding; the last device of each worker along dp is full. `eval_counts`: real held-out images of a device; slots at or past it are padding; the last device of each worker along dp is full.
All inputs are finite; a program needn't handle non-finite values.
Results may differ from the reference program's by a relative error of at most 0.019.
Values may be sent and summed in bfloat16 or wider, within the bound.
A program may use at most 576 MiB of HBM per device.

```python
import math
import jax
import jax.numpy as jnp
from jax import lax

D = 768
HEADS = 12
HEAD = 64
FF = 3072
PATCH_IN = 3072
EMB = 512
PATCHES = 49
CLASSES = 1000
LAYERS = 2
INNER = 1
MICRO = 2
STEP = 10
IMG_DEV = 4
SEQ = 50
ROWS_RAW = 22079
ROWS = 22272
GROUPS = 4
RANKS = 8
IMAGES = 128


CLIP_LIMIT = 0.02


def noise_field(key, shape):
    return jax.random.normal(key, shape, jnp.float32)


def row_layout():
    row_index = jnp.arange(ROWS)
    table_start = PATCH_IN
    layer_start = table_start + SEQ + 1
    block_size = 4 * D + 2 * FF
    norm_start = layer_start + LAYERS * block_size
    head_start = norm_start + 4 * LAYERS + 4
    within = jnp.mod(row_index - layer_start, block_size)
    layer_spread = jnp.where(within < 3 * D, D ** (-0.5), jnp.where(within < 4 * D, 3.0 * D ** (-0.5), jnp.where(within < 4 * D + FF, D ** (-0.5), FF ** (-0.5))))
    spread = jnp.where(row_index < table_start, PATCH_IN ** (-0.5), jnp.where(row_index < layer_start, 0.5, jnp.where(row_index < norm_start, layer_spread, jnp.where(row_index < head_start, 0.1, jnp.where(row_index < ROWS_RAW, D ** (-0.5), 0.02)))))
    is_norm = (row_index >= norm_start) & (row_index < head_start)
    is_gain = is_norm & (jnp.mod(row_index - norm_start, 2) == 0)
    return (spread, is_gain, is_norm)


def grad_size():
    spread, is_gain, is_norm = row_layout()
    base_size = CLIP_LIMIT / math.sqrt(ROWS_RAW * D)
    return base_size * jnp.where(is_norm, 4.0, 1.0)


def draw_master(key, part):
    spread, is_gain, is_norm = row_layout()
    return jnp.where(is_gain, 1.0, 0.0)[:, None] + spread[:, None] * noise_field(key, (ROWS, D))


def draw_first_moment(key, part):
    sizes = grad_size()
    return 0.1 / 0.9 * sizes[None, :, None] * noise_field(key, (GROUPS, ROWS, D))


def draw_second_moment(key, part):
    sizes = grad_size()
    factor = jax.random.uniform(key, (GROUPS, ROWS, D), jnp.float32, 1.0, 4.0)
    return 0.02 / 0.98 * (sizes * sizes)[None, :, None] * factor


def count_law(key, lead_shape):
    slots = GROUPS * RANKS
    device = jnp.arange(slots) % RANKS
    lowest = max(1, (IMG_DEV + 2) // 3)
    base_count = lowest + device * (IMG_DEV - lowest + 1) // RANKS
    jitter = jax.random.randint(key, lead_shape + (slots,), -1, 2)
    filled = jnp.clip(base_count + jitter, 1, IMG_DEV)
    filled = jnp.where(device == RANKS - 1, IMG_DEV, filled)
    return filled.astype(jnp.int32)


def draw_counts(key, part):
    return count_law(key, (INNER, MICRO))


def draw_eval_counts(key, part):
    return count_law(jax.random.fold_in(key, 7), ())


def plant(array, key, low, top_value):
    extent = array.shape
    spot = [jax.random.randint(jax.random.fold_in(key, axis), (), 0, extent[axis]) for axis in range(len(extent))]
    array = array.at[tuple(spot)].set(low)
    longest = extent.index(max(extent))
    spot[longest] = (spot[longest] + 1) % extent[longest]
    return array.at[tuple(spot)].set(top_value)


def block_scale(key, dims, pieces, least, high):
    loudness = 1.0
    for axis_at, shards_of in pieces:
        draws = jax.random.uniform(jax.random.fold_in(jax.random.fold_in(key, 6), axis_at), (shards_of,), jnp.float32, least / len(pieces), high / len(pieces))
        loudness = loudness * jnp.repeat(jnp.exp(draws), dims[axis_at] // shards_of).reshape((-1,) + (1,) * (len(dims) - 1 - axis_at))
    return loudness


def gaussian(stream_key, dims, width, most, shards=(), dtype=jnp.bfloat16):
    values = width * jax.random.normal(stream_key, dims, jnp.float32)
    if shards:
        values = values * block_scale(stream_key, dims, shards, -0.22, 0.18)
    return jnp.clip(values, -most, most).astype(dtype)


def setup_inputs(seed: int = 0) -> dict:
    key_of = jax.random.split(jax.random.key(seed), 12)
    return {
        "pixels": gaussian(key_of[0], (INNER, MICRO, IMAGES, PATCHES, PATCH_IN), 1.0, 6.0, ((2, 32),)),
        "counts": draw_counts(jax.random.fold_in(key_of[11], 71), 0),
        "labels": plant(jax.random.randint(key_of[2], (INNER, MICRO, IMAGES), 0, CLASSES), jax.random.fold_in(key_of[2], 1), 0, CLASSES - 1).astype(jnp.int32),
        "text": gaussian(key_of[3], (CLASSES, EMB), EMB ** -0.5, 0.25),
        "master": draw_master(jax.random.fold_in(key_of[11], 71), 0),
        "outer_momentum": gaussian(key_of[5], (ROWS, D), 0.01, 0.06, ((0, 8),), jnp.float32),
        "first_moment": draw_first_moment(jax.random.fold_in(key_of[11], 71), 0),
        "second_moment": draw_second_moment(jax.random.fold_in(key_of[11], 71), 0),
        "eval_pixels": gaussian(key_of[8], (IMAGES, PATCHES, PATCH_IN), 1.0, 6.0, ((0, 32),)),
        "eval_counts": draw_eval_counts(jax.random.fold_in(key_of[11], 71), 0),
        "eval_labels": plant(jax.random.randint(key_of[10], (IMAGES,), 0, CLASSES), jax.random.fold_in(key_of[10], 1), 0, CLASSES - 1).astype(jnp.int32),
    }


LN_EPS = 1e-05
NORM_EPS = 1e-06
LOGIT_SCALE = 50.0
SMOOTH = 0.1
CLIP_MAX = 0.02
BETA_ONE = 0.9
BETA_TWO = 0.98
ADAM_EPS = 1e-08
RATE = 0.02
DECAY = 0.1
OUTER_RATE = 0.7
OUTER_MOM = 0.9
GELU_SLOPE = 1.702
PRECISE = lax.Precision.HIGHEST

@jax.custom_vjp
def low(v):
    return lax.optimization_barrier(v.astype(jnp.bfloat16)).astype(jnp.float32)

@jax.custom_vjp
def low_back(v):
    return v

def low_keep(v):
    return (low(v), None)

def low_pass(kept, grad):
    return (grad,)

def back_keep(v):
    return (v, None)

def back_low(kept, grad):
    return (low(grad),)
low.defvjp(low_keep, low_pass)
low_back.defvjp(back_keep, back_low)

def product(pattern, first_arg, second_arg):
    return jnp.einsum(pattern, first_arg, second_arg, precision=PRECISE)

def layer_norm(values, gain_row, bias_row):
    row_mean = lax.optimization_barrier(jnp.mean(values, -1, keepdims=True))
    centred = values - row_mean
    row_var = lax.optimization_barrier(jnp.mean(centred * centred, -1, keepdims=True))
    return centred * lax.rsqrt(row_var + LN_EPS) * gain_row + bias_row

def layout_rows():
    table_start = PATCH_IN
    layer_start = table_start + SEQ + 1
    block_size = 4 * D + 2 * FF
    norm_start = layer_start + LAYERS * block_size
    head_start = norm_start + 4 * LAYERS + 4
    return (table_start, layer_start, block_size, norm_start, head_start)

def encoder_layer(hidden, block_rows, norm_rows):
    w_qkv = block_rows[:3 * D].reshape(3, D, D)
    w_out = block_rows[3 * D:4 * D]
    w_in = block_rows[4 * D:4 * D + FF]
    w_back = block_rows[4 * D + FF:]
    batch_size = hidden.shape[0]
    normed = low(layer_norm(hidden, norm_rows[0], norm_rows[1]))
    qkv_rows = low_back(low(product('btd,jde->btje', normed, w_qkv)))
    shaped = qkv_rows.reshape(batch_size, SEQ, 3, HEADS, HEAD)
    query_rows, key_rows, value_rows = (shaped[:, :, 0], shaped[:, :, 1], shaped[:, :, 2])
    scores = low_back(product('bqhd,bkhd->bhqk', query_rows, key_rows) * HEAD ** (-0.5))
    attn_probs = low(jax.nn.softmax(scores, axis=-1))
    mixed_rows = low_back(low(product('bhqk,bkhd->bqhd', attn_probs, value_rows)))
    mixed_rows = mixed_rows.reshape(batch_size, SEQ, D)
    after_attn = hidden + low_back(product('btd,de->bte', mixed_rows, w_out))
    normed_two = low(layer_norm(after_attn, norm_rows[2], norm_rows[3]))
    inner_pre = low_back(product('btd,fd->btf', normed_two, w_in))
    activated = low(inner_pre * jax.nn.sigmoid(GELU_SLOPE * inner_pre))
    return after_attn + low_back(product('btf,fd->btd', activated, w_back))

def forward_rows(flat_rows, pixel_block, mask_row, label_row, text_rows):
    weights = low(flat_rows)
    table_start, layer_start, block_size, norm_start, head_start = layout_rows()
    batch_size = pixel_block.shape[0]
    patches = low_back(product('bpi,id->bpd', pixel_block, weights[:PATCH_IN]))
    class_rows = jnp.broadcast_to(weights[table_start], (batch_size, 1, D))
    hidden = jnp.concatenate([class_rows, patches], axis=1) + weights[table_start + 1:layer_start]
    norm_rows = weights[norm_start:head_start]
    hidden = layer_norm(hidden, norm_rows[0], norm_rows[1])
    for layer_index in range(LAYERS):
        block_rows = weights[layer_start + layer_index * block_size:layer_start + (layer_index + 1) * block_size]
        hidden = encoder_layer(hidden, block_rows, norm_rows[2 + 4 * layer_index:6 + 4 * layer_index])
    pooled = low(layer_norm(hidden[:, 0], norm_rows[-2], norm_rows[-1]))
    embedded = low_back(product('bd,ed->be', pooled, weights[head_start:head_start + EMB]))
    unit_rows = embedded * lax.rsqrt(lax.optimization_barrier(jnp.sum(embedded * embedded, -1, keepdims=True)) + NORM_EPS)
    logits = LOGIT_SCALE * low_back(product('be,ce->bc', low(unit_rows), text_rows))
    log_probs = jax.nn.log_softmax(logits, axis=-1)
    onehot = (label_row[:, None] == jnp.arange(CLASSES)[None, :]).astype(jnp.float32)
    target = (1.0 - SMOOTH) * onehot + SMOOTH / CLASSES
    return -mask_row * lax.optimization_barrier(jnp.sum(target * log_probs, -1))

def forward(flat_rows, pixel_block, mask_row, label_row, text_rows):
    return jnp.sum(forward_rows(flat_rows, pixel_block, mask_row, label_row, text_rows))

def adam_update(params, moment_one, moment_two, clipped, step_number):
    moment_one = BETA_ONE * moment_one + (1.0 - BETA_ONE) * clipped
    moment_two = BETA_TWO * moment_two + (1.0 - BETA_TWO) * clipped * clipped
    corrected_one = moment_one / (1.0 - BETA_ONE ** step_number)
    corrected_two = moment_two / (1.0 - BETA_TWO ** step_number)
    params = params - RATE * (corrected_one / (jnp.sqrt(corrected_two) + ADAM_EPS) + DECAY * params)
    return (params, moment_one, moment_two)

def reference(pixels, counts, labels, text, master, outer_momentum, first_moment, second_moment, eval_pixels, eval_counts, eval_labels):
    batch_size = IMG_DEV * RANKS
    slot_index = jnp.arange(batch_size) % IMG_DEV
    per_image = jnp.repeat(counts.reshape(INNER, MICRO, GROUPS, RANKS), IMG_DEV, axis=-1)
    mask_all = (slot_index[None, None, None, :] < per_image).astype(jnp.float32)
    pixel_groups = jnp.moveaxis(pixels.reshape(INNER, MICRO, GROUPS, batch_size, PATCHES, PATCH_IN), 2, 0)
    mask_groups = jnp.moveaxis(mask_all, 2, 0)
    label_groups = jnp.moveaxis(labels.reshape(INNER, MICRO, GROUPS, batch_size), 2, 0)
    text_rows = text.astype(jnp.float32)
    head_start = layout_rows()[4]

    def train(group_inputs):
        pixel_group, mask_group, label_group, moment_one, moment_two = group_inputs
        params = master
        norm_list, loss_list, count_list, post_list = ([], [], [], [])
        for step_index in range(INNER):
            grad_sum = jnp.zeros_like(master)
            loss_total = jnp.zeros((), jnp.float32)
            for micro_index in range(MICRO):
                pixel_block = pixel_group[step_index, micro_index].astype(jnp.float32)
                mask_row = mask_group[step_index, micro_index]
                label_row = label_group[step_index, micro_index]

                def objective(flat_rows):
                    return forward(flat_rows, pixel_block, mask_row, label_row, text_rows)
                loss_part, pull_back = jax.vjp(objective, params)
                grad_sum = grad_sum + pull_back(jnp.ones_like(loss_part))[0]
                loss_total = loss_total + loss_part
            image_total = jnp.sum(mask_group[step_index])
            gradient = grad_sum / image_total
            grad_norm = jnp.sqrt(jnp.sum(gradient * gradient))
            clipped = gradient * (CLIP_MAX / jnp.maximum(grad_norm, CLIP_MAX))
            params, moment_one, moment_two = adam_update(params, moment_one, moment_two, clipped, STEP + step_index)
            norm_list.append(grad_norm)
            loss_list.append(loss_total)
            count_list.append(image_total)
            post_list.append(clipped[head_start - 2:head_start])
        return (params, moment_one, moment_two, jnp.stack(norm_list), jnp.stack(loss_list), jnp.stack(count_list), jnp.stack(post_list))
    results = lax.map(train, (pixel_groups, mask_groups, label_groups, first_moment, second_moment))
    delta = lax.optimization_barrier(jnp.sum(master[None] - results[0], axis=0)) / GROUPS
    new_outer = OUTER_MOM * outer_momentum + delta
    new_master = master - OUTER_RATE * (delta + OUTER_MOM * new_outer)
    eval_per_image = jnp.repeat(eval_counts.reshape(GROUPS, RANKS), IMG_DEV, axis=-1)
    eval_mask = (slot_index[None, :] < eval_per_image).astype(jnp.float32)
    eval_pixel_groups = eval_pixels.reshape(GROUPS, batch_size, PATCHES, PATCH_IN)
    eval_label_groups = eval_labels.reshape(GROUPS, batch_size)

    def evaluate(group_inputs):
        pixel_block, mask_row, label_row = group_inputs
        return forward_rows(new_master, pixel_block.astype(jnp.float32), mask_row, label_row, text_rows)
    eval_losses = lax.map(evaluate, (eval_pixel_groups, eval_mask, eval_label_groups)).reshape(IMAGES)
    return (new_master, new_outer, results[1], results[2], results[3], results[4], results[5], results[6], eval_losses)
```

```python
import functools

import jax
import jax.numpy as jnp
from jax import lax
from jax.experimental import pallas as pl
from jax.experimental.pallas import tpu as pltpu
from jax.sharding import PartitionSpec as P

MESH = pl.DeviceIdType.MESH

D = 768
HEADS = 12
HEAD = 64
FF = 3072
PATCH_IN = 3072
EMB = 512
CLASSES = 1000
LAYERS = 2
MICRO = 2
STEP = 10
SEQ = 50
ROWS_RAW = 22079


LN_EPS = 1e-05
NORM_EPS = 1e-06
LOGIT_SCALE = 50.0
SMOOTH = 0.1
CLIP_MAX = 0.02
BETA_ONE = 0.9
BETA_TWO = 0.98
ADAM_EPS = 1e-08
RATE = 0.02
DECAY = 0.1
OUTER_RATE = 0.7
OUTER_MOM = 0.9
GELU_SLOPE = 1.702
SPARE = 13


def product(pattern, first_arg, second_arg):
    return jnp.einsum(pattern, first_arg, second_arg, preferred_element_type=jnp.float32)


def layer_norm(values, gain_row, bias_row):
    row_mean = jnp.mean(values, -1, keepdims=True)
    centred = values - row_mean
    row_var = jnp.mean(centred * centred, -1, keepdims=True)
    return centred * lax.rsqrt(row_var + LN_EPS) * gain_row + bias_row


def quick_gelu(inner_pre):
    return inner_pre * jax.nn.sigmoid(GELU_SLOPE * inner_pre)


def unit_length(embedded):
    return embedded * lax.rsqrt(jnp.sum(embedded * embedded, -1, keepdims=True) + NORM_EPS)


def layout_rows():
    table_start = PATCH_IN
    layer_start = table_start + SEQ + 1
    block_size = 4 * D + 2 * FF
    norm_start = layer_start + LAYERS * block_size
    head_start = norm_start + 4 * LAYERS + 4
    return (table_start, layer_start, block_size, norm_start, head_start)


def split_block(block_rows):
    return (
        block_rows[: 3 * D].reshape(3, D, D),
        block_rows[3 * D : 4 * D],
        block_rows[4 * D : 4 * D + FF],
        block_rows[4 * D + FF :],
    )


def split_heads(qkv_rows):
    shaped = qkv_rows.reshape(qkv_rows.shape[0], SEQ, 3, HEADS, HEAD)
    return (shaped[:, :, 0], shaped[:, :, 1], shaped[:, :, 2])


def layer_forward(hidden, block_rows, norm_rows):
    w_qkv, w_out, w_in, w_back = split_block(block_rows)
    batch_size = hidden.shape[0]
    normed, first_back = jax.vjp(layer_norm, hidden, norm_rows[0], norm_rows[1])
    normed = normed.astype(jnp.bfloat16)
    qkv_rows = product("btd,jde->btje", normed, w_qkv).astype(jnp.bfloat16)
    query_rows, key_rows, value_rows = split_heads(qkv_rows)
    scores = product("bqhd,bkhd->bhqk", query_rows, key_rows) * HEAD ** (-0.5)
    log_total = jax.nn.logsumexp(scores, axis=-1, keepdims=True)
    attn_probs = jnp.exp(scores - log_total).astype(jnp.bfloat16)
    mixed_rows = product("bhqk,bkhd->bqhd", attn_probs, value_rows).astype(jnp.bfloat16)
    mixed_rows = mixed_rows.reshape(batch_size, SEQ, D)
    after_attn = hidden + product("btd,de->bte", mixed_rows, w_out)
    normed_two, second_back = jax.vjp(layer_norm, after_attn, norm_rows[2], norm_rows[3])
    normed_two = normed_two.astype(jnp.bfloat16)
    inner_pre = product("btd,fd->btf", normed_two, w_in)
    activated, gelu_back = jax.vjp(quick_gelu, inner_pre)
    activated = activated.astype(jnp.bfloat16)
    output = after_attn + product("btf,fd->btd", activated, w_back)
    kept_state = (
        first_back,
        normed,
        qkv_rows,
        log_total,
        mixed_rows,
        second_back,
        normed_two,
        gelu_back,
        activated,
    )
    return (output, kept_state)


def layer_backward(grad_out, kept_state, block_rows):
    w_qkv, w_out, w_in, w_back = split_block(block_rows)
    (
        first_back,
        normed,
        qkv_rows,
        log_total,
        mixed_rows,
        second_back,
        normed_two,
        gelu_back,
        activated,
    ) = kept_state
    batch_size = grad_out.shape[0]
    grad_branch = grad_out.astype(jnp.bfloat16)
    grad_act = product("btd,fd->btf", grad_branch, w_back)
    grad_w_back = product("btf,btd->fd", activated, grad_branch)
    grad_pre = gelu_back(grad_act)[0].astype(jnp.bfloat16)
    grad_w_in = product("btf,btd->fd", grad_pre, normed_two)
    grad_normed_two = product("btf,fd->btd", grad_pre, w_in)
    grad_attn_in, grad_gain_two, grad_bias_two = second_back(grad_normed_two)
    grad_after = grad_out + grad_attn_in
    grad_proj = grad_after.astype(jnp.bfloat16)
    grad_w_out = product("btd,bte->de", mixed_rows, grad_proj)
    grad_mixed = product("bte,de->btd", grad_proj, w_out).astype(jnp.bfloat16)
    grad_mixed = grad_mixed.reshape(batch_size, SEQ, HEADS, HEAD)
    query_rows, key_rows, value_rows = split_heads(qkv_rows)
    scale_factor = HEAD ** (-0.5)
    scores = product("bqhd,bkhd->bhqk", query_rows, key_rows) * scale_factor
    soft_rows = jnp.exp(scores - log_total)
    grad_soft = product("bqhd,bkhd->bhqk", grad_mixed, value_rows)
    grad_value = product("bhqk,bqhd->bkhd", soft_rows.astype(jnp.bfloat16), grad_mixed)
    grad_scores = soft_rows * (grad_soft - jnp.sum(grad_soft * soft_rows, -1, keepdims=True))
    grad_scores = grad_scores.astype(jnp.bfloat16)
    grad_query = product("bhqk,bkhd->bqhd", grad_scores, key_rows) * scale_factor
    grad_key = product("bhqk,bqhd->bkhd", grad_scores, query_rows) * scale_factor
    grad_qkv = jnp.stack([grad_query, grad_key, grad_value], axis=2)
    grad_qkv = grad_qkv.reshape(batch_size, SEQ, 3, D).astype(jnp.bfloat16)
    grad_w_qkv = product("btd,btje->jde", normed, grad_qkv).reshape(3 * D, D)
    grad_normed = product("btje,jde->btd", grad_qkv, w_qkv)
    grad_in, grad_gain_one, grad_bias_one = first_back(grad_normed)
    weight_grads = jnp.concatenate(
        [piece.astype(jnp.bfloat16) for piece in (grad_w_qkv, grad_w_out, grad_w_in, grad_w_back)], axis=0
    )
    norm_grads = jnp.stack([grad_gain_one, grad_bias_one, grad_gain_two, grad_bias_two])
    return (grad_after + grad_in, weight_grads, norm_grads)


def micro_step(weights, pixel_block, live_mask, label_row, text, with_grads):
    table_start, layer_start, block_size, norm_start, head_start = layout_rows()
    batch_size = pixel_block.shape[0]
    table_rows = weights[table_start:layer_start].astype(jnp.float32)
    norm_rows = weights[norm_start:head_start].astype(jnp.float32)
    head_rows = weights[head_start : head_start + EMB]
    patches = product("bpi,id->bpd", pixel_block, weights[:PATCH_IN])
    class_rows = jnp.broadcast_to(table_rows[0], (batch_size, 1, D))
    embedded_in = jnp.concatenate([class_rows, patches], axis=1) + table_rows[1:]
    hidden, pre_back = jax.vjp(layer_norm, embedded_in, norm_rows[0], norm_rows[1])
    kept_layers = []
    for layer_index in range(LAYERS):
        block_rows = weights[
            layer_start + layer_index * block_size : layer_start + (layer_index + 1) * block_size
        ]
        hidden, kept_state = layer_forward(
            hidden, block_rows, norm_rows[2 + 4 * layer_index : 6 + 4 * layer_index]
        )
        kept_layers.append(kept_state)
    pooled, post_back = jax.vjp(layer_norm, hidden[:, 0], norm_rows[-2], norm_rows[-1])
    pooled = pooled.astype(jnp.bfloat16)
    embedded = product("bd,ed->be", pooled, head_rows)
    unit_rows, unit_back = jax.vjp(unit_length, embedded)
    logits = LOGIT_SCALE * product("be,ce->bc", unit_rows.astype(jnp.bfloat16), text)
    log_probs = jax.nn.log_softmax(logits, axis=-1)
    onehot = (label_row[:, None] == jnp.arange(CLASSES)[None, :]).astype(jnp.float32)
    target = (1.0 - SMOOTH) * onehot + SMOOTH / CLASSES
    image_losses = -live_mask * jnp.sum(target * log_probs, -1)
    if not with_grads:
        return (image_losses, None)
    loss_sum = jnp.sum(image_losses)
    grad_logits = (jnp.exp(log_probs) - target) * live_mask[:, None]
    grad_raw = (LOGIT_SCALE * grad_logits).astype(jnp.bfloat16)
    grad_unit = product("bc,ce->be", grad_raw, text)
    grad_embed = unit_back(grad_unit)[0].astype(jnp.bfloat16)
    grad_head = product("be,bd->ed", grad_embed, pooled)
    grad_pooled = product("be,ed->bd", grad_embed, head_rows)
    grad_class, grad_gain_post, grad_bias_post = post_back(grad_pooled)
    grad_hidden = jnp.concatenate(
        [grad_class[:, None], jnp.zeros((batch_size, SEQ - 1, D), jnp.float32)], axis=1
    )
    layer_grads = [None] * LAYERS
    layer_norm_grads = [None] * LAYERS
    for layer_index in reversed(range(LAYERS)):
        block_rows = weights[
            layer_start + layer_index * block_size : layer_start + (layer_index + 1) * block_size
        ]
        grad_hidden, layer_grads[layer_index], layer_norm_grads[layer_index] = layer_backward(
            grad_hidden, kept_layers[layer_index], block_rows
        )
    grad_embedded, grad_gain_pre, grad_bias_pre = pre_back(grad_hidden)
    grad_patches = grad_embedded[:, 1:].astype(jnp.bfloat16)
    grad_patch_w = product("bpi,bpd->id", pixel_block, grad_patches)
    grad_table = jnp.concatenate(
        [jnp.sum(grad_embedded[:, 0], axis=0)[None], jnp.sum(grad_embedded, axis=0)], axis=0
    )
    grad_norms = jnp.concatenate(
        [jnp.stack([grad_gain_pre, grad_bias_pre])]
        + layer_norm_grads
        + [jnp.stack([grad_gain_post, grad_bias_post])],
        axis=0,
    )
    spare = jnp.zeros((SPARE, D), jnp.float32)
    padding = jnp.zeros((weights.shape[0] - ROWS_RAW - SPARE, D), jnp.float32)
    table_block = jnp.concatenate([grad_table, spare], axis=0)
    tail_block = jnp.concatenate([grad_norms, grad_head, padding], axis=0)
    grad_rows = jnp.concatenate(
        [
            piece.astype(jnp.bfloat16)
            for piece in [grad_patch_w, table_block] + layer_grads + [tail_block]
        ],
        axis=0,
    )
    return (loss_sum, grad_rows)


def on_grid():
    return lax.axis_size("group") == 4 and lax.axis_size("dp") == 8


def place():
    worker = lax.axis_index("group")
    rank = lax.axis_index("dp")
    return (worker // 2, worker % 2, rank // 2, rank % 2)


def device_at(y, c, z, x):
    return (y * 2 + c, z * 2 + x)


def chunk_rows(total, count):
    units = total // 16
    chunks = []
    start = 0
    for index in range(count):
        size = units * (index + 1) // count - units * index // count
        first = size // 2 if index % 2 else size - size // 2
        chunks.append((start * 16, first * 16, (size - first) * 16))
        start += size
    return chunks


def gather_kernel(chunks, part_ref, full_ref, local_sem, sends, recvs):
    half_cols = part_ref.shape[1]
    y, c, z, x = place()
    cols = pl.ds(pl.multiple_of(c * half_cols, half_cols), half_cols)
    over_x = device_at(y, c, z, 1 - x)
    over_y = device_at(1 - y, c, z, x)
    sibling = device_at(y, 1 - c, z, x)
    along_z = [device_at(y, c, (z + step) % 4, x) for step in (1, 2, 3)]
    barrier = pltpu.get_barrier_semaphore()
    for other in [over_x, over_y, sibling] + along_z:
        pl.semaphore_signal(barrier, inc=1, device_id=other, device_id_type=MESH)
    local = pltpu.make_async_copy(part_ref, full_ref.at[z, x, y, :, cols], local_sem)
    local.start()
    pl.semaphore_wait(barrier, 6)

    def send(piece, other, stage, index):
        pltpu.make_async_remote_copy(
            src_ref=piece,
            dst_ref=piece,
            send_sem=sends.at[stage, index],
            recv_sem=recvs.at[stage, index],
            device_id=other,
            device_id_type=MESH,
        ).start()

    def arrived(piece, stage, index):
        pltpu.make_async_copy(piece, piece, recvs.at[stage, index]).wait()

    def sent(piece, stage, index):
        pltpu.make_async_copy(piece, piece, sends.at[stage, index]).wait()

    def pieces(index):
        start, first, second = chunks[index]
        rows = pl.ds(start, first + second)
        rows_a = pl.ds(start, first)
        rows_b = pl.ds(start + first, second)
        return {
            0: full_ref.at[pl.ds(0, 3), 0, 0, rows, cols],
            1: full_ref.at[:, x, y, rows_a, cols],
            2: full_ref.at[:, x, y, rows_b, cols],
            3: full_ref.at[:, x, :, rows_a, cols],
            4: full_ref.at[:, :, y, rows_b, cols],
            5: full_ref.at[:, :, :, rows, cols],
        }

    total = len(chunks)
    for step in range(total + 5):
        if step < total:
            start, first, second = chunks[step]
            rows = pl.ds(start, first + second)
            for other in along_z:
                pltpu.make_async_remote_copy(
                    src_ref=part_ref.at[rows],
                    dst_ref=full_ref.at[z, x, y, rows, cols],
                    send_sem=sends.at[0, step],
                    recv_sem=recvs.at[0, step],
                    device_id=other,
                    device_id_type=MESH,
                ).start()
        if step == 0:
            local.wait()
        index = step - 1
        if 0 <= index < total:
            block = pieces(index)
            arrived(block[0], 0, index)
            send(block[1], over_y, 1, index)
            send(block[2], over_x, 2, index)
        index = step - 2
        if 0 <= index < total:
            block = pieces(index)
            arrived(block[1], 1, index)
            send(block[3], over_x, 3, index)
            arrived(block[2], 2, index)
            send(block[4], over_y, 4, index)
        index = step - 3
        if 0 <= index < total:
            block = pieces(index)
            arrived(block[3], 3, index)
            arrived(block[4], 4, index)
            send(block[5], sibling, 5, index)
    for index in range(total):
        block = pieces(index)
        arrived(block[5], 5, index)
        for stage in range(6):
            sent(block[stage], stage, index)


def gather_rows(part, shard_rows):
    chunks = chunk_rows(part.shape[0], 8)
    full = pl.pallas_call(
        functools.partial(gather_kernel, chunks),
        out_shape=jax.ShapeDtypeStruct((4, 2, 2, part.shape[0], 2 * part.shape[1]), part.dtype),
        in_specs=[pl.BlockSpec(memory_space=pl.ANY)],
        out_specs=pl.BlockSpec(memory_space=pl.ANY),
        scratch_shapes=[
            pltpu.SemaphoreType.DMA,
            pltpu.SemaphoreType.DMA((6, len(chunks))),
            pltpu.SemaphoreType.DMA((6, len(chunks))),
        ],
        compiler_params=pltpu.CompilerParams(collective_id=0, has_side_effects=True),
        name="gather",
    )(part)
    return full.reshape(8 * shard_rows, 2 * part.shape[1])


def reduce_kernel(
    chunks,
    grad_ref,
    own_ref,
    mine,
    first_sum,
    sum_a,
    sum_b,
    last_sum,
    load_sems,
    sends,
    recvs,
):
    half_cols = mine.shape[-1]
    y, c, z, x = place()
    home_y, home_c = z % 2, z // 2
    at_home = jnp.logical_and(home_y == y, home_c == c)
    from_plane = 2 * c + y
    my_cols = pl.ds(pl.multiple_of(c * half_cols, half_cols), half_cols)
    other_cols = pl.ds(pl.multiple_of((1 - c) * half_cols, half_cols), half_cols)
    over_x = device_at(y, c, z, 1 - x)
    over_y = device_at(1 - y, c, z, x)
    sibling = device_at(y, 1 - c, z, x)
    barrier = pltpu.get_barrier_semaphore()
    for other in (over_x, over_y, sibling):
        pl.semaphore_signal(barrier, inc=1, device_id=other, device_id_type=MESH)
    for other_y in range(2):
        for other_c in range(2):
            itself = jnp.logical_and(at_home, jnp.logical_and(y == other_y, c == other_c))

            @pl.when(jnp.logical_not(itself))
            def _():
                pl.semaphore_signal(
                    barrier,
                    inc=1,
                    device_id=device_at(other_y, other_c, from_plane, x),
                    device_id_type=MESH,
                )

    def spans(index):
        start, first, second = chunks[index]
        start_a = sum(chunk[1] for chunk in chunks[:index])
        start_b = sum(chunk[2] for chunk in chunks[:index])
        return (
            pl.ds(start, first + second),
            pl.ds(start, first),
            pl.ds(start + first, second),
            pl.ds(start_a, first),
            pl.ds(start_b, second),
        )

    def send(source, target, other, stage, index):
        pltpu.make_async_remote_copy(
            src_ref=source,
            dst_ref=target,
            send_sem=sends.at[stage, index],
            recv_sem=recvs.at[stage, index],
            device_id=other,
            device_id_type=MESH,
        ).start()

    def arrived(piece, stage, index):
        pltpu.make_async_copy(piece, piece, recvs.at[stage, index]).wait()

    def sent(piece, stage, index):
        pltpu.make_async_copy(piece, piece, sends.at[stage, index]).wait()

    def load(index):
        rows = spans(index)[0]
        return pltpu.make_async_copy(
            grad_ref.at[:, :, :, rows, my_cols],
            mine.at[index % 2, :, :, :, pl.ds(0, rows.size)],
            load_sems.at[index % 2],
        )

    def send_core(index):
        rows = spans(index)[0]
        send(
            grad_ref.at[:, :, :, rows, other_cols],
            first_sum.at[:, :, :, rows],
            sibling,
            0,
            index,
        )

    def add(target, source):
        summed = target[...].astype(jnp.float32) + source[...].astype(jnp.float32)
        target[...] = summed.astype(target.dtype)

    total = len(chunks)
    load(0).start()
    pl.semaphore_wait(barrier, 3 + jnp.where(at_home, 3, 4))
    send_core(0)
    send_core(1)
    for step in range(total + 4):
        index = step
        if index < total:
            if index + 1 < total:
                load(index + 1).start()
            if index + 2 < total:
                send_core(index + 2)
            rows, rows_a, rows_b, in_a, in_b = spans(index)
            load(index).wait()
            arrived(first_sum.at[:, :, :, rows], 0, index)

            @pl.loop(0, 16)
            def _(block):
                zz, rest = block // 4, block % 4
                add(
                    first_sum.at[zz, rest // 2, rest % 2, rows],
                    mine.at[index % 2, zz, rest // 2, rest % 2, pl.ds(0, rows.size)],
                )

            send(first_sum.at[:, 1 - x, :, rows_a], sum_a.at[:, :, in_a], over_x, 1, index)
            send(first_sum.at[:, :, 1 - y, rows_b], sum_b.at[:, :, in_b], over_y, 2, index)
        index = step - 1
        if 0 <= index < total:
            rows, rows_a, rows_b, in_a, in_b = spans(index)
            arrived(sum_a.at[:, :, in_a], 1, index)

            @pl.loop(0, 8)
            def _(block):
                add(
                    sum_a.at[block // 2, block % 2, in_a],
                    first_sum.at[block // 2, x, block % 2, rows_a],
                )

            send(sum_a.at[:, 1 - y, in_a], last_sum.at[:, rows_a], over_y, 3, index)
            arrived(sum_b.at[:, :, in_b], 2, index)

            @pl.loop(0, 8)
            def _(block):
                add(
                    sum_b.at[block // 2, block % 2, in_b],
                    first_sum.at[block // 2, block % 2, y, rows_b],
                )

            send(sum_b.at[:, 1 - x, in_b], last_sum.at[:, rows_b], over_x, 4, index)
        index = step - 2
        if 0 <= index < total:
            rows, rows_a, rows_b, in_a, in_b = spans(index)
            arrived(last_sum.at[:, rows_a], 3, index)
            arrived(last_sum.at[:, rows_b], 4, index)

            @pl.loop(0, 4)
            def _(block):
                add(last_sum.at[block, rows_a], sum_a.at[block, y, in_a])
                add(last_sum.at[block, rows_b], sum_b.at[block, x, in_b])

            for to_z in range(4):
                itself = jnp.logical_and(at_home, z == to_z)
                source = last_sum.at[to_z, rows]
                target = own_ref.at[y, rows, my_cols]

                @pl.when(jnp.logical_not(itself))
                def _():
                    send(source, target, device_at(home_y, home_c, to_z, x), 5, index)

                @pl.when(itself)
                def _():
                    pltpu.make_async_copy(source, target, recvs.at[5, index]).start()

    for index in range(total):
        rows, rows_a, rows_b, in_a, in_b = spans(index)
        arrived(own_ref.at[:, rows], 5, index)
        sent(first_sum.at[:, :, :, rows], 0, index)
        sent(sum_a.at[:, :, in_a], 1, index)
        sent(sum_b.at[:, :, in_b], 2, index)
        sent(last_sum.at[:, rows_a], 3, index)
        sent(last_sum.at[:, rows_b], 4, index)

        @pl.when(at_home)
        def _():
            sent(last_sum.at[pl.ds(0, 3), rows], 5, index)

        @pl.when(jnp.logical_not(at_home))
        def _():
            sent(last_sum.at[:, rows], 5, index)


def reduce_chunks(total, count, share):
    units = total // 16
    chunks = []
    start = 0
    for index in range(count):
        size = units * (index + 1) // count - units * index // count
        first = int(round(size * share))
        chunks.append((start * 16, first * 16, (size - first) * 16))
        start += size
    return chunks


def sum_on_plane(grad_rows):
    half_rows, width = grad_rows.shape[0] // 16, grad_rows.shape[1]
    chunks = reduce_chunks(half_rows, 8, 0.75)
    most = max(first + second for _, first, second in chunks)
    half_cols = width // 2
    dtype = grad_rows.dtype
    own = pl.pallas_call(
        functools.partial(reduce_kernel, chunks),
        out_shape=jax.ShapeDtypeStruct((2, half_rows, width), dtype),
        in_specs=[pl.BlockSpec(memory_space=pl.ANY)],
        out_specs=pl.BlockSpec(memory_space=pl.ANY),
        scratch_shapes=[
            pltpu.VMEM((2, 4, 2, 2, most, half_cols), dtype),
            pltpu.VMEM((4, 2, 2, half_rows, half_cols), dtype),
            pltpu.VMEM((4, 2, sum(chunk[1] for chunk in chunks), half_cols), dtype),
            pltpu.VMEM((4, 2, sum(chunk[2] for chunk in chunks), half_cols), dtype),
            pltpu.VMEM((4, half_rows, half_cols), dtype),
            pltpu.SemaphoreType.DMA((2,)),
            pltpu.SemaphoreType.DMA((6, len(chunks))),
            pltpu.SemaphoreType.DMA((6, len(chunks))),
        ],
        compiler_params=pltpu.CompilerParams(
            collective_id=1, has_side_effects=True, vmem_limit_bytes=56 * 2**20
        ),
        name="reduce",
    )(grad_rows.reshape(4, 2, 2, half_rows, width))
    return own.reshape(2 * half_rows, width)


def to_planes(values):
    pairs = []
    for source in range(32):
        y, c, z, x = source // 16, source // 8 % 2, source // 2 % 4, source % 2
        pairs.append((source, (z % 2 * 2 + z // 2) * 8 + (2 * c + y) * 2 + x))
    return lax.ppermute(values, ("group", "dp"), pairs)


def fetch_weights(params):
    if not on_grid():
        return lax.all_gather(params.astype(jnp.bfloat16), "dp", axis=0, tiled=True)
    y, c, _, _ = place()
    rows, width = params.shape
    part = lax.dynamic_slice(params, (y * (rows // 2), c * (width // 2)), (rows // 2, width // 2))
    return gather_rows(part.astype(jnp.bfloat16), rows)


def reduce_rows(grad_rows):
    if on_grid():
        shard = sum_on_plane(grad_rows)
    else:
        shard = lax.psum_scatter(grad_rows, "dp", scatter_dimension=0, tiled=True)
    ranks, rank = lax.axis_size("dp"), lax.axis_index("dp")
    count = shard.shape[0]
    following = lax.ppermute(shard[:16], "dp", [(source, source - 1) for source in range(1, ranks)])
    shifted = jnp.concatenate([shard[SPARE:], following[:SPARE]], axis=0)
    flat_row = rank * count + jnp.arange(count)
    return jnp.where((flat_row < layout_rows()[1])[:, None], shard, shifted).astype(jnp.float32)


def adam_update(params, moment_one, moment_two, clipped, step_number):
    moment_one = BETA_ONE * moment_one + (1.0 - BETA_ONE) * clipped
    moment_two = BETA_TWO * moment_two + (1.0 - BETA_TWO) * clipped * clipped
    corrected_one = moment_one / (1.0 - BETA_ONE**step_number)
    corrected_two = moment_two / (1.0 - BETA_TWO**step_number)
    params = params - RATE * (corrected_one / (jnp.sqrt(corrected_two) + ADAM_EPS) + DECAY * params)
    return (params, moment_one, moment_two)


def nesterov(master_rows, momentum_rows, mean_delta):
    momentum_next = OUTER_MOM * momentum_rows + mean_delta
    return (master_rows - OUTER_RATE * (mean_delta + OUTER_MOM * momentum_next), momentum_next)


def post_rows_local(reduced):
    head_start = layout_rows()[4]
    rank, count = lax.axis_index("dp"), reduced.shape[0]
    return jnp.concatenate(
        [
            jnp.where(rank == row // count, reduced[row % count : row % count + 1], 0.0)
            for row in (head_start - 2, head_start - 1)
        ],
        axis=0,
    )


def per_device(
    pixels,
    counts,
    labels,
    text,
    master,
    outer_momentum,
    first_moment,
    second_moment,
    eval_pixels,
    eval_counts,
    eval_labels,
):
    params = master
    moment_one = first_moment[0]
    moment_two = second_moment[0]
    norm_list, loss_list, count_list, post_list = ([], [], [], [])
    weights = fetch_weights(params)
    slots = pixels.shape[2]
    step_pixels, step_counts, step_labels = pixels[0], counts[0], labels[0]
    group, worker = lax.axis_index("group"), lax.axis_index("group")
    if on_grid():
        step_pixels = to_planes(step_pixels)
        step_counts, step_labels = to_planes(step_counts), to_planes(step_labels)
        plane = place()[2]
        worker = plane % 2 * 2 + plane // 2
    live = (jnp.arange(slots)[None, :] < step_counts).astype(jnp.float32).reshape(-1)
    loss_total, grad_total = micro_step(
        weights,
        step_pixels.reshape((-1,) + pixels.shape[3:]),
        live,
        step_labels.reshape(-1),
        text,
        True,
    )
    reduced = reduce_rows(grad_total)
    image_total = jnp.sum(counts[0]).astype(jnp.float32)
    squares = jnp.sum(reduced * reduced)
    post_local = post_rows_local(reduced)
    groups = lax.axis_size("group")
    at_worker = (jnp.arange(groups) == worker).astype(jnp.float32)
    at_group = (jnp.arange(groups) == group).astype(jnp.float32)
    figures = jnp.stack([at_group * image_total, at_group * squares, at_worker * loss_total])
    figures, posts = lax.psum(
        (figures, jnp.where(at_group[:, None, None] > 0, post_local[None], 0.0)), ("group", "dp")
    )
    count_all, square_all, loss_all = [jnp.sum(row * at_group) for row in figures]
    post_all = lax.dynamic_index_in_dim(posts, group, keepdims=False)
    gradient = reduced / count_all
    grad_norm = jnp.sqrt(square_all) / count_all
    clip_factor = CLIP_MAX / jnp.maximum(grad_norm, CLIP_MAX)
    clipped = gradient * clip_factor
    params, moment_one, moment_two = adam_update(params, moment_one, moment_two, clipped, STEP)
    norm_list.append(grad_norm)
    loss_list.append(loss_all)
    count_list.append(count_all)
    post_list.append(post_all / count_all * clip_factor)
    delta = master - params
    mean_delta = lax.psum(delta.astype(jnp.bfloat16), "group").astype(jnp.float32) / groups
    new_master, new_outer = nesterov(master, outer_momentum, mean_delta)
    soup_rows = fetch_weights(new_master)
    eval_live = (jnp.arange(eval_pixels.shape[0]) < eval_counts[0]).astype(jnp.float32)
    eval_losses, unused_grads = micro_step(
        soup_rows, eval_pixels, eval_live, eval_labels, text, False
    )
    return (
        new_master,
        new_outer,
        moment_one[None],
        moment_two[None],
        jnp.stack(norm_list)[None],
        jnp.stack(loss_list)[None],
        jnp.stack(count_list)[None],
        jnp.stack(post_list)[None],
        eval_losses,
    )


def solution(mesh):
    return jax.shard_map(
        per_device,
        mesh=mesh,
        in_specs=(
            P(None, None, ("group", "dp"), None, None),
            P(None, None, ("group", "dp")),
            P(None, None, ("group", "dp")),
            P(),
            P("dp", None),
            P("dp", None),
            P("group", "dp", None),
            P("group", "dp", None),
            P(("group", "dp"), None, None),
            P(("group", "dp")),
            P(("group", "dp")),
        ),
        out_specs=(
            P("dp", None),
            P("dp", None),
            P("group", "dp", None),
            P("group", "dp", None),
            P("group", None),
            P("group", None),
            P("group", None),
            P("group", None, None, None),
            P(("group", "dp")),
        ),
        check_vma=False,
    )
```

```python
import functools

import jax
import jax.numpy as jnp
from jax import lax
from jax.experimental import pallas as pl
from jax.experimental.pallas import tpu as pltpu
from jax.sharding import PartitionSpec as P

MESH = pl.DeviceIdType.MESH

D = 768
HEADS = 12
HEAD = 64
FF = 3072
PATCH_IN = 3072
EMB = 512
CLASSES = 1000
LAYERS = 2
MICRO = 2
STEP = 10
SEQ = 50
ROWS_RAW = 22079


LN_EPS = 1e-05
NORM_EPS = 1e-06
LOGIT_SCALE = 50.0
SMOOTH = 0.1
CLIP_MAX = 0.02
BETA_ONE = 0.9
BETA_TWO = 0.98
ADAM_EPS = 1e-08
RATE = 0.02
DECAY = 0.1
OUTER_RATE = 0.7
OUTER_MOM = 0.9
GELU_SLOPE = 1.702
SPARE = 13


def layout_rows():
    table_start = PATCH_IN
    layer_start = table_start + SEQ + 1
    block_size = 4 * D + 2 * FF
    norm_start = layer_start + LAYERS * block_size
    head_start = norm_start + 4 * LAYERS + 4
    return (table_start, layer_start, block_size, norm_start, head_start)


TOKENS = 56
CLASS_AT = 49
PAIR = 2 * TOKENS
BLOCK = 3072
TAIL_START = BLOCK + SEQ + 1 + SPARE + LAYERS * (4 * D + 2 * FF)
TAIL_ROWS = 544
HEAD_AT = 4 * LAYERS + 4
TABLE_ROWS = SEQ + 1 + SPARE
LOW_COLS = 2 * FF
FIRST_LAYER = BLOCK + TABLE_ROWS
DENSE_END = FIRST_LAYER + 4 * D + 2 * FF + 3 * D


def dot(first, second, first_dim=1, second_dim=0):
    return lax.dot_general(
        first,
        second,
        (((first_dim,), (second_dim,)), ((), ())),
        preferred_element_type=jnp.float32,
    )


def low(values):
    return values.astype(jnp.bfloat16)


def norm_parts(values):
    centred = values - jnp.mean(values, -1, keepdims=True)
    scale = lax.rsqrt(jnp.mean(centred * centred, -1, keepdims=True) + LN_EPS)
    return (centred * scale, scale)


def norm_back(values, gain, grad):
    unit, scale = norm_parts(values)
    weighted = grad * gain
    mean_one = jnp.mean(weighted, -1, keepdims=True)
    mean_two = jnp.mean(weighted * unit, -1, keepdims=True)
    return (scale * (weighted - mean_one - unit * mean_two), grad * unit)


def wide(values, rows):
    return jnp.concatenate(
        [values, jnp.zeros((rows - values.shape[0], values.shape[1]), values.dtype)], axis=0
    )


def head_mask(rows, lanes, first_head):
    row = lax.broadcasted_iota(jnp.int32, (rows, lanes), 0)
    lane = lax.broadcasted_iota(jnp.int32, (rows, lanes), 1)
    return (lane // HEAD + first_head) == row


def lane_pick(values, head):
    lane = lax.broadcasted_iota(jnp.int32, values.shape, 1)
    return jnp.where(lane // HEAD == head, values, jnp.zeros_like(values))


def stack_heads(values):
    return jnp.concatenate([lane_pick(values, head) for head in range(4)], axis=0)


def fold_heads(values):
    rows = values.shape[0] // 4
    total = lane_pick(values[:rows], 0)
    for head in range(1, 4):
        total = total + lane_pick(values[head * rows : (head + 1) * rows], head)
    return total


def soft(scores):
    scores = scores - jnp.max(scores, -1, keepdims=True)
    grown = jnp.exp(scores)
    return grown / jnp.sum(grown, -1, keepdims=True)


def pair_bias():
    row = lax.broadcasted_iota(jnp.int32, (PAIR, PAIR), 0)
    col = lax.broadcasted_iota(jnp.int32, (PAIR, PAIR), 1)
    fits = (row // TOKENS == col // TOKENS) & (col % TOKENS < SEQ)
    return jnp.where(fits, 0.0, -1e30)


def class_bias():
    row = lax.broadcasted_iota(jnp.int32, (32, PAIR), 0)
    col = lax.broadcasted_iota(jnp.int32, (32, PAIR), 1)
    fits = (row // 16 == col // TOKENS) & (col % TOKENS < SEQ)
    return jnp.where(fits, 0.0, -1e30)


def spread_heads(values):
    keep = head_mask(16, D, 0)
    rows = jnp.broadcast_to(values[:, None, :], (8, 16, D))
    return jnp.where(keep[None], rows, 0.0).reshape(128, D)


def unspread_heads(values):
    keep = head_mask(16, D, 0)
    return jnp.sum(jnp.where(keep[None], values.reshape(8, 16, D), 0.0), axis=1)


def tower_kernel(images, with_grads, *refs):
    rows_all = images * TOKENS
    pairs = images // 2
    (w_hbm, pix_hbm, text_ref, label_ref, live_ref), refs = refs[:5], refs[5:]
    if with_grads:
        (g_hbm, factor_ref, extra_ref), refs = refs[:3], refs[3:]
    else:
        (loss_ref,), refs = refs[:1], refs[1:]
    (wbuf, tail, table, pix, emb, hid0, mid0, hid1, acc, qkv, norm_a, norm_b, mixed, pre, act), refs = (
        refs[:15],
        refs[15:],
    )
    (norm_c, kv), refs = refs[:2], refs[2:]
    if with_grads:
        (dhid, dqkv, gb, dmix, stage, stage_sem), refs = refs[:6], refs[6:]
    (wsem, small_sem) = refs

    layer_at = [FIRST_LAYER + index * (4 * D + 2 * FF) for index in range(LAYERS)]
    order = [0]
    for start in layer_at:
        order += [start, start + 4 * D, start + 4 * D + FF]
    if with_grads:
        order += [layer_at[0] + 4 * D + FF, layer_at[0] + 4 * D, layer_at[0]]
    slot_of = [0, 1, 2, 0, 1, 2, 0, 0, 2, 1]

    def fetch(index):
        return pltpu.make_async_copy(
            w_hbm.at[pl.ds(order[index], BLOCK)], wbuf.at[slot_of[index]], wsem.at[slot_of[index]]
        )

    load_pix = pltpu.make_async_copy(pix_hbm, pix, small_sem.at[0])
    load_tail = pltpu.make_async_copy(
        w_hbm.at[pl.ds(TAIL_START, TAIL_ROWS)], tail, small_sem.at[1]
    )
    load_table = pltpu.make_async_copy(w_hbm.at[pl.ds(BLOCK, TABLE_ROWS)], table, small_sem.at[2])
    fetch(0).start()
    load_pix.start()
    load_table.start()
    load_tail.start()
    fetch(1).start()
    fetch(2).start()

    def chunks_of(count=rows_all // PAIR):
        return pl.loop(0, count)

    def rows_at(index):
        return pl.ds(pl.multiple_of(index * PAIR, PAIR), PAIR)

    def norm_row(index):
        return tail[0:16, :].astype(jnp.float32)[index : index + 1]

    def class_rows(ref):
        picked = [ref[TOKENS * i + CLASS_AT : TOKENS * i + CLASS_AT + 1, :] for i in range(images)]
        if images < 8:
            picked.append(jnp.zeros((8 - images, ref.shape[1]), ref.dtype))
        return jnp.concatenate(picked, axis=0)

    def add_class_rows(ref, values):
        for i in range(images):
            at = slice(TOKENS * i + CLASS_AT, TOKENS * i + CLASS_AT + 1)
            ref[at, :] = ref[at, :] + values[i : i + 1]

    def layer_norm_into(source, target, gain_row):
        gain, bias = norm_row(gain_row), norm_row(gain_row + 1)

        @chunks_of()
        def _(index):
            rows = rows_at(index)
            unit, _ = norm_parts(source[rows, :])
            target[rows, :] = (unit * gain + bias).astype(target.dtype)

    load_table.wait()
    load_tail.wait()
    load_pix.wait()
    fetch(0).wait()
    emb[...] = dot(pix[...], wbuf[0])
    fetch(3).start()
    rows_table = table[...].astype(jnp.float32)
    added = pltpu.roll(rows_table, TABLE_ROWS - 2, 0)[:TOKENS]
    token = lax.broadcasted_iota(jnp.int32, (TOKENS, D), 0)
    added = jnp.where(token == CLASS_AT, rows_table[0:1] + rows_table[1:2], added)
    added = jnp.where(token < SEQ, added, 0.0)

    gain, bias = norm_row(0), norm_row(1)

    @chunks_of()
    def _(index):
        rows = rows_at(index)
        values = emb[rows, :] + jnp.concatenate([added, added], axis=0)
        emb[rows, :] = values
        unit, _ = norm_parts(values)
        hid0[rows, :] = unit * gain + bias

    layer_norm_into(hid0, norm_a, 2)
    fetch(1).wait()

    @pl.loop(0, 3)
    def _(part):
        at = pl.ds(pl.multiple_of(part * D, D), D)
        qkv[:, at] = low(dot(norm_a[...], wbuf[1, at, :]))

    bias_pair = pair_bias()

    def lanes(part, group):
        return slice(part * D + group * 256, part * D + (group + 1) * 256)

    def pair_soft(queries, keys):
        scores = dot(queries, keys, 1, 1) * HEAD ** (-0.5)
        scores = scores.reshape(4, PAIR, PAIR) + bias_pair[None]
        return soft(scores).reshape(4 * PAIR, PAIR)

    @pl.loop(0, pairs)
    def _(index):
        rows = rows_at(index)
        for group in range(3):
            queries = stack_heads(qkv[rows, lanes(0, group)])
            probs = low(pair_soft(queries, qkv[rows, lanes(1, group)]))
            out = dot(probs, qkv[rows, lanes(2, group)])
            mixed[rows, lanes(0, group)] = low(fold_heads(out))

    acc[...] = dot(mixed[...], wbuf[1, 3 * D : 4 * D, :])
    fetch(4).start()
    gain2, bias2 = norm_row(4), norm_row(5)

    @chunks_of()
    def _(index):
        rows = rows_at(index)
        values = hid0[rows, :] + acc[rows, :]
        mid0[rows, :] = values
        unit, _ = norm_parts(values)
        norm_b[rows, :] = low(unit * gain2 + bias2)

    fetch(2).wait()

    @pl.loop(0, 3)
    def _(part):
        at = pl.ds(pl.multiple_of(part * 1024, 1024), 1024)
        values = dot(norm_b[...], wbuf[2, at, :], 1, 1)
        if with_grads:
            pre[:, at] = low(values)
        act[:, at] = low(values * jax.nn.sigmoid(GELU_SLOPE * values))

    fetch(5).start()
    fetch(3).wait()
    acc[...] = dot(act[...], wbuf[0])
    fetch(6).start()
    gain3, bias3 = norm_row(6), norm_row(7)

    @chunks_of()
    def _(index):
        rows = rows_at(index)
        values = mid0[rows, :] + acc[rows, :]
        hid1[rows, :] = values
        unit, _ = norm_parts(values)
        norm_c[rows, :] = low(unit * gain3 + bias3)

    fetch(4).wait()

    @pl.loop(0, 2)
    def _(part):
        kv[:, pl.ds(pl.multiple_of(part * D, D), D)] = low(
            dot(norm_c[...], wbuf[1, pl.ds(pl.multiple_of(part * D + D, D), D), :])
        )

    class_hid = class_rows(hid1)
    unit_one, _ = norm_parts(class_hid)
    class_a = low(wide(unit_one * gain3 + bias3, 16))
    class_q = low(dot(class_a, wbuf[1, 0:D, :]))
    spread_q = low(spread_heads(class_q[:8].astype(jnp.float32)))
    bias_class = class_bias()
    class_probs, outs = [], []
    for pair in range(pairs):
        rows = slice(pair * PAIR, (pair + 1) * PAIR)
        scores = dot(spread_q[32 * pair : 32 * pair + 32], kv[rows, 0:D], 1, 1)
        probs = soft(scores * HEAD ** (-0.5) + bias_class)
        class_probs.append(probs)
        outs.append(dot(low(probs), kv[rows, D : 2 * D]))
    for _ in range(4 - pairs):
        outs.append(jnp.zeros((32, D), jnp.float32))
    class_mix = low(wide(unspread_heads(jnp.concatenate(outs, axis=0)), 16))
    class_mid = class_hid + dot(class_mix, wbuf[1, 3 * D : 4 * D, :])[:8]
    unit_two, _ = norm_parts(class_mid)
    gain4, bias4 = norm_row(8), norm_row(9)
    class_b = low(wide(unit_two * gain4 + bias4, 16))
    fetch(5).wait()
    class_pre = dot(class_b, wbuf[2], 1, 1)
    gate = jax.nn.sigmoid(GELU_SLOPE * class_pre)
    class_act = low(class_pre * gate)
    fetch(6).wait()
    class_out = class_mid + dot(class_act, wbuf[0])[:8]
    gain5, bias5 = norm_row(10), norm_row(11)
    unit_post, _ = norm_parts(class_out)
    pooled = low(wide(unit_post * gain5 + bias5, 16))

    pooled_out = dot(pooled, tail[...], 1, 1)
    pooled_out = jnp.concatenate([pooled_out, jnp.zeros((16, 640 - TAIL_ROWS), jnp.float32)], axis=1)
    embedded = pltpu.roll(pooled_out, 640 - HEAD_AT, 1)[:8, :EMB]
    length = lax.rsqrt(jnp.sum(embedded * embedded, -1, keepdims=True) + NORM_EPS)
    unit_rows = embedded * length
    logits = LOGIT_SCALE * dot(low(wide(unit_rows, 16)), text_ref[...], 1, 1)[:8]
    top = jnp.max(logits, -1, keepdims=True)
    log_total = top + jnp.log(jnp.sum(jnp.exp(logits - top), -1, keepdims=True))
    log_probs = logits - log_total
    classes = lax.broadcasted_iota(jnp.int32, logits.shape, 1)
    target = jnp.where(classes == label_ref[...], 1.0 - SMOOTH, 0.0) + SMOOTH / CLASSES
    live = live_ref[...]
    losses = -live * jnp.sum(target * log_probs, -1, keepdims=True)
    if not with_grads:
        loss_ref[...] = jnp.broadcast_to(losses, loss_ref.shape)
        return

    grad_raw = low(wide(LOGIT_SCALE * ((jnp.exp(log_probs) - target) * live), 16))
    grad_unit = dot(grad_raw, text_ref[...])[:8]
    along = jnp.sum(grad_unit * embedded, -1, keepdims=True)
    grad_embed = grad_unit * length - embedded * (length * length * length * along)
    grad_embed = low(wide(grad_embed, 16))
    grad_tail = jnp.concatenate(
        [grad_embed.astype(jnp.float32), jnp.zeros((16, 640 - EMB), jnp.float32)], axis=1
    )
    grad_tail = low(pltpu.roll(grad_tail, HEAD_AT, 1)[:, :TAIL_ROWS])
    grad_pooled = dot(grad_tail, tail[...])[:8]

    def put_extra(row, values):
        extra_ref[row : row + 1, :] = values

    extra_ref[...] = jnp.zeros_like(extra_ref)
    lane = lax.broadcasted_iota(jnp.int32, (1, D), 1)
    put_extra(12, jnp.where(lane == 0, jnp.sum(losses), jnp.where(lane == 1, jnp.sum(live), 0.0)))

    def class_norm_back(values, gain_row, grad):
        result, terms = norm_back(values, norm_row(gain_row), grad)
        put_extra(gain_row, jnp.sum(terms, 0, keepdims=True))
        put_extra(gain_row + 1, jnp.sum(grad, 0, keepdims=True))
        return result

    grad_out = class_norm_back(class_out, 10, grad_pooled)

    grad_b = low(wide(grad_out, 16))
    grad_act = dot(grad_b, wbuf[0], 1, 1)
    grad_pre = low(grad_act * (gate + GELU_SLOPE * class_pre * gate * (1.0 - gate)))
    fetch(7).start()
    grad_mid = grad_out + class_norm_back(class_mid, 8, dot(grad_pre, wbuf[2])[:8])
    fetch(8).start()
    grad_proj = low(wide(grad_mid, 16))
    grad_mix = low(dot(grad_proj, wbuf[1, 3 * D : 4 * D, :], 1, 1))
    spread_g = low(spread_heads(grad_mix[:8].astype(jnp.float32)))
    grad_qs = []
    for pair in range(pairs):
        rows = slice(pair * PAIR, (pair + 1) * PAIR)
        some_g, some_q = spread_g[32 * pair : 32 * pair + 32], spread_q[32 * pair : 32 * pair + 32]
        probs = class_probs[pair]
        grad_probs = dot(some_g, kv[rows, D : 2 * D], 1, 1)
        dqkv[rows, 2 * D : 3 * D] = low(dot(low(probs), some_g, 0, 0))
        grad_scores = probs * (grad_probs - jnp.sum(grad_probs * probs, -1, keepdims=True))
        grad_scores = low(grad_scores)
        grad_qs.append(dot(grad_scores, kv[rows, 0:D]))
        dqkv[rows, D : 2 * D] = low(dot(grad_scores, some_q, 0, 0) * HEAD ** (-0.5))
    grad_q = low(wide(unspread_heads(jnp.concatenate(grad_qs, axis=0)) * HEAD ** (-0.5), 16))

    def pack(first, second, at, width):
        factor_ref[:, at : at + width] = low(
            jnp.concatenate([first[:8].astype(jnp.float32), second[:8].astype(jnp.float32)], axis=0)
        )

    pack(grad_pre, class_act, 0, FF)
    pack(class_a, class_mix, FF, D)
    pack(grad_q, grad_proj, FF + D, D)
    pack(class_b, grad_b, FF + 2 * D, D)
    embed_wide = jnp.concatenate(
        [grad_embed.astype(jnp.float32), jnp.zeros((16, D - EMB), jnp.float32)], axis=1
    )
    pack(embed_wide, pooled, FF + 3 * D, D)

    started = [0]

    def push(slot, at):
        return pltpu.make_async_copy(stage.at[slot], g_hbm.at[pl.ds(at, D)], stage_sem.at[slot])

    def weight_grad(left, left_at, right, right_at, at, count):
        base = started[0]

        def one(block):
            slot = lax.rem(base + block, 2)

            @pl.when(base + block >= 2)
            def _():
                push(slot, at).wait()

            from_lane = pl.multiple_of(left_at + block * D, D) if count > 1 else left_at
            stage[slot] = low(dot(left[:, pl.ds(from_lane, D)], right[:, right_at : right_at + D], 0, 0))
            push(slot, pl.multiple_of(at + block * D, 16)).start()

        if count > 1:
            pl.loop(0, count)(one)
        else:
            one(0)
        started[0] = base + count

    def norm_back_rows(values, gain_row, grad, finish):
        gain = norm_row(gain_row)
        extra_ref[gain_row : gain_row + 2, :] = jnp.zeros((2, D), jnp.float32)

        @chunks_of()
        def _(index):
            rows = rows_at(index)
            grad_rows = grad[rows, :]
            result, terms = norm_back(values[rows, :], gain, grad_rows)
            at = slice(gain_row, gain_row + 1)
            extra_ref[at, :] = extra_ref[at, :] + jnp.sum(terms, 0, keepdims=True)
            at = slice(gain_row + 1, gain_row + 2)
            extra_ref[at, :] = extra_ref[at, :] + jnp.sum(grad_rows, 0, keepdims=True)
            finish(rows, result)

    weight_grad(norm_c, 0, dqkv, D, layer_at[1] + D, 1)
    weight_grad(norm_c, 0, dqkv, 2 * D, layer_at[1] + 2 * D, 1)
    acc[...] = dot(dqkv[:, D : 2 * D], wbuf[1, D : 2 * D, :], 1, 1)
    acc[...] = acc[...] + dot(dqkv[:, 2 * D : 3 * D], wbuf[1, 2 * D : 3 * D, :], 1, 1)
    add_class_rows(acc, dot(grad_q, wbuf[1, 0:D, :], 1, 1))
    fetch(9).start()

    def finish_second(rows, result):
        dhid[rows, :] = result

    norm_back_rows(hid1, 6, acc, finish_second)
    add_class_rows(dhid, grad_mid)

    gb[...] = low(dhid[...])
    fetch(7).wait()
    weight_grad(act, 0, gb, 0, layer_at[0] + 4 * D + FF, FF // D)

    @pl.loop(0, 3)
    def _(part):
        at = pl.ds(pl.multiple_of(part * 1024, 1024), 1024)
        grad_rows = dot(gb[...], wbuf[0, at, :], 1, 1)
        values = pre[:, at].astype(jnp.float32)
        gates = jax.nn.sigmoid(GELU_SLOPE * values)
        pre[:, at] = low(grad_rows * (gates + GELU_SLOPE * values * gates * (1.0 - gates)))

    weight_grad(pre, 0, norm_b, 0, layer_at[0] + 4 * D, FF // D)
    fetch(8).wait()
    acc[...] = dot(pre[...], wbuf[2])

    def finish_mid(rows, result):
        total = dhid[rows, :] + result
        dhid[rows, :] = total
        gb[rows, :] = low(total)

    norm_back_rows(mid0, 4, acc, finish_mid)
    weight_grad(mixed, 0, gb, 0, layer_at[0] + 3 * D, 1)
    fetch(9).wait()
    dmix[...] = low(dot(gb[...], wbuf[1, 3 * D : 4 * D, :], 1, 1))

    @pl.loop(0, pairs)
    def _(index):
        rows = rows_at(index)
        for group in range(3):
            queries = stack_heads(qkv[rows, lanes(0, group)])
            keys = qkv[rows, lanes(1, group)]
            probs = pair_soft(queries, keys)
            some_g = stack_heads(dmix[rows, lanes(0, group)])
            grad_probs = dot(some_g, qkv[rows, lanes(2, group)], 1, 1)
            dqkv[rows, lanes(2, group)] = low(dot(low(probs), some_g, 0, 0))
            grad_scores = probs * (grad_probs - jnp.sum(grad_probs * probs, -1, keepdims=True))
            grad_scores = low(grad_scores)
            grad_queries = fold_heads(dot(grad_scores, keys))
            dqkv[rows, lanes(0, group)] = low(grad_queries * HEAD ** (-0.5))
            grad_keys = dot(grad_scores, queries, 0, 0)
            dqkv[rows, lanes(1, group)] = low(grad_keys * HEAD ** (-0.5))

    for part in range(3):
        weight_grad(norm_a, 0, dqkv, part * D, layer_at[0] + part * D, 1)
    acc[...] = dot(dqkv[:, 0:D], wbuf[1, 0:D, :], 1, 1)
    for part in (1, 2):
        at = slice(part * D, (part + 1) * D)
        acc[...] = acc[...] + dot(dqkv[:, at], wbuf[1, at, :], 1, 1)

    def finish_first(rows, result):
        dhid[rows, :] = dhid[rows, :] + result

    norm_back_rows(hid0, 2, acc, finish_first)

    def finish_embedding(rows, result):
        dhid[rows, :] = result
        gb[rows, :] = low(result)

    norm_back_rows(emb, 0, dhid, finish_embedding)
    weight_grad(pix, 0, gb, 0, 0, PATCH_IN // D)
    grad_tokens = dhid[0:TOKENS, :]
    for i in range(1, images):
        grad_tokens = grad_tokens + dhid[TOKENS * i : TOKENS * (i + 1), :]
    class_grad = grad_tokens[CLASS_AT : CLASS_AT + 1]
    grad_tokens = jnp.concatenate(
        [grad_tokens, jnp.zeros((TABLE_ROWS - TOKENS, D), jnp.float32)], axis=0
    )
    grad_table = pltpu.roll(grad_tokens, 2, 0)
    row = lax.broadcasted_iota(jnp.int32, (TABLE_ROWS, D), 0)
    grad_table = jnp.where(row < 2, class_grad, jnp.where(row < SEQ + 1, grad_table, 0.0))
    table[...] = low(grad_table)
    put_table = pltpu.make_async_copy(table, g_hbm.at[pl.ds(BLOCK, TABLE_ROWS)], small_sem.at[0])
    put_table.start()
    put_table.wait()
    for slot in range(2):
        push(slot, 0).wait()


def run_tower(weights, pixel_rows, label_row, live_mask, text, with_grads):
    images = label_row.shape[0]
    rows_all = images * TOKENS
    bf16, f32 = jnp.bfloat16, jnp.float32
    labels = jnp.zeros((8, 1), jnp.int32).at[:images, 0].set(label_row)
    live = jnp.zeros((8, 1), f32).at[:images, 0].set(live_mask)
    scratch = [
        pltpu.VMEM((3, BLOCK, D), bf16),
        pltpu.VMEM((TAIL_ROWS, D), bf16),
        pltpu.VMEM((TABLE_ROWS, D), bf16),
        pltpu.VMEM((rows_all, PATCH_IN), bf16),
        pltpu.VMEM((rows_all, D), f32),
        pltpu.VMEM((rows_all, D), f32),
        pltpu.VMEM((rows_all, D), f32),
        pltpu.VMEM((rows_all, D), f32),
        pltpu.VMEM((rows_all, D), f32),
        pltpu.VMEM((rows_all, 3 * D), bf16),
        pltpu.VMEM((rows_all, D), bf16),
        pltpu.VMEM((rows_all, D), bf16),
        pltpu.VMEM((rows_all, D), bf16),
        pltpu.VMEM((rows_all if with_grads else 16, FF), bf16),
        pltpu.VMEM((rows_all, FF), bf16),
        pltpu.VMEM((rows_all, D), bf16),
        pltpu.VMEM((rows_all, 2 * D), bf16),
    ]
    if with_grads:
        scratch += [
            pltpu.VMEM((rows_all, D), f32),
            pltpu.VMEM((rows_all, 3 * D), bf16),
            pltpu.VMEM((rows_all, D), bf16),
            pltpu.VMEM((rows_all, D), bf16),
            pltpu.VMEM((2, D, D), bf16),
            pltpu.SemaphoreType.DMA((2,)),
        ]
        out_shape = (
            jax.ShapeDtypeStruct((grad_rows_kept(weights.shape[0]), D), bf16),
            jax.ShapeDtypeStruct((16, LOW_COLS), bf16),
            jax.ShapeDtypeStruct((16, D), f32),
        )
        out_specs = (
            pl.BlockSpec(memory_space=pl.ANY),
            pl.BlockSpec(memory_space=pltpu.VMEM),
            pl.BlockSpec(memory_space=pltpu.VMEM),
        )
    else:
        out_shape = jax.ShapeDtypeStruct((8, 128), f32)
        out_specs = pl.BlockSpec(memory_space=pltpu.VMEM)
    scratch += [pltpu.SemaphoreType.DMA((3,)), pltpu.SemaphoreType.DMA((3,))]
    vmem = pl.BlockSpec(memory_space=pltpu.VMEM)
    hbm = pl.BlockSpec(memory_space=pl.ANY)
    return pl.pallas_call(
        functools.partial(tower_kernel, images, with_grads),
        out_shape=out_shape,
        in_specs=[hbm, hbm, vmem, vmem, vmem],
        out_specs=out_specs,
        scratch_shapes=scratch,
        compiler_params=pltpu.CompilerParams(vmem_limit_bytes=60 * 2**20),
        name="train" if with_grads else "evaluate",
    )(weights, pixel_rows, text, labels, live)


def grad_rows_kept(rows):
    if not on_grid():
        return DENSE_END
    plane_rows = rows // 4
    return (DENSE_END + plane_rows - 1) // plane_rows * plane_rows


def on_grid():
    return lax.axis_size("group") == 4 and lax.axis_size("dp") == 8


def place():
    worker = lax.axis_index("group")
    rank = lax.axis_index("dp")
    return (worker // 2, worker % 2, rank // 2, rank % 2)


def device_at(y, c, z, x):
    return (y * 2 + c, z * 2 + x)


def chunk_rows(total, count):
    units = total // 16
    chunks = []
    start = 0
    for index in range(count):
        size = units * (index + 1) // count - units * index // count
        first = size // 2 if index % 2 else size - size // 2
        chunks.append((start * 16, first * 16, (size - first) * 16))
        start += size
    return chunks


def gather_kernel(chunks, part_ref, full_ref, local_sem, sends, recvs):
    half_cols = part_ref.shape[1]
    y, c, z, x = place()
    cols = pl.ds(pl.multiple_of(c * half_cols, half_cols), half_cols)
    over_x = device_at(y, c, z, 1 - x)
    over_y = device_at(1 - y, c, z, x)
    sibling = device_at(y, 1 - c, z, x)
    along_z = [device_at(y, c, (z + step) % 4, x) for step in (1, 2, 3)]
    barrier = pltpu.get_barrier_semaphore()
    for other in [over_x, over_y, sibling] + along_z:
        pl.semaphore_signal(barrier, inc=1, device_id=other, device_id_type=MESH)
    local = pltpu.make_async_copy(part_ref, full_ref.at[z, x, y, :, cols], local_sem)
    local.start()
    pl.semaphore_wait(barrier, 6)

    def send(piece, other, stage, index):
        pltpu.make_async_remote_copy(
            src_ref=piece,
            dst_ref=piece,
            send_sem=sends.at[stage, index],
            recv_sem=recvs.at[stage, index],
            device_id=other,
            device_id_type=MESH,
        ).start()

    def arrived(piece, stage, index):
        pltpu.make_async_copy(piece, piece, recvs.at[stage, index]).wait()

    def sent(piece, stage, index):
        pltpu.make_async_copy(piece, piece, sends.at[stage, index]).wait()

    def pieces(index):
        start, first, second = chunks[index]
        rows = pl.ds(start, first + second)
        rows_a = pl.ds(start, first)
        rows_b = pl.ds(start + first, second)
        return {
            0: full_ref.at[pl.ds(0, 3), 0, 0, rows, cols],
            1: full_ref.at[:, x, y, rows_a, cols],
            2: full_ref.at[:, x, y, rows_b, cols],
            3: full_ref.at[:, x, :, rows_a, cols],
            4: full_ref.at[:, :, y, rows_b, cols],
            5: full_ref.at[:, :, :, rows, cols],
        }

    total = len(chunks)
    for step in range(total + 5):
        if step < total:
            start, first, second = chunks[step]
            rows = pl.ds(start, first + second)
            for other in along_z:
                pltpu.make_async_remote_copy(
                    src_ref=part_ref.at[rows],
                    dst_ref=full_ref.at[z, x, y, rows, cols],
                    send_sem=sends.at[0, step],
                    recv_sem=recvs.at[0, step],
                    device_id=other,
                    device_id_type=MESH,
                ).start()
        if step == 0:
            local.wait()
        index = step - 1
        if 0 <= index < total:
            block = pieces(index)
            arrived(block[0], 0, index)
            send(block[1], over_y, 1, index)
            send(block[2], over_x, 2, index)
        index = step - 2
        if 0 <= index < total:
            block = pieces(index)
            arrived(block[1], 1, index)
            send(block[3], over_x, 3, index)
            arrived(block[2], 2, index)
            send(block[4], over_y, 4, index)
        index = step - 3
        if 0 <= index < total:
            block = pieces(index)
            arrived(block[3], 3, index)
            arrived(block[4], 4, index)
            send(block[5], sibling, 5, index)
    for index in range(total):
        block = pieces(index)
        arrived(block[5], 5, index)
        for stage in range(6):
            sent(block[stage], stage, index)


def gather_rows(part, shard_rows):
    chunks = chunk_rows(part.shape[0], 8)
    full = pl.pallas_call(
        functools.partial(gather_kernel, chunks),
        out_shape=jax.ShapeDtypeStruct((4, 2, 2, part.shape[0], 2 * part.shape[1]), part.dtype),
        in_specs=[pl.BlockSpec(memory_space=pl.ANY)],
        out_specs=pl.BlockSpec(memory_space=pl.ANY),
        scratch_shapes=[
            pltpu.SemaphoreType.DMA,
            pltpu.SemaphoreType.DMA((6, len(chunks))),
            pltpu.SemaphoreType.DMA((6, len(chunks))),
        ],
        compiler_params=pltpu.CompilerParams(collective_id=0, has_side_effects=True),
        name="gather",
    )(part)
    return full.reshape(8 * shard_rows, 2 * part.shape[1])


def reduce_kernel(
    chunks,
    low_from,
    grad_ref,
    factor_ref,
    extra_ref,
    own_ref,
    factors_ref,
    extras_ref,
    mine,
    first_sum,
    sum_a,
    sum_b,
    last_sum,
    load_sems,
    sends,
    recvs,
    small_sends,
    small_recvs,
):
    half_cols = mine.shape[-1]
    planes = grad_ref.shape[0]
    y, c, z, x = place()
    home_y, home_c = z % 2, z // 2
    at_home = jnp.logical_and(home_y == y, home_c == c)
    from_plane = 2 * c + y
    my_cols = pl.ds(pl.multiple_of(c * half_cols, half_cols), half_cols)
    other_cols = pl.ds(pl.multiple_of((1 - c) * half_cols, half_cols), half_cols)
    over_x = device_at(y, c, z, 1 - x)
    over_y = device_at(1 - y, c, z, x)
    sibling = device_at(y, 1 - c, z, x)
    barrier = pltpu.get_barrier_semaphore()
    for other in (over_x, over_y, sibling):
        pl.semaphore_signal(barrier, inc=1, device_id=other, device_id_type=MESH)
    for other in range(8):
        other_y, other_c, other_x = other // 4, other // 2 % 2, other % 2
        same = jnp.logical_and(y == other_y, jnp.logical_and(c == other_c, x == other_x))
        itself = jnp.logical_and(at_home, same)

        @pl.when(jnp.logical_not(itself))
        def _():
            pl.semaphore_signal(
                barrier,
                inc=1,
                device_id=device_at(other_y, other_c, from_plane, other_x),
                device_id_type=MESH,
            )

    def spans(index):
        start, first, second = chunks[index]
        start_a = sum(chunk[1] for chunk in chunks[:index])
        start_b = sum(chunk[2] for chunk in chunks[:index])
        return (
            pl.ds(start, first + second),
            pl.ds(start, first),
            pl.ds(start + first, second),
            pl.ds(start_a, first),
            pl.ds(start_b, second),
        )

    def send(source, target, other, stage, index):
        pltpu.make_async_remote_copy(
            src_ref=source,
            dst_ref=target,
            send_sem=sends.at[stage, index],
            recv_sem=recvs.at[stage, index],
            device_id=other,
            device_id_type=MESH,
        ).start()

    def arrived(piece, stage, index):
        pltpu.make_async_copy(piece, piece, recvs.at[stage, index]).wait()

    def sent(piece, stage, index):
        pltpu.make_async_copy(piece, piece, sends.at[stage, index]).wait()

    def load(index):
        rows = spans(index)[0]
        return pltpu.make_async_copy(
            grad_ref.at[:, :, :, rows, my_cols],
            mine.at[index % 2, :, :, :, pl.ds(0, rows.size)],
            load_sems.at[index % 2],
        )

    def send_core(index):
        rows = spans(index)[0]
        send(
            grad_ref.at[:, :, :, rows, other_cols],
            first_sum.at[:, :, :, rows],
            sibling,
            0,
            index,
        )

    def add(target, source):
        summed = target[...].astype(jnp.float32) + source[...].astype(jnp.float32)
        target[...] = summed.astype(target.dtype)

    total = len(chunks)
    load(0).start()
    pl.semaphore_wait(barrier, 3 + jnp.where(at_home, 7, 8))
    send_core(0)
    send_core(1)
    slot = (y * 2 + c) * 2 + x
    for other in range(8):
        other_z, other_x = other // 2, other % 2
        itself = jnp.logical_and(at_home, jnp.logical_and(z == other_z, x == other_x))
        for which, (source, target) in enumerate(
            ((extra_ref, extras_ref.at[slot]), (factor_ref, factors_ref.at[slot]))
        ):
            if which == 1 and other_z < low_from:
                continue

            @pl.when(jnp.logical_not(itself))
            def _():
                pltpu.make_async_remote_copy(
                    src_ref=source,
                    dst_ref=target,
                    send_sem=small_sends.at[which],
                    recv_sem=small_recvs.at[which],
                    device_id=device_at(home_y, home_c, other_z, other_x),
                    device_id_type=MESH,
                ).start()

            @pl.when(itself)
            def _():
                pltpu.make_async_copy(source, target, small_recvs.at[which]).start()

    for step in range(total + 4):
        index = step
        if index < total:
            if index + 1 < total:
                load(index + 1).start()
            if index + 2 < total:
                send_core(index + 2)
            rows, rows_a, rows_b, in_a, in_b = spans(index)
            load(index).wait()
            arrived(first_sum.at[:, :, :, rows], 0, index)

            @pl.loop(0, 4 * planes)
            def _(block):
                zz, rest = block // 4, block % 4
                add(
                    first_sum.at[zz, rest // 2, rest % 2, rows],
                    mine.at[index % 2, zz, rest // 2, rest % 2, pl.ds(0, rows.size)],
                )

            send(first_sum.at[:, 1 - x, :, rows_a], sum_a.at[:, :, in_a], over_x, 1, index)
            send(first_sum.at[:, :, 1 - y, rows_b], sum_b.at[:, :, in_b], over_y, 2, index)
        index = step - 1
        if 0 <= index < total:
            rows, rows_a, rows_b, in_a, in_b = spans(index)
            arrived(sum_a.at[:, :, in_a], 1, index)

            @pl.loop(0, 2 * planes)
            def _(block):
                add(
                    sum_a.at[block // 2, block % 2, in_a],
                    first_sum.at[block // 2, x, block % 2, rows_a],
                )

            send(sum_a.at[:, 1 - y, in_a], last_sum.at[:, rows_a], over_y, 3, index)
            arrived(sum_b.at[:, :, in_b], 2, index)

            @pl.loop(0, 2 * planes)
            def _(block):
                add(
                    sum_b.at[block // 2, block % 2, in_b],
                    first_sum.at[block // 2, block % 2, y, rows_b],
                )

            send(sum_b.at[:, 1 - x, in_b], last_sum.at[:, rows_b], over_x, 4, index)
        index = step - 2
        if 0 <= index < total:
            rows, rows_a, rows_b, in_a, in_b = spans(index)
            arrived(last_sum.at[:, rows_a], 3, index)
            arrived(last_sum.at[:, rows_b], 4, index)

            @pl.loop(0, planes)
            def _(block):
                add(last_sum.at[block, rows_a], sum_a.at[block, y, in_a])
                add(last_sum.at[block, rows_b], sum_b.at[block, x, in_b])

            for to_z in range(planes):
                itself = jnp.logical_and(at_home, z == to_z)
                source = last_sum.at[to_z, rows]
                target = own_ref.at[y, rows, my_cols]

                @pl.when(jnp.logical_not(itself))
                def _():
                    send(source, target, device_at(home_y, home_c, to_z, x), 5, index)

                @pl.when(itself)
                def _():
                    pltpu.make_async_copy(source, target, recvs.at[5, index]).start()

    for index in range(total):
        rows, rows_a, rows_b, in_a, in_b = spans(index)

        @pl.when(z < planes)
        def _():
            arrived(own_ref.at[:, rows], 5, index)

        sent(first_sum.at[:, :, :, rows], 0, index)
        sent(sum_a.at[:, :, in_a], 1, index)
        sent(sum_b.at[:, :, in_b], 2, index)
        sent(last_sum.at[:, rows_a], 3, index)
        sent(last_sum.at[:, rows_b], 4, index)

        kept = jnp.logical_and(at_home, z < planes)

        @pl.when(kept)
        def _():
            sent(last_sum.at[pl.ds(0, planes - 1), rows], 5, index)

        @pl.when(jnp.logical_not(kept))
        def _():
            sent(last_sum.at[:, rows], 5, index)

    def all_of(ref, count, sem):
        piece = ref.at[pl.ds(0, count)]
        pltpu.make_async_copy(piece, piece, sem).wait()

    all_of(extras_ref, 8, small_recvs.at[0])

    @pl.when(z >= low_from)
    def _():
        all_of(factors_ref, 8, small_recvs.at[1])

    @pl.when(at_home)
    def _():
        all_of(extras_ref, 7, small_sends.at[0])

    @pl.when(jnp.logical_not(at_home))
    def _():
        all_of(extras_ref, 8, small_sends.at[0])

    low_targets = 2 * (4 - low_from)
    low_kept = jnp.logical_and(at_home, z >= low_from)

    @pl.when(low_kept)
    def _():
        all_of(factors_ref, low_targets - 1, small_sends.at[1])

    @pl.when(jnp.logical_not(low_kept))
    def _():
        all_of(factors_ref, low_targets, small_sends.at[1])


def reduce_chunks(total, count, share):
    units = total // 16
    chunks = []
    start = 0
    for index in range(count):
        size = units * (index + 1) // count - units * index // count
        first = int(round(size * share))
        chunks.append((start * 16, first * 16, (size - first) * 16))
        start += size
    return chunks


def sum_on_plane(grad_rows, factors, extra, shard_rows):
    half_rows, width = shard_rows // 2, grad_rows.shape[1]
    planes = grad_rows.shape[0] // (2 * shard_rows)
    chunks = reduce_chunks(half_rows, 8, 0.75)
    most = max(first + second for _, first, second in chunks)
    half_cols = width // 2
    dtype = grad_rows.dtype
    low_from = (FIRST_LAYER + 4 * D + 2 * FF) // (2 * shard_rows)
    own, all_factors, all_extra = pl.pallas_call(
        functools.partial(reduce_kernel, chunks, low_from),
        out_shape=(
            jax.ShapeDtypeStruct((2, half_rows, width), dtype),
            jax.ShapeDtypeStruct((8,) + factors.shape, factors.dtype),
            jax.ShapeDtypeStruct((8,) + extra.shape, extra.dtype),
        ),
        in_specs=[pl.BlockSpec(memory_space=pl.ANY)] * 3,
        out_specs=[pl.BlockSpec(memory_space=pl.ANY)] * 3,
        scratch_shapes=[
            pltpu.VMEM((2, planes, 2, 2, most, half_cols), dtype),
            pltpu.VMEM((planes, 2, 2, half_rows, half_cols), dtype),
            pltpu.VMEM((planes, 2, sum(chunk[1] for chunk in chunks), half_cols), dtype),
            pltpu.VMEM((planes, 2, sum(chunk[2] for chunk in chunks), half_cols), dtype),
            pltpu.VMEM((planes, half_rows, half_cols), dtype),
            pltpu.SemaphoreType.DMA((2,)),
            pltpu.SemaphoreType.DMA((6, len(chunks))),
            pltpu.SemaphoreType.DMA((6, len(chunks))),
            pltpu.SemaphoreType.DMA((2,)),
            pltpu.SemaphoreType.DMA((2,)),
        ],
        compiler_params=pltpu.CompilerParams(
            collective_id=1, has_side_effects=True, vmem_limit_bytes=56 * 2**20
        ),
        name="reduce",
    )(grad_rows.reshape(planes, 2, 2, half_rows, width), factors, extra)
    return (own.reshape(shard_rows, width), all_factors, all_extra)


def to_planes(values):
    pairs = []
    for source in range(32):
        y, c, z, x = source // 16, source // 8 % 2, source // 2 % 4, source % 2
        pairs.append((source, (z % 2 * 2 + z // 2) * 8 + (2 * c + y) * 2 + x))
    return lax.ppermute(values, ("group", "dp"), pairs)


def fetch_weights(params):
    rows, width = params.shape
    ranks, rank = lax.axis_size("dp"), lax.axis_index("dp")
    before = lax.ppermute(params[-16:], "dp", [(source, source + 1) for source in range(ranks - 1)])
    longer = jnp.concatenate([before, params], axis=0)
    in_place = lax.broadcasted_iota(jnp.int32, (rows, 1), 0) + rank * rows < layout_rows()[1]
    if not on_grid():
        moved = jnp.where(in_place, params, longer[16 - SPARE :][:rows])
        return lax.all_gather(moved.astype(jnp.bfloat16), "dp", axis=0, tiled=True)
    y, c, _, _ = place()
    half, half_cols = rows // 2, width // 2
    part = lax.dynamic_slice(params, (y * half, c * half_cols), (half, half_cols))
    moved = lax.dynamic_slice(longer, (y * half + 16 - SPARE, c * half_cols), (half, half_cols))
    in_place = lax.dynamic_slice(in_place, (y * half, 0), (half, 1))
    return gather_rows(jnp.where(in_place, part, moved).astype(jnp.bfloat16), rows)


def low_rank_rows(factors, extra, first_row, count):
    last_layer = FIRST_LAYER + 4 * D + 2 * FF
    devices = factors.shape[0]

    def half(at, width, which):
        piece = factors[:, 8 * which : 8 * which + 8, at : at + width]
        return piece.reshape(devices * 8, width)

    norms = extra[:16].astype(jnp.bfloat16)
    sections = [
        (last_layer, half(FF, D, 0), half(FF + D, D, 0)),
        (last_layer + 3 * D, half(FF, D, 1), half(FF + D, D, 1)),
        (last_layer + 4 * D, half(0, FF, 0), half(FF + 2 * D, D, 0)),
        (last_layer + 4 * D + FF, half(0, FF, 1), half(FF + 2 * D, D, 1)),
        (TAIL_START, jnp.eye(16, HEAD_AT, dtype=jnp.bfloat16), norms),
        (TAIL_START + HEAD_AT, half(FF + 3 * D, EMB, 0), half(FF + 3 * D, D, 1)),
    ]
    row = first_row + jnp.arange(count)
    lefts, rights = [], []
    for start, left, right in sections:
        width = left.shape[1]
        padded = jnp.pad(left, ((0, 0), (count, count)))
        at = jnp.clip(first_row - start + count, 0, width + count)
        window = lax.dynamic_slice(padded, (0, at), (left.shape[0], count))
        inside = (row >= start) & (row < start + width)
        lefts.append(jnp.where(inside[None], window, jnp.zeros_like(window)))
        rights.append(right)
    return lax.dot_general(
        jnp.concatenate(lefts, axis=0),
        jnp.concatenate(rights, axis=0),
        (((0,), (0,)), ((), ())),
        preferred_element_type=jnp.float32,
    )


def reduce_rows(grad_rows, factors, extra, count):
    ranks, rank = lax.axis_size("dp"), lax.axis_index("dp")
    last_layer = FIRST_LAYER + 4 * D + 2 * FF
    flat_row = rank * count + lax.broadcasted_iota(jnp.int32, (count, 1), 0)
    if on_grid():
        shard, factors, extra = sum_on_plane(grad_rows, factors, extra, count)
        extra = jnp.sum(extra, axis=0)
    else:
        rest = low_rank_rows(factors[None], extra, 0, ranks * count).astype(jnp.bfloat16)
        whole = jnp.where(dense_row(jnp.arange(DENSE_END))[:, None], grad_rows, rest[:DENSE_END])
        whole = jnp.concatenate([whole, rest[DENSE_END:]], axis=0)
        shard = lax.psum_scatter(whole, "dp", scatter_dimension=0, tiled=True)
        extra = lax.psum(extra, "dp")
    following = lax.ppermute(shard[:16], "dp", [(source, source - 1) for source in range(1, ranks)])
    shifted = jnp.concatenate([shard[SPARE:], following[:SPARE]], axis=0)
    summed = jnp.where(flat_row < layout_rows()[1], shard, shifted).astype(jnp.float32)
    if on_grid():
        rest = low_rank_rows(factors, extra, rank * count + SPARE, count)
        spared = jnp.where(flat_row < layout_rows()[1], flat_row, flat_row + SPARE)
        summed = jnp.where(dense_row(spared), summed, rest)
    return (summed, extra)


def dense_row(row):
    last_layer = FIRST_LAYER + 4 * D + 2 * FF
    return (row < last_layer) | ((row >= last_layer + D) & (row < DENSE_END))


def adam_update(params, moment_one, moment_two, clipped, step_number):
    moment_one = BETA_ONE * moment_one + (1.0 - BETA_ONE) * clipped
    moment_two = BETA_TWO * moment_two + (1.0 - BETA_TWO) * clipped * clipped
    corrected_one = moment_one / (1.0 - BETA_ONE**step_number)
    corrected_two = moment_two / (1.0 - BETA_TWO**step_number)
    params = params - RATE * (corrected_one / (jnp.sqrt(corrected_two) + ADAM_EPS) + DECAY * params)
    return (params, moment_one, moment_two)


def nesterov(master_rows, momentum_rows, mean_delta):
    momentum_next = OUTER_MOM * momentum_rows + mean_delta
    return (master_rows - OUTER_RATE * (mean_delta + OUTER_MOM * momentum_next), momentum_next)


def token_rows(pixel_block):
    images, patches, _ = pixel_block.shape
    padded = jnp.pad(pixel_block, ((0, 0), (0, TOKENS - patches), (0, 0)))
    return padded.reshape(images * TOKENS, PATCH_IN)


def per_device(
    pixels,
    counts,
    labels,
    text,
    master,
    outer_momentum,
    first_moment,
    second_moment,
    eval_pixels,
    eval_counts,
    eval_labels,
):
    params = master
    moment_one = first_moment[0]
    moment_two = second_moment[0]
    norm_list, loss_list, count_list, post_list = ([], [], [], [])
    slots = pixels.shape[2]
    live = (jnp.arange(slots)[None, :] < counts[0]).astype(jnp.float32).reshape(-1)
    step_labels = labels[0].reshape(-1)
    step_pixels = token_rows(pixels[0].reshape((-1,) + pixels.shape[3:]))
    if on_grid():
        step_pixels, live, step_labels = [
            to_planes(values) for values in (step_pixels, live, step_labels)
        ]
    weights = fetch_weights(params)
    grad_rows, factors, extra = run_tower(weights, step_pixels, step_labels, live, text, True)
    reduced, extra = reduce_rows(grad_rows, factors, extra, params.shape[0])
    loss_all, count_all, post_all = extra[12, 0], extra[12, 1], extra[10:12]
    square_all = lax.psum(jnp.sum(reduced * reduced), "dp")
    gradient = reduced / count_all
    grad_norm = jnp.sqrt(square_all) / count_all
    clip_factor = CLIP_MAX / jnp.maximum(grad_norm, CLIP_MAX)
    clipped = gradient * clip_factor
    params, moment_one, moment_two = adam_update(params, moment_one, moment_two, clipped, STEP)
    norm_list.append(grad_norm)
    loss_list.append(loss_all)
    count_list.append(count_all)
    post_list.append(post_all / count_all * clip_factor)
    delta = master - params
    groups = lax.axis_size("group")
    mean_delta = lax.psum(delta.astype(jnp.bfloat16), "group").astype(jnp.float32) / groups
    new_master, new_outer = nesterov(master, outer_momentum, mean_delta)
    soup_rows = fetch_weights(new_master)
    eval_live = (jnp.arange(eval_pixels.shape[0]) < eval_counts[0]).astype(jnp.float32)
    eval_tile = run_tower(soup_rows, token_rows(eval_pixels), eval_labels, eval_live, text, False)
    eval_losses = eval_tile[: eval_labels.shape[0], 0]
    return (
        new_master,
        new_outer,
        moment_one[None],
        moment_two[None],
        jnp.stack(norm_list)[None],
        jnp.stack(loss_list)[None],
        jnp.stack(count_list)[None],
        jnp.stack(post_list)[None],
        eval_losses,
    )


def solution(mesh):
    return jax.shard_map(
        per_device,
        mesh=mesh,
        in_specs=(
            P(None, None, ("group", "dp"), None, None),
            P(None, None, ("group", "dp")),
            P(None, None, ("group", "dp")),
            P(),
            P("dp", None),
            P("dp", None),
            P("group", "dp", None),
            P("group", "dp", None),
            P(("group", "dp"), None, None),
            P(("group", "dp")),
            P(("group", "dp")),
        ),
        out_specs=(
            P("dp", None),
            P("dp", None),
            P("group", "dp", None),
            P("group", "dp", None),
            P("group", None),
            P("group", None),
            P("group", None),
            P("group", None, None, None),
            P(("group", "dp")),
        ),
        check_vma=False,
    )
```

```python
import functools

import jax
import jax.numpy as jnp
from jax import lax
from jax.experimental import pallas as pl
from jax.experimental.pallas import tpu as pltpu
from jax.sharding import PartitionSpec as P

MESH = pl.DeviceIdType.MESH

D = 768
HEADS = 12
HEAD = 64
FF = 3072
PATCH_IN = 3072
EMB = 512
CLASSES = 1000
LAYERS = 2
MICRO = 2
STEP = 10
SEQ = 50
ROWS_RAW = 22079


LN_EPS = 1e-05
NORM_EPS = 1e-06
LOGIT_SCALE = 50.0
SMOOTH = 0.1
CLIP_MAX = 0.02
BETA_ONE = 0.9
BETA_TWO = 0.98
ADAM_EPS = 1e-08
RATE = 0.02
DECAY = 0.1
OUTER_RATE = 0.7
OUTER_MOM = 0.9
GELU_SLOPE = 1.702
SPARE = 13
FIRST_SHARE = 0.6
LOOK_AHEAD = 3
PARCEL_STEP = 1
REDUCE_HEAD = [4, 6]
REDUCE_TAIL = [4]


def layout_rows():
    table_start = PATCH_IN
    layer_start = table_start + SEQ + 1
    block_size = 4 * D + 2 * FF
    norm_start = layer_start + LAYERS * block_size
    head_start = norm_start + 4 * LAYERS + 4
    return (table_start, layer_start, block_size, norm_start, head_start)


TOKENS = 56
CLASS_AT = 49
PAIR = 2 * TOKENS
BLOCK = 3072
TAIL_START = BLOCK + SEQ + 1 + SPARE + LAYERS * (4 * D + 2 * FF)
TAIL_ROWS = 544
HEAD_AT = 4 * LAYERS + 4
TABLE_ROWS = SEQ + 1 + SPARE
LOW_COLS = 2 * FF
FIRST_LAYER = BLOCK + TABLE_ROWS
DENSE_END = FIRST_LAYER + 4 * D + 2 * FF + 3 * D


def dot(first, second, first_dim=1, second_dim=0):
    return lax.dot_general(
        first,
        second,
        (((first_dim,), (second_dim,)), ((), ())),
        preferred_element_type=jnp.float32,
    )


def low(values):
    return values.astype(jnp.bfloat16)


def norm_parts(values):
    centred = values - jnp.mean(values, -1, keepdims=True)
    scale = lax.rsqrt(jnp.mean(centred * centred, -1, keepdims=True) + LN_EPS)
    return (centred * scale, scale)


def norm_back(values, gain, grad):
    unit, scale = norm_parts(values)
    weighted = grad * gain
    mean_one = jnp.mean(weighted, -1, keepdims=True)
    mean_two = jnp.mean(weighted * unit, -1, keepdims=True)
    return (scale * (weighted - mean_one - unit * mean_two), grad * unit)


def wide(values, rows):
    return jnp.concatenate(
        [values, jnp.zeros((rows - values.shape[0], values.shape[1]), values.dtype)], axis=0
    )


def head_mask(rows, lanes, first_head):
    row = lax.broadcasted_iota(jnp.int32, (rows, lanes), 0)
    lane = lax.broadcasted_iota(jnp.int32, (rows, lanes), 1)
    return (lane // HEAD + first_head) == row


def lane_pick(values, head):
    lane = lax.broadcasted_iota(jnp.int32, values.shape, 1)
    return jnp.where(lane // HEAD == head, values, jnp.zeros_like(values))


def stack_heads(values):
    return jnp.concatenate([lane_pick(values, head) for head in range(4)], axis=0)


def fold_heads(values):
    rows = values.shape[0] // 4
    total = lane_pick(values[:rows], 0)
    for head in range(1, 4):
        total = total + lane_pick(values[head * rows : (head + 1) * rows], head)
    return total


def soft(scores):
    scores = scores - jnp.max(scores, -1, keepdims=True)
    grown = jnp.exp(scores)
    return grown / jnp.sum(grown, -1, keepdims=True)


def pair_bias():
    row = lax.broadcasted_iota(jnp.int32, (PAIR, PAIR), 0)
    col = lax.broadcasted_iota(jnp.int32, (PAIR, PAIR), 1)
    fits = (row // TOKENS == col // TOKENS) & (col % TOKENS < SEQ)
    return jnp.where(fits, 0.0, -1e30)


def class_bias():
    row = lax.broadcasted_iota(jnp.int32, (32, PAIR), 0)
    col = lax.broadcasted_iota(jnp.int32, (32, PAIR), 1)
    fits = (row // 16 == col // TOKENS) & (col % TOKENS < SEQ)
    return jnp.where(fits, 0.0, -1e30)


def spread_heads(values):
    keep = head_mask(16, D, 0)
    rows = jnp.broadcast_to(values[:, None, :], (8, 16, D))
    return jnp.where(keep[None], rows, 0.0).reshape(128, D)


def unspread_heads(values):
    keep = head_mask(16, D, 0)
    return jnp.sum(jnp.where(keep[None], values.reshape(8, 16, D), 0.0), axis=1)


def tower_kernel(images, with_grads, carry, *refs):
    rows_all = images * TOKENS
    pairs = images // 2
    (w_hbm, pix_hbm, text_ref, note_ref), refs = refs[:4], refs[4:]
    if with_grads:
        (g_hbm, factor_ref, extra_ref), refs = refs[:3], refs[3:]
    else:
        carried, refs = refs[:carry], refs[carry:]
        (loss_ref,), refs = refs[:1], refs[1:]
        carried_out, refs = refs[:carry], refs[carry:]
    (wbuf, tail, table, pix, emb, hid0, mid0, hid1, acc, qkv, norm_a, norm_b, mixed, pre, act), refs = (
        refs[:15],
        refs[15:],
    )
    (norm_c, kv), refs = refs[:2], refs[2:]
    if with_grads:
        (dhid, dqkv, gb, dmix, stage, stage_sem), refs = refs[:6], refs[6:]
    elif carry:
        (hold, hold_sems), refs = refs[:2], refs[2:]
    (wsem, small_sem) = refs

    layer_at = [FIRST_LAYER + index * (4 * D + 2 * FF) for index in range(LAYERS)]
    order = [0]
    for start in layer_at:
        order += [start, start + 4 * D, start + 4 * D + FF]
    if with_grads:
        order += [layer_at[0] + 4 * D + FF, layer_at[0] + 4 * D, layer_at[0]]
    slot_of = [0, 1, 2, 0, 1, 2, 0, 0, 2, 1]

    def fetch(index):
        return pltpu.make_async_copy(
            w_hbm.at[pl.ds(order[index], BLOCK)], wbuf.at[slot_of[index]], wsem.at[slot_of[index]]
        )

    hops = []
    if carry:
        piece = hold.shape[1]
        for source, target in zip(carried, carried_out):
            for start in range(0, source.shape[0], piece):
                hops.append((source.at[pl.ds(start, piece)], target.at[pl.ds(start, piece)]))

    def hop_in(index):
        slot = index % 4
        return pltpu.make_async_copy(hops[index][0], hold.at[slot], hold_sems.at[0, slot])

    def hop_out(index):
        slot = index % 4
        return pltpu.make_async_copy(hold.at[slot], hops[index][1], hold_sems.at[1, slot])

    hopped = [0]

    def hop():
        index = hopped[0]
        if index < len(hops):
            hop_in(index).wait()
            hop_out(index).start()
            if index >= 2:
                hop_out(index - 2).wait()
            if 2 <= index and index + 2 < len(hops):
                hop_in(index + 2).start()
        hopped[0] = index + 1

    for index in range(min(4, len(hops))):
        hop_in(index).start()

    load_pix = pltpu.make_async_copy(pix_hbm, pix, small_sem.at[0])
    load_tail = pltpu.make_async_copy(
        w_hbm.at[pl.ds(TAIL_START, TAIL_ROWS)], tail, small_sem.at[1]
    )
    load_table = pltpu.make_async_copy(w_hbm.at[pl.ds(BLOCK, TABLE_ROWS)], table, small_sem.at[2])
    fetch(0).start()
    load_pix.start()
    load_table.start()
    load_tail.start()
    fetch(1).start()
    fetch(2).start()

    def chunks_of(count=rows_all // PAIR):
        return pl.loop(0, count)

    def rows_at(index):
        return pl.ds(pl.multiple_of(index * PAIR, PAIR), PAIR)

    def norm_row(index):
        return tail[0:16, :].astype(jnp.float32)[index : index + 1]

    def class_rows(ref):
        picked = [ref[TOKENS * i + CLASS_AT : TOKENS * i + CLASS_AT + 1, :] for i in range(images)]
        if images < 8:
            picked.append(jnp.zeros((8 - images, ref.shape[1]), ref.dtype))
        return jnp.concatenate(picked, axis=0)

    def add_class_rows(ref, values):
        for i in range(images):
            at = slice(TOKENS * i + CLASS_AT, TOKENS * i + CLASS_AT + 1)
            ref[at, :] = ref[at, :] + values[i : i + 1]

    def layer_norm_into(source, target, gain_row):
        gain, bias = norm_row(gain_row), norm_row(gain_row + 1)

        @chunks_of()
        def _(index):
            rows = rows_at(index)
            unit, _ = norm_parts(source[rows, :])
            target[rows, :] = (unit * gain + bias).astype(target.dtype)

    load_table.wait()
    load_tail.wait()
    load_pix.wait()
    fetch(0).wait()
    emb[...] = dot(pix[...], wbuf[0])
    hop()
    fetch(3).start()
    rows_table = table[...].astype(jnp.float32)
    added = pltpu.roll(rows_table, TABLE_ROWS - 2, 0)[:TOKENS]
    token = lax.broadcasted_iota(jnp.int32, (TOKENS, D), 0)
    added = jnp.where(token == CLASS_AT, rows_table[0:1] + rows_table[1:2], added)
    added = jnp.where(token < SEQ, added, 0.0)

    gain, bias = norm_row(0), norm_row(1)

    @chunks_of()
    def _(index):
        rows = rows_at(index)
        values = emb[rows, :] + jnp.concatenate([added, added], axis=0)
        emb[rows, :] = values
        unit, _ = norm_parts(values)
        hid0[rows, :] = unit * gain + bias

    layer_norm_into(hid0, norm_a, 2)
    hop()
    fetch(1).wait()

    @pl.loop(0, 3)
    def _(part):
        at = pl.ds(pl.multiple_of(part * D, D), D)
        qkv[:, at] = low(dot(norm_a[...], wbuf[1, at, :]))

    bias_pair = pair_bias()
    hop()

    def lanes(part, group):
        return slice(part * D + group * 256, part * D + (group + 1) * 256)

    def pair_soft(queries, keys):
        scores = dot(queries, keys, 1, 1) * HEAD ** (-0.5)
        scores = scores.reshape(4, PAIR, PAIR) + bias_pair[None]
        return soft(scores).reshape(4 * PAIR, PAIR)

    @pl.loop(0, pairs)
    def _(index):
        rows = rows_at(index)
        for group in range(3):
            queries = stack_heads(qkv[rows, lanes(0, group)])
            probs = low(pair_soft(queries, qkv[rows, lanes(1, group)]))
            out = dot(probs, qkv[rows, lanes(2, group)])
            mixed[rows, lanes(0, group)] = low(fold_heads(out))

    acc[...] = dot(mixed[...], wbuf[1, 3 * D : 4 * D, :])
    hop()
    fetch(4).start()
    gain2, bias2 = norm_row(4), norm_row(5)
    hop()

    @chunks_of()
    def _(index):
        rows = rows_at(index)
        values = hid0[rows, :] + acc[rows, :]
        mid0[rows, :] = values
        unit, _ = norm_parts(values)
        norm_b[rows, :] = low(unit * gain2 + bias2)

    fetch(2).wait()

    @pl.loop(0, 3)
    def _(part):
        at = pl.ds(pl.multiple_of(part * 1024, 1024), 1024)
        values = dot(norm_b[...], wbuf[2, at, :], 1, 1)
        if with_grads:
            pre[:, at] = low(values)
        act[:, at] = low(values * jax.nn.sigmoid(GELU_SLOPE * values))

    fetch(5).start()
    fetch(3).wait()
    hop()
    acc[...] = dot(act[...], wbuf[0])
    fetch(6).start()
    gain3, bias3 = norm_row(6), norm_row(7)
    hop()

    @chunks_of()
    def _(index):
        rows = rows_at(index)
        values = mid0[rows, :] + acc[rows, :]
        hid1[rows, :] = values
        unit, _ = norm_parts(values)
        norm_c[rows, :] = low(unit * gain3 + bias3)

    fetch(4).wait()

    @pl.loop(0, 2)
    def _(part):
        kv[:, pl.ds(pl.multiple_of(part * D, D), D)] = low(
            dot(norm_c[...], wbuf[1, pl.ds(pl.multiple_of(part * D + D, D), D), :])
        )

    class_hid = class_rows(hid1)
    hop()
    unit_one, _ = norm_parts(class_hid)
    class_a = low(wide(unit_one * gain3 + bias3, 16))
    class_q = low(dot(class_a, wbuf[1, 0:D, :]))
    spread_q = low(spread_heads(class_q[:8].astype(jnp.float32)))
    bias_class = class_bias()
    class_probs, outs = [], []
    for pair in range(pairs):
        rows = slice(pair * PAIR, (pair + 1) * PAIR)
        scores = dot(spread_q[32 * pair : 32 * pair + 32], kv[rows, 0:D], 1, 1)
        probs = soft(scores * HEAD ** (-0.5) + bias_class)
        class_probs.append(probs)
        outs.append(dot(low(probs), kv[rows, D : 2 * D]))
    for _ in range(4 - pairs):
        outs.append(jnp.zeros((32, D), jnp.float32))
    class_mix = low(wide(unspread_heads(jnp.concatenate(outs, axis=0)), 16))
    class_mid = class_hid + dot(class_mix, wbuf[1, 3 * D : 4 * D, :])[:8]
    hop()
    unit_two, _ = norm_parts(class_mid)
    gain4, bias4 = norm_row(8), norm_row(9)
    class_b = low(wide(unit_two * gain4 + bias4, 16))
    fetch(5).wait()
    class_pre = dot(class_b, wbuf[2], 1, 1)
    hop()
    gate = jax.nn.sigmoid(GELU_SLOPE * class_pre)
    class_act = low(class_pre * gate)
    fetch(6).wait()
    class_out = class_mid + dot(class_act, wbuf[0])[:8]
    hop()
    gain5, bias5 = norm_row(10), norm_row(11)
    unit_post, _ = norm_parts(class_out)
    pooled = low(wide(unit_post * gain5 + bias5, 16))

    hop()
    pooled_out = dot(pooled, tail[...], 1, 1)
    pooled_out = jnp.concatenate([pooled_out, jnp.zeros((16, 640 - TAIL_ROWS), jnp.float32)], axis=1)
    embedded = pltpu.roll(pooled_out, 640 - HEAD_AT, 1)[:8, :EMB]
    length = lax.rsqrt(jnp.sum(embedded * embedded, -1, keepdims=True) + NORM_EPS)
    unit_rows = embedded * length
    logits = LOGIT_SCALE * dot(low(wide(unit_rows, 16)), text_ref[...], 1, 1)[:8]
    top = jnp.max(logits, -1, keepdims=True)
    log_total = top + jnp.log(jnp.sum(jnp.exp(logits - top), -1, keepdims=True))
    log_probs = logits - log_total
    classes = lax.broadcasted_iota(jnp.int32, logits.shape, 1)
    label = note_ref[:, 0:1].astype(jnp.int32)
    target = jnp.where(classes == label, 1.0 - SMOOTH, 0.0) + SMOOTH / CLASSES
    live = note_ref[:, 1:2]
    losses = -live * jnp.sum(target * log_probs, -1, keepdims=True)
    if not with_grads:
        loss_ref[...] = jnp.broadcast_to(losses, loss_ref.shape)
        while hopped[0] < len(hops):
            hop()
        for index in range(max(0, len(hops) - 2), len(hops)):
            hop_out(index).wait()
        return

    grad_raw = low(wide(LOGIT_SCALE * ((jnp.exp(log_probs) - target) * live), 16))
    grad_unit = dot(grad_raw, text_ref[...])[:8]
    along = jnp.sum(grad_unit * embedded, -1, keepdims=True)
    grad_embed = grad_unit * length - embedded * (length * length * length * along)
    grad_embed = low(wide(grad_embed, 16))
    grad_tail = jnp.concatenate(
        [grad_embed.astype(jnp.float32), jnp.zeros((16, 640 - EMB), jnp.float32)], axis=1
    )
    grad_tail = low(pltpu.roll(grad_tail, HEAD_AT, 1)[:, :TAIL_ROWS])
    grad_pooled = dot(grad_tail, tail[...])[:8]

    def put_extra(row, values):
        extra_ref[row : row + 1, :] = values

    extra_ref[...] = jnp.zeros_like(extra_ref)
    lane = lax.broadcasted_iota(jnp.int32, (1, D), 1)
    put_extra(12, jnp.where(lane == 0, jnp.sum(losses), jnp.where(lane == 1, jnp.sum(live), 0.0)))

    def class_norm_back(values, gain_row, grad):
        result, terms = norm_back(values, norm_row(gain_row), grad)
        put_extra(gain_row, jnp.sum(terms, 0, keepdims=True))
        put_extra(gain_row + 1, jnp.sum(grad, 0, keepdims=True))
        return result

    grad_out = class_norm_back(class_out, 10, grad_pooled)

    grad_b = low(wide(grad_out, 16))
    grad_act = dot(grad_b, wbuf[0], 1, 1)
    grad_pre = low(grad_act * (gate + GELU_SLOPE * class_pre * gate * (1.0 - gate)))
    fetch(7).start()
    grad_mid = grad_out + class_norm_back(class_mid, 8, dot(grad_pre, wbuf[2])[:8])
    fetch(8).start()
    grad_proj = low(wide(grad_mid, 16))
    grad_mix = low(dot(grad_proj, wbuf[1, 3 * D : 4 * D, :], 1, 1))
    spread_g = low(spread_heads(grad_mix[:8].astype(jnp.float32)))
    grad_qs = []
    for pair in range(pairs):
        rows = slice(pair * PAIR, (pair + 1) * PAIR)
        some_g, some_q = spread_g[32 * pair : 32 * pair + 32], spread_q[32 * pair : 32 * pair + 32]
        probs = class_probs[pair]
        grad_probs = dot(some_g, kv[rows, D : 2 * D], 1, 1)
        dqkv[rows, 2 * D : 3 * D] = low(dot(low(probs), some_g, 0, 0))
        grad_scores = probs * (grad_probs - jnp.sum(grad_probs * probs, -1, keepdims=True))
        grad_scores = low(grad_scores)
        grad_qs.append(dot(grad_scores, kv[rows, 0:D]))
        dqkv[rows, D : 2 * D] = low(dot(grad_scores, some_q, 0, 0) * HEAD ** (-0.5))
    grad_q = low(wide(unspread_heads(jnp.concatenate(grad_qs, axis=0)) * HEAD ** (-0.5), 16))

    def pack(first, second, at, width):
        factor_ref[:, at : at + width] = low(
            jnp.concatenate([first[:8].astype(jnp.float32), second[:8].astype(jnp.float32)], axis=0)
        )

    pack(grad_pre, class_act, 0, FF)
    pack(class_a, class_mix, FF, D)
    pack(grad_q, grad_proj, FF + D, D)
    pack(class_b, grad_b, FF + 2 * D, D)
    embed_wide = jnp.concatenate(
        [grad_embed.astype(jnp.float32), jnp.zeros((16, D - EMB), jnp.float32)], axis=1
    )
    pack(embed_wide, pooled, FF + 3 * D, D)

    started = [0]

    def push(slot, at):
        return pltpu.make_async_copy(stage.at[slot], g_hbm.at[pl.ds(at, D)], stage_sem.at[slot])

    def weight_grad(left, left_at, right, right_at, at, count):
        base = started[0]

        def one(block):
            slot = lax.rem(base + block, 2)

            @pl.when(base + block >= 2)
            def _():
                push(slot, at).wait()

            from_lane = pl.multiple_of(left_at + block * D, D) if count > 1 else left_at
            stage[slot] = low(dot(left[:, pl.ds(from_lane, D)], right[:, right_at : right_at + D], 0, 0))
            push(slot, pl.multiple_of(at + block * D, 16)).start()

        if count > 1:
            pl.loop(0, count)(one)
        else:
            one(0)
        started[0] = base + count

    def norm_back_rows(values, gain_row, grad, finish):
        gain = norm_row(gain_row)
        extra_ref[gain_row : gain_row + 2, :] = jnp.zeros((2, D), jnp.float32)

        @chunks_of()
        def _(index):
            rows = rows_at(index)
            grad_rows = grad[rows, :]
            result, terms = norm_back(values[rows, :], gain, grad_rows)
            at = slice(gain_row, gain_row + 1)
            extra_ref[at, :] = extra_ref[at, :] + jnp.sum(terms, 0, keepdims=True)
            at = slice(gain_row + 1, gain_row + 2)
            extra_ref[at, :] = extra_ref[at, :] + jnp.sum(grad_rows, 0, keepdims=True)
            finish(rows, result)

    weight_grad(norm_c, 0, dqkv, D, layer_at[1] + D, 1)
    weight_grad(norm_c, 0, dqkv, 2 * D, layer_at[1] + 2 * D, 1)
    acc[...] = dot(dqkv[:, D : 2 * D], wbuf[1, D : 2 * D, :], 1, 1)
    acc[...] = acc[...] + dot(dqkv[:, 2 * D : 3 * D], wbuf[1, 2 * D : 3 * D, :], 1, 1)
    add_class_rows(acc, dot(grad_q, wbuf[1, 0:D, :], 1, 1))
    fetch(9).start()

    def finish_second(rows, result):
        dhid[rows, :] = result

    norm_back_rows(hid1, 6, acc, finish_second)
    add_class_rows(dhid, grad_mid)

    gb[...] = low(dhid[...])
    fetch(7).wait()
    weight_grad(act, 0, gb, 0, layer_at[0] + 4 * D + FF, FF // D)

    @pl.loop(0, 3)
    def _(part):
        at = pl.ds(pl.multiple_of(part * 1024, 1024), 1024)
        grad_rows = dot(gb[...], wbuf[0, at, :], 1, 1)
        values = pre[:, at].astype(jnp.float32)
        gates = jax.nn.sigmoid(GELU_SLOPE * values)
        pre[:, at] = low(grad_rows * (gates + GELU_SLOPE * values * gates * (1.0 - gates)))

    weight_grad(pre, 0, norm_b, 0, layer_at[0] + 4 * D, FF // D)
    fetch(8).wait()
    acc[...] = dot(pre[...], wbuf[2])

    def finish_mid(rows, result):
        total = dhid[rows, :] + result
        dhid[rows, :] = total
        gb[rows, :] = low(total)

    norm_back_rows(mid0, 4, acc, finish_mid)
    weight_grad(mixed, 0, gb, 0, layer_at[0] + 3 * D, 1)
    fetch(9).wait()
    dmix[...] = low(dot(gb[...], wbuf[1, 3 * D : 4 * D, :], 1, 1))

    @pl.loop(0, pairs)
    def _(index):
        rows = rows_at(index)
        for group in range(3):
            queries = stack_heads(qkv[rows, lanes(0, group)])
            keys = qkv[rows, lanes(1, group)]
            probs = pair_soft(queries, keys)
            some_g = stack_heads(dmix[rows, lanes(0, group)])
            grad_probs = dot(some_g, qkv[rows, lanes(2, group)], 1, 1)
            dqkv[rows, lanes(2, group)] = low(dot(low(probs), some_g, 0, 0))
            grad_scores = probs * (grad_probs - jnp.sum(grad_probs * probs, -1, keepdims=True))
            grad_scores = low(grad_scores)
            grad_queries = fold_heads(dot(grad_scores, keys))
            dqkv[rows, lanes(0, group)] = low(grad_queries * HEAD ** (-0.5))
            grad_keys = dot(grad_scores, queries, 0, 0)
            dqkv[rows, lanes(1, group)] = low(grad_keys * HEAD ** (-0.5))

    for part in range(3):
        weight_grad(norm_a, 0, dqkv, part * D, layer_at[0] + part * D, 1)
    acc[...] = dot(dqkv[:, 0:D], wbuf[1, 0:D, :], 1, 1)
    for part in (1, 2):
        at = slice(part * D, (part + 1) * D)
        acc[...] = acc[...] + dot(dqkv[:, at], wbuf[1, at, :], 1, 1)

    def finish_first(rows, result):
        dhid[rows, :] = dhid[rows, :] + result

    norm_back_rows(hid0, 2, acc, finish_first)

    def finish_embedding(rows, result):
        dhid[rows, :] = result
        gb[rows, :] = low(result)

    norm_back_rows(emb, 0, dhid, finish_embedding)
    weight_grad(pix, 0, gb, 0, 0, PATCH_IN // D)
    grad_tokens = dhid[0:TOKENS, :]
    for i in range(1, images):
        grad_tokens = grad_tokens + dhid[TOKENS * i : TOKENS * (i + 1), :]
    class_grad = grad_tokens[CLASS_AT : CLASS_AT + 1]
    grad_tokens = jnp.concatenate(
        [grad_tokens, jnp.zeros((TABLE_ROWS - TOKENS, D), jnp.float32)], axis=0
    )
    grad_table = pltpu.roll(grad_tokens, 2, 0)
    row = lax.broadcasted_iota(jnp.int32, (TABLE_ROWS, D), 0)
    grad_table = jnp.where(row < 2, class_grad, jnp.where(row < SEQ + 1, grad_table, 0.0))
    table[...] = low(grad_table)
    put_table = pltpu.make_async_copy(table, g_hbm.at[pl.ds(BLOCK, TABLE_ROWS)], small_sem.at[0])
    put_table.start()
    put_table.wait()
    for slot in range(2):
        push(slot, 0).wait()


def image_notes(label_row, live_mask):
    notes = jnp.stack([label_row.astype(jnp.float32), live_mask], axis=1)
    return jnp.pad(notes, ((0, 8 - notes.shape[0]), (0, 126)))


def run_tower(weights, pixel_rows, notes, text, with_grads, carried=()):
    rows_all = pixel_rows.shape[0]
    images = rows_all // TOKENS
    bf16, f32 = jnp.bfloat16, jnp.float32
    scratch = [
        pltpu.VMEM((3, BLOCK, D), bf16),
        pltpu.VMEM((TAIL_ROWS, D), bf16),
        pltpu.VMEM((TABLE_ROWS, D), bf16),
        pltpu.VMEM((rows_all, PATCH_IN), bf16),
        pltpu.VMEM((rows_all, D), f32),
        pltpu.VMEM((rows_all, D), f32),
        pltpu.VMEM((rows_all, D), f32),
        pltpu.VMEM((rows_all, D), f32),
        pltpu.VMEM((rows_all, D), f32),
        pltpu.VMEM((rows_all, 3 * D), bf16),
        pltpu.VMEM((rows_all, D), bf16),
        pltpu.VMEM((rows_all, D), bf16),
        pltpu.VMEM((rows_all, D), bf16),
        pltpu.VMEM((rows_all if with_grads else 16, FF), bf16),
        pltpu.VMEM((rows_all, FF), bf16),
        pltpu.VMEM((rows_all, D), bf16),
        pltpu.VMEM((rows_all, 2 * D), bf16),
    ]
    if with_grads:
        scratch += [
            pltpu.VMEM((rows_all, D), f32),
            pltpu.VMEM((rows_all, 3 * D), bf16),
            pltpu.VMEM((rows_all, D), bf16),
            pltpu.VMEM((rows_all, D), bf16),
            pltpu.VMEM((2, D, D), bf16),
            pltpu.SemaphoreType.DMA((2,)),
        ]
        out_shape = (
            jax.ShapeDtypeStruct((grad_rows_kept(weights.shape[0]), D), bf16),
            jax.ShapeDtypeStruct((16, LOW_COLS), bf16),
            jax.ShapeDtypeStruct((16, D), f32),
        )
        out_specs = (
            pl.BlockSpec(memory_space=pl.ANY),
            pl.BlockSpec(memory_space=pltpu.VMEM),
            pl.BlockSpec(memory_space=pltpu.VMEM),
        )
    else:
        out_shape = (jax.ShapeDtypeStruct((8, 128), f32),)
        out_shape += tuple(jax.ShapeDtypeStruct(array.shape, array.dtype) for array in carried)
        out_specs = (pl.BlockSpec(memory_space=pltpu.VMEM),)
        out_specs += (pl.BlockSpec(memory_space=pl.ANY),) * len(carried)
        if carried:
            scratch += [
                pltpu.VMEM((4, carried[0].shape[0] // 6, carried[0].shape[1]), carried[0].dtype),
                pltpu.SemaphoreType.DMA((2, 4)),
            ]
    scratch += [pltpu.SemaphoreType.DMA((3,)), pltpu.SemaphoreType.DMA((3,))]
    vmem = pl.BlockSpec(memory_space=pltpu.VMEM)
    hbm = pl.BlockSpec(memory_space=pl.ANY)
    return pl.pallas_call(
        functools.partial(tower_kernel, images, with_grads, len(carried)),
        out_shape=out_shape,
        in_specs=[hbm, hbm, vmem, vmem] + [hbm] * len(carried),
        out_specs=out_specs,
        scratch_shapes=scratch,
        compiler_params=pltpu.CompilerParams(vmem_limit_bytes=60 * 2**20),
        cost_estimate=pl.CostEstimate(
            flops=(6 if with_grads else 2) * rows_all * weights.shape[0] * D,
            bytes_accessed=2 * weights.shape[0] * D,
            transcendentals=rows_all * 2 * FF,
        ),
        name="train" if with_grads else "evaluate",
    )(weights, pixel_rows, text, notes, *carried)


def grad_rows_kept(rows):
    if not on_grid():
        return DENSE_END
    plane_rows = rows // 4
    return (DENSE_END + plane_rows - 1) // plane_rows * plane_rows


def on_grid():
    return lax.axis_size("group") == 4 and lax.axis_size("dp") == 8


def place():
    worker = lax.axis_index("group")
    rank = lax.axis_index("dp")
    return (worker // 2, worker % 2, rank // 2, rank % 2)


def device_at(y, c, z, x):
    return (y * 2 + c, z * 2 + x)


def chunk_rows(total, share):
    units = total // 16
    sizes = [3, 4] + [6] * ((units - 15) // 6) + [4, 4 + (units - 15) % 6]
    chunks = []
    start = taken = 0
    for size in sizes:
        first = int(round((start + size) * share)) - taken
        taken += first
        chunks.append((start * 16, first * 16, (size - first) * 16))
        start += size
    return chunks


def image_device():
    y, c, z, x = place()
    return device_at((z + c) % 2, z // 2, 2 * c + y, x)


def image_source():
    y, c, z, x = place()
    return device_at(z % 2, z // 2, 2 * c + (y + z // 2) % 2, x)


def gather_kernel(chunks, images, *refs):
    if images:
        (part_ref, pixel_ref, note_ref, full_ref, moved_ref, moved_note_ref), refs = refs[:6], refs[6:]
        (local_sem, sends, recvs, pixel_sems) = refs
        count = pixel_ref.shape[0] // TOKENS
        parcels = [(note_ref, moved_note_ref)]
        for index in range(count):
            rows = pl.ds(index * TOKENS, TOKENS)
            parcels.append((pixel_ref.at[rows], moved_ref.at[rows]))
    else:
        (part_ref, full_ref, local_sem, sends, recvs) = refs
    half_cols = part_ref.shape[1]
    y, c, z, x = place()
    cols = pl.ds(pl.multiple_of(c * half_cols, half_cols), half_cols)
    over_x = device_at(y, c, z, 1 - x)
    over_y = device_at(1 - y, c, z, x)
    sibling = device_at(y, 1 - c, z, x)
    along_z = [device_at(y, c, (z + step) % 4, x) for step in (1, 2, 3)]
    target = image_device()
    stays = jnp.logical_and(target[0] == y * 2 + c, target[1] == z * 2 + x)
    barrier = pltpu.get_barrier_semaphore()
    for other in [over_x, over_y, sibling] + along_z:
        pl.semaphore_signal(barrier, inc=1, device_id=other, device_id_type=MESH)
    if images:

        @pl.when(jnp.logical_not(stays))
        def _():
            pl.semaphore_signal(barrier, inc=1, device_id=image_source(), device_id_type=MESH)

    def keep(index):
        start, first, second = chunks[index]
        rows = pl.ds(start, first + second)
        return pltpu.make_async_copy(
            part_ref.at[rows], full_ref.at[z, x, y, rows, cols], local_sem.at[index]
        )

    for index in range(len(chunks)):
        keep(index).start()
    pl.semaphore_wait(barrier, 6 + (jnp.where(stays, 0, 1) if images else 0))

    def send(piece, other, stage, index):
        pltpu.make_async_remote_copy(
            src_ref=piece,
            dst_ref=piece,
            send_sem=sends.at[stage, index],
            recv_sem=recvs.at[stage, index],
            device_id=other,
            device_id_type=MESH,
        ).start()

    def move_parcel(which):
        source, place_at = parcels[which]

        @pl.when(stays)
        def _():
            pltpu.make_async_copy(source, place_at, pixel_sems.at[0, which]).start()

        @pl.when(jnp.logical_not(stays))
        def _():
            pltpu.make_async_remote_copy(
                src_ref=source,
                dst_ref=place_at,
                send_sem=pixel_sems.at[1, which],
                recv_sem=pixel_sems.at[0, which],
                device_id=target,
                device_id_type=MESH,
            ).start()

    def arrived(piece, stage, index):
        pltpu.make_async_copy(piece, piece, recvs.at[stage, index]).wait()

    def sent(piece, stage, index):
        pltpu.make_async_copy(piece, piece, sends.at[stage, index]).wait()

    def pieces(index):
        start, first, second = chunks[index]
        rows = pl.ds(start, first + second)
        rows_a = pl.ds(start, first)
        rows_b = pl.ds(start + first, second)
        return {
            0: full_ref.at[pl.ds(0, 3), 0, 0, rows, cols],
            1: full_ref.at[:, x, y, rows_a, cols],
            2: full_ref.at[:, x, y, rows_b, cols],
            3: full_ref.at[:, x, :, rows_a, cols],
            4: full_ref.at[:, :, y, rows_b, cols],
            5: full_ref.at[:, :, :, rows, cols],
        }

    total = len(chunks)

    def send_along_z(index):
        start, first, second = chunks[index]
        rows = pl.ds(start, first + second)
        for other in along_z:
            pltpu.make_async_remote_copy(
                src_ref=part_ref.at[rows],
                dst_ref=full_ref.at[z, x, y, rows, cols],
                send_sem=sends.at[0, index],
                recv_sem=recvs.at[0, index],
                device_id=other,
                device_id_type=MESH,
            ).start()

    ahead = LOOK_AHEAD if images else 1
    for step in range(total + 3):
        for index in range(ahead) if step == 0 else [step + ahead - 1]:
            if index < total:
                send_along_z(index)
        if images and step % PARCEL_STEP == 0 and step // PARCEL_STEP < len(parcels):
            move_parcel(step // PARCEL_STEP)
        index = step - 1
        if 0 <= index < total:
            block = pieces(index)
            arrived(block[0], 0, index)
            keep(index).wait()
            send(block[1], over_y, 1, index)
            send(block[2], over_x, 2, index)
        index = step - 2
        if 0 <= index < total:
            block = pieces(index)
            arrived(block[1], 1, index)
            send(block[3], over_x, 3, index)
            arrived(block[2], 2, index)
            send(block[4], over_y, 4, index)
        index = step - 3
        if 0 <= index < total:
            block = pieces(index)
            arrived(block[3], 3, index)
            arrived(block[4], 4, index)
            send(block[5], sibling, 5, index)
    for index in range(total):
        block = pieces(index)
        arrived(block[5], 5, index)
        for stage in range(6):
            sent(block[stage], stage, index)
    if images:
        for which, (_, place_at) in enumerate(parcels):
            pltpu.make_async_copy(place_at, place_at, pixel_sems.at[0, which]).wait()

        @pl.when(jnp.logical_not(stays))
        def _():
            for which, (_, place_at) in enumerate(parcels):
                pltpu.make_async_copy(place_at, place_at, pixel_sems.at[1, which]).wait()


def gather_rows(part, shard_rows, pixel_rows=None, notes=None):
    images = pixel_rows is not None
    chunks = chunk_rows(part.shape[0], FIRST_SHARE if images else 0.5)
    hbm = pl.BlockSpec(memory_space=pl.ANY)
    width = 2 * part.shape[1]
    full_shape = jax.ShapeDtypeStruct((4, 2, 2, part.shape[0], width), part.dtype)
    semaphores = [
        pltpu.SemaphoreType.DMA((len(chunks),)),
        pltpu.SemaphoreType.DMA((6, len(chunks))),
        pltpu.SemaphoreType.DMA((6, len(chunks))),
    ]
    kernel = functools.partial(gather_kernel, chunks, images)
    if not images:
        full = pl.pallas_call(
            kernel,
            out_shape=full_shape,
            in_specs=[hbm],
            out_specs=hbm,
            scratch_shapes=semaphores,
            compiler_params=pltpu.CompilerParams(collective_id=0, has_side_effects=True),
            name="gather",
        )(part)
        return full.reshape(8 * shard_rows, width)
    full, moved, moved_notes = pl.pallas_call(
        kernel,
        out_shape=(
            full_shape,
            jax.ShapeDtypeStruct(pixel_rows.shape, pixel_rows.dtype),
            jax.ShapeDtypeStruct(notes.shape, notes.dtype),
        ),
        in_specs=[hbm, hbm, hbm],
        out_specs=[hbm, hbm, hbm],
        scratch_shapes=semaphores
        + [pltpu.SemaphoreType.DMA((2, 1 + pixel_rows.shape[0] // TOKENS))],
        compiler_params=pltpu.CompilerParams(collective_id=2, has_side_effects=True),
        name="gather_first",
    )(part, pixel_rows, notes)
    return (full.reshape(8 * shard_rows, width), moved, moved_notes)


def reduce_kernel(
    chunks,
    low_from,
    grad_ref,
    factor_ref,
    extra_ref,
    own_ref,
    factors_ref,
    extras_ref,
    squares_ref,
    mine,
    first_sum,
    sum_a,
    sum_b,
    last_sum,
    squares,
    passed_factor,
    passed_extra,
    load_sems,
    sends,
    recvs,
    small_sends,
    small_recvs,
    pass_sends,
    pass_recvs,
):
    half_cols = mine.shape[-1]
    planes = grad_ref.shape[0]
    y, c, z, x = place()
    home_y, home_c = z % 2, z // 2
    at_home = jnp.logical_and(home_y == y, home_c == c)
    from_plane = 2 * c + y
    my_cols = pl.ds(pl.multiple_of(c * half_cols, half_cols), half_cols)
    other_cols = pl.ds(pl.multiple_of((1 - c) * half_cols, half_cols), half_cols)
    over_x = device_at(y, c, z, 1 - x)
    over_y = device_at(1 - y, c, z, x)
    sibling = device_at(y, 1 - c, z, x)
    barrier = pltpu.get_barrier_semaphore()
    for other in (over_x, over_y, sibling):
        pl.semaphore_signal(barrier, inc=1, device_id=other, device_id_type=MESH)
    for other in range(8):
        other_y, other_c, other_x = other // 4, other // 2 % 2, other % 2
        same = jnp.logical_and(y == other_y, jnp.logical_and(c == other_c, x == other_x))
        itself = jnp.logical_and(at_home, same)

        @pl.when(jnp.logical_not(itself))
        def _():
            pl.semaphore_signal(
                barrier,
                inc=1,
                device_id=device_at(other_y, other_c, from_plane, other_x),
                device_id_type=MESH,
            )

    def spans(index):
        start, first, second = chunks[index]
        start_a = sum(chunk[1] for chunk in chunks[:index])
        start_b = sum(chunk[2] for chunk in chunks[:index])
        return (
            pl.ds(start, first + second),
            pl.ds(start, first),
            pl.ds(start + first, second),
            pl.ds(start_a, first),
            pl.ds(start_b, second),
        )

    def send(source, target, other, stage, index):
        pltpu.make_async_remote_copy(
            src_ref=source,
            dst_ref=target,
            send_sem=sends.at[stage, index],
            recv_sem=recvs.at[stage, index],
            device_id=other,
            device_id_type=MESH,
        ).start()

    def arrived(piece, stage, index):
        pltpu.make_async_copy(piece, piece, recvs.at[stage, index]).wait()

    def sent(piece, stage, index):
        pltpu.make_async_copy(piece, piece, sends.at[stage, index]).wait()

    def load(index):
        rows = spans(index)[0]
        return pltpu.make_async_copy(
            grad_ref.at[:, :, :, rows, my_cols],
            mine.at[index % 2, :, :, :, pl.ds(0, rows.size)],
            load_sems.at[index % 2],
        )

    def send_core(index):
        rows = spans(index)[0]
        send(
            grad_ref.at[:, :, :, rows, other_cols],
            first_sum.at[:, :, :, rows],
            sibling,
            0,
            index,
        )

    def add(target, source):
        summed = target[...].astype(jnp.float32) + source[...].astype(jnp.float32)
        target[...] = summed.astype(target.dtype)

    total = len(chunks)
    load(0).start()
    pl.semaphore_wait(barrier, 3 + jnp.where(at_home, 7, 8))
    send_core(0)
    send_core(1)
    def slot_of(from_y):
        return (from_y * 2 + c) * 2 + x

    def to_owners(source, target, which, first_z, way):
        for other in range(2 * first_z, 8):
            other_z, other_x = other // 2, other % 2
            itself = jnp.logical_and(at_home, jnp.logical_and(z == other_z, x == other_x))

            @pl.when(jnp.logical_not(itself))
            def _():
                pltpu.make_async_remote_copy(
                    src_ref=source,
                    dst_ref=target,
                    send_sem=small_sends.at[way, which],
                    recv_sem=small_recvs.at[which],
                    device_id=device_at(home_y, home_c, other_z, other_x),
                    device_id_type=MESH,
                ).start()

            @pl.when(itself)
            def _():
                pltpu.make_async_copy(source, target, small_recvs.at[which]).start()

    def passing(which):
        source, target = ((extra_ref, passed_extra), (factor_ref, passed_factor))[which]
        return pltpu.make_async_remote_copy(
            src_ref=source,
            dst_ref=target,
            send_sem=pass_sends.at[which],
            recv_sem=pass_recvs.at[which],
            device_id=over_y,
            device_id_type=MESH,
        )

    gives = y != home_y

    @pl.when(gives)
    def _():
        for which in range(2):
            passing(which).start()

    @pl.when(jnp.logical_not(gives))
    def _():
        to_owners(extra_ref, extras_ref.at[slot_of(y)], 0, 0, 0)
        to_owners(factor_ref, factors_ref.at[slot_of(y)], 1, low_from, 0)

    def pass_on():
        @pl.when(jnp.logical_not(gives))
        def _():
            for which in range(2):
                passing(which).wait_recv()
            to_owners(passed_extra, extras_ref.at[slot_of(1 - y)], 0, 0, 1)
            to_owners(passed_factor, factors_ref.at[slot_of(1 - y)], 1, low_from, 1)

    squares[...] = jnp.zeros_like(squares)
    half_rows = grad_ref.shape[3]
    last_layer = FIRST_LAYER + 4 * D + 2 * FF

    def add_squares(block, rows):
        values = last_sum[block, rows].astype(jnp.float32)
        row = ((block * 2 + x) * 2 + y) * half_rows + rows.start
        row = row + lax.broadcasted_iota(jnp.int32, values.shape, 0)
        values = jnp.where(dense_row(row), values * values, 0.0)
        values = jnp.sum(values.reshape(rows.size // 8, 8, half_cols), axis=0)
        for part in range(half_cols // 128):
            squares[...] += values[:, part * 128 : (part + 1) * 128]

    for step in range(total + 4):
        index = step
        if index < total:
            if index + 1 < total:
                load(index + 1).start()
            if index + 2 < total:
                send_core(index + 2)
            rows, rows_a, rows_b, in_a, in_b = spans(index)
            load(index).wait()
            arrived(first_sum.at[:, :, :, rows], 0, index)

            @pl.loop(0, 4 * planes)
            def _(block):
                zz, rest = block // 4, block % 4
                add(
                    first_sum.at[zz, rest // 2, rest % 2, rows],
                    mine.at[index % 2, zz, rest // 2, rest % 2, pl.ds(0, rows.size)],
                )

            if index == 1:
                pass_on()
            send(first_sum.at[:, 1 - x, :, rows_a], sum_a.at[:, :, in_a], over_x, 1, index)
            send(first_sum.at[:, :, 1 - y, rows_b], sum_b.at[:, :, in_b], over_y, 2, index)
        index = step - 1
        if 0 <= index < total:
            rows, rows_a, rows_b, in_a, in_b = spans(index)
            arrived(sum_a.at[:, :, in_a], 1, index)

            @pl.loop(0, 2 * planes)
            def _(block):
                add(
                    sum_a.at[block // 2, block % 2, in_a],
                    first_sum.at[block // 2, x, block % 2, rows_a],
                )

            send(sum_a.at[:, 1 - y, in_a], last_sum.at[:, rows_a], over_y, 3, index)
            arrived(sum_b.at[:, :, in_b], 2, index)

            @pl.loop(0, 2 * planes)
            def _(block):
                add(
                    sum_b.at[block // 2, block % 2, in_b],
                    first_sum.at[block // 2, block % 2, y, rows_b],
                )

            send(sum_b.at[:, 1 - x, in_b], last_sum.at[:, rows_b], over_x, 4, index)
        index = step - 2
        if 0 <= index < total:
            rows, rows_a, rows_b, in_a, in_b = spans(index)
            arrived(last_sum.at[:, rows_a], 3, index)
            arrived(last_sum.at[:, rows_b], 4, index)

            @pl.loop(0, planes)
            def _(block):
                add(last_sum.at[block, rows_a], sum_a.at[block, y, in_a])
                add(last_sum.at[block, rows_b], sum_b.at[block, x, in_b])
                add_squares(block, rows)

            for to_z in range(planes):
                itself = jnp.logical_and(at_home, z == to_z)
                source = last_sum.at[to_z, rows]
                target = own_ref.at[pl.ds(pl.multiple_of(y * half_rows + rows.start, 16), rows.size), my_cols]

                @pl.when(jnp.logical_not(itself))
                def _():
                    send(source, target, device_at(home_y, home_c, to_z, x), 5, index)

                @pl.when(itself)
                def _():
                    pltpu.make_async_copy(source, target, recvs.at[5, index]).start()

    to_owners(squares, squares_ref.at[slot_of(y)], 2, 0, 0)
    for index in range(total):
        rows, rows_a, rows_b, in_a, in_b = spans(index)

        @pl.when(z < planes)
        def _():
            arrived(own_ref.at[pl.ds(0, 2 * rows.size)], 5, index)

        sent(first_sum.at[:, :, :, rows], 0, index)
        sent(sum_a.at[:, :, in_a], 1, index)
        sent(sum_b.at[:, :, in_b], 2, index)
        sent(last_sum.at[:, rows_a], 3, index)
        sent(last_sum.at[:, rows_b], 4, index)

        kept = jnp.logical_and(at_home, z < planes)

        @pl.when(kept)
        def _():
            sent(last_sum.at[pl.ds(0, planes - 1), rows], 5, index)

        @pl.when(jnp.logical_not(kept))
        def _():
            sent(last_sum.at[:, rows], 5, index)

    def all_of(ref, count, sem):
        piece = ref.at[pl.ds(0, count)]
        pltpu.make_async_copy(piece, piece, sem).wait()

    all_of(extras_ref, 8, small_recvs.at[0])
    all_of(squares_ref, 8, small_recvs.at[2])

    @pl.when(z >= low_from)
    def _():
        all_of(factors_ref, 8, small_recvs.at[1])

    def sent_to_owners(ref, count, kept, which, way):
        @pl.when(kept)
        def _():
            all_of(ref, count - 1, small_sends.at[way, which])

        @pl.when(jnp.logical_not(kept))
        def _():
            all_of(ref, count, small_sends.at[way, which])

    sent_to_owners(squares_ref, 8, at_home, 2, 0)

    @pl.when(gives)
    def _():
        for which in range(2):
            passing(which).wait_send()

    @pl.when(jnp.logical_not(gives))
    def _():
        low_kept = jnp.logical_and(at_home, z >= low_from)
        for way in range(2):
            sent_to_owners(extras_ref, 8, at_home, 0, way)
            sent_to_owners(factors_ref, 2 * (4 - low_from), low_kept, 1, way)


def reduce_chunks(total, share):
    units = total // 16
    middle = units - sum(REDUCE_HEAD + REDUCE_TAIL)
    sizes = [8] * (middle // 8)
    sizes[-1] += middle % 8
    sizes = REDUCE_HEAD + sizes + REDUCE_TAIL
    chunks = []
    start = taken = 0
    for size in sizes:
        first = int(round((start + size) * share)) - taken
        taken += first
        chunks.append((start * 16, first * 16, (size - first) * 16))
        start += size
    return chunks


def low_plane(shard_rows):
    return (FIRST_LAYER + 4 * D + 2 * FF) // (2 * shard_rows)


def sum_on_plane(grad_rows, factors, extra, shard_rows):
    half_rows, width = shard_rows // 2, grad_rows.shape[1]
    planes = grad_rows.shape[0] // (2 * shard_rows)
    chunks = reduce_chunks(half_rows, 0.75)
    most = max(first + second for _, first, second in chunks)
    half_cols = width // 2
    dtype = grad_rows.dtype
    return pl.pallas_call(
        functools.partial(reduce_kernel, chunks, low_plane(shard_rows)),
        out_shape=(
            jax.ShapeDtypeStruct((shard_rows + 16, width), dtype),
            jax.ShapeDtypeStruct((8,) + factors.shape, factors.dtype),
            jax.ShapeDtypeStruct((8,) + extra.shape, extra.dtype),
            jax.ShapeDtypeStruct((8, 8, 128), jnp.float32),
        ),
        in_specs=[pl.BlockSpec(memory_space=pl.ANY)] * 3,
        out_specs=[pl.BlockSpec(memory_space=pl.ANY)] * 4,
        scratch_shapes=[
            pltpu.VMEM((2, planes, 2, 2, most, half_cols), dtype),
            pltpu.VMEM((planes, 2, 2, half_rows, half_cols), dtype),
            pltpu.VMEM((planes, 2, sum(chunk[1] for chunk in chunks), half_cols), dtype),
            pltpu.VMEM((planes, 2, sum(chunk[2] for chunk in chunks), half_cols), dtype),
            pltpu.VMEM((planes, half_rows, half_cols), dtype),
            pltpu.VMEM((8, 128), jnp.float32),
            pltpu.VMEM(factors.shape, factors.dtype),
            pltpu.VMEM(extra.shape, extra.dtype),
            pltpu.SemaphoreType.DMA((2,)),
            pltpu.SemaphoreType.DMA((6, len(chunks))),
            pltpu.SemaphoreType.DMA((6, len(chunks))),
            pltpu.SemaphoreType.DMA((2, 3)),
            pltpu.SemaphoreType.DMA((3,)),
            pltpu.SemaphoreType.DMA((2,)),
            pltpu.SemaphoreType.DMA((2,)),
        ],
        compiler_params=pltpu.CompilerParams(
            collective_id=1, has_side_effects=True, vmem_limit_bytes=56 * 2**20
        ),
        name="reduce",
    )(grad_rows.reshape(planes, 2, 2, half_rows, width), factors, extra)


def update_kernel(
    shape,
    own_hbm,
    rest_hbm,
    master_hbm,
    first_hbm,
    second_hbm,
    factors_ref,
    extras_ref,
    squares_ref,
    first_out,
    second_out,
    total_out,
    summary_ref,
    own,
    rest,
    weights,
    first,
    second,
    new_first,
    new_second,
    mine,
    other,
    core_in,
    y_out,
    y_in,
    load_sems,
    store_sems,
    sends,
    recvs,
    total_sem,
    low_squares_ref,
    low_sems,
):
    half_rows, piece, pieces, low_from = shape
    half_cols = mine.shape[-1]
    y, c, z, x = place()
    over_y = device_at(1 - y, c, z, x)
    sibling = device_at(y, 1 - c, z, x)
    barrier = pltpu.get_barrier_semaphore()
    for partner in (over_y, sibling):
        pl.semaphore_signal(barrier, inc=1, device_id=partner, device_id_type=MESH)
    has_factors = z >= low_from

    @pl.when(z < 4 - low_from)
    def _():
        pl.semaphore_signal(
            barrier, inc=1, device_id=device_at(y, c, z + low_from, x), device_id_type=MESH
        )

    def row_at(index):
        half = jnp.where(index < pieces, 1 - y, y)
        return pl.multiple_of(half * half_rows + index % pieces * piece, 16)

    def loads(index):
        slot = index % 2
        rows = pl.ds(row_at(index), piece)
        longer = pl.ds(row_at(index), piece + 16)
        return [
            pltpu.make_async_copy(own_hbm.at[longer], own.at[slot], load_sems.at[0, slot]),
            pltpu.make_async_copy(rest_hbm.at[rows], rest.at[slot], load_sems.at[1, slot]),
            pltpu.make_async_copy(master_hbm.at[rows], weights.at[slot], load_sems.at[2, slot]),
            pltpu.make_async_copy(first_hbm.at[rows], first.at[slot], load_sems.at[3, slot]),
            pltpu.make_async_copy(second_hbm.at[rows], second.at[slot], load_sems.at[4, slot]),
        ]

    def stores(index):
        slot = index % 2
        rows = pl.ds(row_at(index), piece)
        return [
            pltpu.make_async_copy(new_first.at[slot], first_out.at[rows], store_sems.at[0, slot]),
            pltpu.make_async_copy(new_second.at[slot], second_out.at[rows], store_sems.at[1, slot]),
        ]

    for copy in loads(0):
        copy.start()

    def gram(at, width):
        values = factors_ref[:, :, at : at + width].reshape(128, width)
        return dot(values, values, 1, 1)

    row = lax.broadcasted_iota(jnp.int32, (128, 128), 0) % 16
    col = lax.broadcasted_iota(jnp.int32, (128, 128), 1) % 16
    head = gram(FF + 3 * D, D)
    shifted_head = pltpu.roll(pltpu.roll(head, 120, 0), 120, 1)
    products = gram(0, FF) * gram(FF + 2 * D, D) + gram(FF, D) * gram(FF + D, D)
    low_squares = jnp.where(row // 8 == col // 8, products, 0.0)
    low_squares = low_squares + jnp.where((row < 8) & (col < 8), head * shifted_head, 0.0)
    pl.semaphore_wait(barrier, 2 + jnp.where(has_factors, 1, 0))
    to_low = pltpu.make_async_remote_copy(
        src_ref=low_squares_ref,
        dst_ref=low_squares_ref,
        send_sem=low_sems.at[0],
        recv_sem=low_sems.at[1],
        device_id=device_at(y, c, z - low_from, x),
        device_id_type=MESH,
    )

    @pl.when(has_factors)
    def _():
        low_squares_ref[...] = jnp.sum(low_squares.reshape(16, 8, 128), axis=0)
        to_low.start()

    @pl.when(jnp.logical_not(has_factors))
    def _():
        to_low.wait_recv()

    extra = jnp.sum(extras_ref[...], axis=0)
    norm_squares = extra[:HEAD_AT] * extra[:HEAD_AT]
    square_all = jnp.sum(squares_ref[...]) + jnp.sum(low_squares_ref[...]) + jnp.sum(norm_squares)
    count_all = extra[12:13, 1:2]
    grad_norm = jnp.sqrt(jnp.zeros((1, 1), jnp.float32) + square_all) / count_all
    factor = CLIP_MAX / jnp.maximum(grad_norm, CLIP_MAX) / count_all
    summary_ref[...] = extra
    summary_ref[10:12, :] = extra[10:12] * factor
    summary_ref[13:14, :] = jnp.broadcast_to(grad_norm, (1, D))

    flat_start = (z * 2 + x) * (2 * half_rows)
    layer_start = BLOCK + SEQ + 1

    def step(index):
        slot = index % 2
        for copy in loads(index):
            copy.wait()

        @pl.loop(0, piece // 16)
        def _(block):
            at = pl.multiple_of(block * 16, 16)
            rows = pl.ds(at, 16)
            longer = own[slot, pl.ds(at, 32), :].astype(jnp.float32)
            flat = flat_start + row_at(index) + at + lax.broadcasted_iota(jnp.int32, (16, D), 0)
            grads = jnp.where(flat < layer_start, longer[:16], longer[SPARE : SPARE + 16])
            spared = jnp.where(flat < layer_start, flat, flat + SPARE)
            grads = jnp.where(dense_row(spared), grads, rest[slot, rows, :].astype(jnp.float32))
            clipped = grads * factor
            moment_one = BETA_ONE * first[slot, rows, :] + (1.0 - BETA_ONE) * clipped
            moment_two = BETA_TWO * second[slot, rows, :] + (1.0 - BETA_TWO) * clipped * clipped
            new_first[slot, rows, :] = moment_one
            new_second[slot, rows, :] = moment_two
            corrected_one = moment_one * (1.0 / (1.0 - BETA_ONE**STEP))
            corrected_two = moment_two * (1.0 / (1.0 - BETA_TWO**STEP))
            change = corrected_one / (jnp.sqrt(corrected_two) + ADAM_EPS) + DECAY * weights[slot, rows, :]
            change = low(RATE * change)
            left, right = change[:, :half_cols], change[:, half_cols:]
            mine[index, rows, :] = jnp.where(c == 0, left, right)
            other[index, rows, :] = jnp.where(c == 0, right, left)

        for copy in stores(index):
            copy.start()
        pltpu.make_async_remote_copy(
            src_ref=other.at[index],
            dst_ref=core_in.at[index],
            send_sem=sends.at[index],
            recv_sem=recvs.at[index],
            device_id=sibling,
            device_id_type=MESH,
        ).start()

    def fold(index):
        pltpu.make_async_copy(core_in.at[index], core_in.at[index], recvs.at[index]).wait()
        total = mine[index].astype(jnp.float32) + core_in[index].astype(jnp.float32)
        if index < pieces:
            y_out[index] = low(total)
            pltpu.make_async_remote_copy(
                src_ref=y_out.at[index],
                dst_ref=y_in.at[index],
                send_sem=sends.at[2 * pieces + index],
                recv_sem=recvs.at[2 * pieces + index],
                device_id=over_y,
                device_id_type=MESH,
            ).start()
        else:
            mine[index] = low(total)

    steps = 2 * pieces
    for index in range(steps):
        if index + 1 < steps:
            if index >= 1:
                for copy in stores(index - 1):
                    copy.wait()
            for copy in loads(index + 1):
                copy.start()
        step(index)
        if index >= 1:
            fold(index - 1)
    fold(steps - 1)

    def hand_over(index):
        rows = pl.ds(index * piece, piece)
        return pltpu.make_async_copy(mine.at[pieces + index], total_out.at[rows], total_sem.at[index])

    for index in range(pieces):
        at = 2 * pieces + index
        pltpu.make_async_copy(y_in.at[index], y_in.at[index], recvs.at[at]).wait()
        total = mine[pieces + index].astype(jnp.float32) + y_in[index].astype(jnp.float32)
        mine[pieces + index] = low(total)
        hand_over(index).start()
    for index in range(steps - 2, steps):
        for copy in stores(index):
            copy.wait()
    for index in range(steps):
        pltpu.make_async_copy(other.at[index], other.at[index], sends.at[index]).wait()
    for index in range(pieces):
        pltpu.make_async_copy(y_out.at[index], y_out.at[index], sends.at[steps + index]).wait()
        hand_over(index).wait()

    @pl.when(has_factors)
    def _():
        to_low.wait_send()


def update_rows(own, rest, master, first, second, factors, extras, squares):
    rows, width = master.shape
    half_rows, half_cols = rows // 2, width // 2
    pieces = 3
    piece = half_rows // pieces
    f32, bf16 = jnp.float32, jnp.bfloat16
    hbm = pl.BlockSpec(memory_space=pl.ANY)
    vmem = pl.BlockSpec(memory_space=pltpu.VMEM)
    return pl.pallas_call(
        functools.partial(update_kernel, (half_rows, piece, pieces, low_plane(rows))),
        out_shape=(
            jax.ShapeDtypeStruct((rows, width), f32),
            jax.ShapeDtypeStruct((rows, width), f32),
            jax.ShapeDtypeStruct((half_rows, half_cols), bf16),
            jax.ShapeDtypeStruct((16, width), f32),
        ),
        in_specs=[hbm] * 5 + [vmem] * 3,
        out_specs=[hbm] * 3 + [vmem],
        scratch_shapes=[
            pltpu.VMEM((2, piece + 16, width), bf16),
            pltpu.VMEM((2, piece, width), bf16),
            pltpu.VMEM((2, piece, width), f32),
            pltpu.VMEM((2, piece, width), f32),
            pltpu.VMEM((2, piece, width), f32),
            pltpu.VMEM((2, piece, width), f32),
            pltpu.VMEM((2, piece, width), f32),
            pltpu.VMEM((2 * pieces, piece, half_cols), bf16),
            pltpu.VMEM((2 * pieces, piece, half_cols), bf16),
            pltpu.VMEM((2 * pieces, piece, half_cols), bf16),
            pltpu.VMEM((pieces, piece, half_cols), bf16),
            pltpu.VMEM((pieces, piece, half_cols), bf16),
            pltpu.SemaphoreType.DMA((5, 2)),
            pltpu.SemaphoreType.DMA((2, 2)),
            pltpu.SemaphoreType.DMA((3 * pieces,)),
            pltpu.SemaphoreType.DMA((3 * pieces,)),
            pltpu.SemaphoreType.DMA((pieces,)),
            pltpu.VMEM((8, 128), f32),
            pltpu.SemaphoreType.DMA((2,)),
        ],
        compiler_params=pltpu.CompilerParams(
            collective_id=3, has_side_effects=True, vmem_limit_bytes=48 * 2**20
        ),
        name="update",
    )(own, rest, master, first, second, factors, extras, squares)


def pairs_of(partner):
    pairs = []
    for source in range(32):
        y, c, z, x = source // 16, source // 8 % 2, source // 2 % 4, source % 2
        target = partner(y, c, z, x)
        if target is not None:
            pairs.append((source, (target[0] * 2 + target[1]) * 8 + target[2] * 2 + target[3]))
    return pairs


def next_half(y, c, z, x):
    place_in_row = (z * 2 + x) * 2 + y + 1
    if place_in_row == 16:
        return None
    return (place_in_row % 2, c, place_in_row // 4, place_in_row // 2 % 2)


def on_grid_step(grad_rows, factors, extra, master, outer_momentum, first, second):
    rows, width = master.shape
    half_rows, half_cols = rows // 2, width // 2
    y, c, z, x = place()
    rank = lax.axis_index("dp")
    own, factors, extras, squares = sum_on_plane(grad_rows, factors, extra, rows)
    following = lax.ppermute(own[:16], "dp", [(source, source - 1) for source in range(1, 8)])
    own = lax.dynamic_update_slice(own, following, (rows, 0))
    rest = low_rank_rows(factors, jnp.sum(extras, axis=0), rank * rows + SPARE, rows)
    first, second, total, summary = update_rows(
        own, rest.astype(jnp.bfloat16), master, first, second, factors, extras, squares
    )
    groups = lax.axis_size("group")
    at = (y * half_rows, c * half_cols)
    quarter = [lax.dynamic_slice(whole, at, (half_rows, half_cols)) for whole in (master, outer_momentum)]
    part, _ = nesterov(*quarter, total.astype(jnp.float32) / groups)
    before = lax.ppermute(part[-16:], ("group", "dp"), pairs_of(next_half))
    moved = jnp.concatenate([before, part], axis=0)[16 - SPARE :][:half_rows]
    flat_row = rank * rows + y * half_rows + lax.broadcasted_iota(jnp.int32, (half_rows, 1), 0)
    part = jnp.where(flat_row < layout_rows()[1], part, moved).astype(jnp.bfloat16)
    soup_rows = gather_rows(part, rows)
    total, soup_rows = lax.optimization_barrier((total, soup_rows))
    over_y = lax.ppermute(total, ("group", "dp"), pairs_of(lambda y, c, z, x: (1 - y, c, z, x)))

    def finish(over_y):
        column = jnp.where(y == 0, jnp.stack([total, over_y]), jnp.stack([over_y, total]))
        column = column.reshape(rows, half_cols)
        sibling = lax.ppermute(
            column, ("group", "dp"), pairs_of(lambda y, c, z, x: (y, 1 - c, z, x))
        )
        whole = jnp.where(
            c == 0,
            jnp.concatenate([column, sibling], axis=1),
            jnp.concatenate([sibling, column], axis=1),
        )
        return nesterov(master, outer_momentum, whole.astype(jnp.float32) / groups)

    return (over_y, finish, first, second, summary, soup_rows)


def fetch_weights(params, pixel_rows=None, notes=None):
    rows, width = params.shape
    ranks, rank = lax.axis_size("dp"), lax.axis_index("dp")
    before = lax.ppermute(params[-16:], "dp", [(source, source + 1) for source in range(ranks - 1)])
    longer = jnp.concatenate([before, params], axis=0)
    in_place = lax.broadcasted_iota(jnp.int32, (rows, 1), 0) + rank * rows < layout_rows()[1]
    if not on_grid():
        moved = jnp.where(in_place, params, longer[16 - SPARE :][:rows])
        full = lax.all_gather(moved.astype(jnp.bfloat16), "dp", axis=0, tiled=True)
        return full if pixel_rows is None else (full, pixel_rows, notes)
    y, c, _, _ = place()
    half, half_cols = rows // 2, width // 2
    part = lax.dynamic_slice(params, (y * half, c * half_cols), (half, half_cols))
    moved = lax.dynamic_slice(longer, (y * half + 16 - SPARE, c * half_cols), (half, half_cols))
    in_place = lax.dynamic_slice(in_place, (y * half, 0), (half, 1))
    return gather_rows(jnp.where(in_place, part, moved).astype(jnp.bfloat16), rows, pixel_rows, notes)


def low_rank_rows(factors, extra, first_row, count):
    last_layer = FIRST_LAYER + 4 * D + 2 * FF
    devices = factors.shape[0]

    def half(at, width, which):
        piece = factors[:, 8 * which : 8 * which + 8, at : at + width]
        return piece.reshape(devices * 8, width)

    norms = extra[:16].astype(jnp.bfloat16)
    sections = [
        (last_layer, half(FF, D, 0), half(FF + D, D, 0)),
        (last_layer + 3 * D, half(FF, D, 1), half(FF + D, D, 1)),
        (last_layer + 4 * D, half(0, FF, 0), half(FF + 2 * D, D, 0)),
        (last_layer + 4 * D + FF, half(0, FF, 1), half(FF + 2 * D, D, 1)),
        (TAIL_START, jnp.eye(16, HEAD_AT, dtype=jnp.bfloat16), norms),
        (TAIL_START + HEAD_AT, half(FF + 3 * D, EMB, 0), half(FF + 3 * D, D, 1)),
    ]
    row = first_row + jnp.arange(count)
    lefts, rights = [], []
    for start, left, right in sections:
        width = left.shape[1]
        padded = jnp.pad(left, ((0, 0), (count, count)))
        at = jnp.clip(first_row - start + count, 0, width + count)
        window = lax.dynamic_slice(padded, (0, at), (left.shape[0], count))
        inside = (row >= start) & (row < start + width)
        lefts.append(jnp.where(inside[None], window, jnp.zeros_like(window)))
        rights.append(right)
    return lax.dot_general(
        jnp.concatenate(lefts, axis=0),
        jnp.concatenate(rights, axis=0),
        (((0,), (0,)), ((), ())),
        preferred_element_type=jnp.float32,
    )


def reduce_rows(grad_rows, factors, extra, count):
    ranks, rank = lax.axis_size("dp"), lax.axis_index("dp")
    flat_row = rank * count + lax.broadcasted_iota(jnp.int32, (count, 1), 0)
    rest = low_rank_rows(factors[None], extra, 0, ranks * count).astype(jnp.bfloat16)
    whole = jnp.where(dense_row(jnp.arange(DENSE_END))[:, None], grad_rows, rest[:DENSE_END])
    whole = jnp.concatenate([whole, rest[DENSE_END:]], axis=0)
    shard = lax.psum_scatter(whole, "dp", scatter_dimension=0, tiled=True)
    following = lax.ppermute(shard[:16], "dp", [(source, source - 1) for source in range(1, ranks)])
    shifted = jnp.concatenate([shard[SPARE:], following[:SPARE]], axis=0)
    summed = jnp.where(flat_row < layout_rows()[1], shard, shifted).astype(jnp.float32)
    return (summed, lax.psum(extra, "dp"))


def any_grid_step(grad_rows, factors, extra, master, outer_momentum, first, second):
    reduced, extra = reduce_rows(grad_rows, factors, extra, master.shape[0])
    count_all = extra[12, 1]
    grad_norm = jnp.sqrt(lax.psum(jnp.sum(reduced * reduced), "dp")) / count_all
    factor = CLIP_MAX / jnp.maximum(grad_norm, CLIP_MAX) / count_all
    params, first, second = adam_update(master, first, second, reduced * factor, STEP)
    delta = (master - params).astype(jnp.bfloat16)
    mean_delta = lax.psum(delta, "group").astype(jnp.float32) / lax.axis_size("group")
    outer = nesterov(master, outer_momentum, mean_delta)
    summary = jnp.concatenate(
        [extra[:10], extra[10:12] * factor, extra[12:13], jnp.full((3, D), grad_norm)], axis=0
    )
    return (outer, lambda done: done, first, second, summary, fetch_weights(outer[0]))


def dense_row(row):
    last_layer = FIRST_LAYER + 4 * D + 2 * FF
    return (row < last_layer) | ((row >= last_layer + D) & (row < DENSE_END))


def adam_update(params, moment_one, moment_two, clipped, step_number):
    moment_one = BETA_ONE * moment_one + (1.0 - BETA_ONE) * clipped
    moment_two = BETA_TWO * moment_two + (1.0 - BETA_TWO) * clipped * clipped
    corrected_one = moment_one / (1.0 - BETA_ONE**step_number)
    corrected_two = moment_two / (1.0 - BETA_TWO**step_number)
    params = params - RATE * (corrected_one / (jnp.sqrt(corrected_two) + ADAM_EPS) + DECAY * params)
    return (params, moment_one, moment_two)


def nesterov(master_rows, momentum_rows, mean_delta):
    momentum_next = OUTER_MOM * momentum_rows + mean_delta
    return (master_rows - OUTER_RATE * (mean_delta + OUTER_MOM * momentum_next), momentum_next)


def token_rows(pixel_block):
    images, patches, _ = pixel_block.shape
    padded = jnp.pad(pixel_block, ((0, 0), (0, TOKENS - patches), (0, 0)))
    return padded.reshape(images * TOKENS, PATCH_IN)


def per_device(
    pixels,
    counts,
    labels,
    text,
    master,
    outer_momentum,
    first_moment,
    second_moment,
    eval_pixels,
    eval_counts,
    eval_labels,
):
    slots = pixels.shape[2]
    live = (jnp.arange(slots)[None, :] < counts[0]).astype(jnp.float32).reshape(-1)
    step_labels = labels[0].reshape(-1)
    step_pixels = token_rows(pixels[0].reshape((-1,) + pixels.shape[3:]))
    notes = image_notes(step_labels, live)
    weights, step_pixels, notes = fetch_weights(master, step_pixels, notes)
    grad_rows, factors, extra = run_tower(weights, step_pixels, notes, text, True)
    step = on_grid_step if on_grid() else any_grid_step
    waiting, finish, moment_one, moment_two, summary, soup_rows = step(
        grad_rows, factors, extra, master, outer_momentum, first_moment[0], second_moment[0]
    )
    eval_live = (jnp.arange(eval_pixels.shape[0]) < eval_counts[0]).astype(jnp.float32)
    eval_notes = image_notes(eval_labels, eval_live)
    carried = (moment_one, moment_two) if on_grid() else ()
    eval_tile, *carried = run_tower(
        soup_rows, token_rows(eval_pixels), eval_notes, text, False, carried
    )
    if on_grid():
        moment_one, moment_two = carried
    eval_tile, waiting = lax.optimization_barrier((eval_tile, waiting))
    new_master, new_outer = finish(waiting)
    eval_losses = eval_tile[: eval_labels.shape[0], 0]
    return (
        new_master,
        new_outer,
        moment_one[None],
        moment_two[None],
        summary[13:14, :1],
        summary[12:13, :1],
        summary[12:13, 1:2],
        summary[10:12][None, None],
        eval_losses,
    )


def solution(mesh):
    return jax.shard_map(
        per_device,
        mesh=mesh,
        in_specs=(
            P(None, None, ("group", "dp"), None, None),
            P(None, None, ("group", "dp")),
            P(None, None, ("group", "dp")),
            P(),
            P("dp", None),
            P("dp", None),
            P("group", "dp", None),
            P("group", "dp", None),
            P(("group", "dp"), None, None),
            P(("group", "dp")),
            P(("group", "dp")),
        ),
        out_specs=(
            P("dp", None),
            P("dp", None),
            P("group", "dp", None),
            P("group", "dp", None),
            P("group", None),
            P("group", None),
            P("group", None),
            P("group", None, None, None),
            P(("group", "dp")),
        ),
        check_vma=False,
    )
```

```python
import functools

import jax
import jax.numpy as jnp
from jax import lax
from jax.experimental import pallas as pl
from jax.experimental.pallas import tpu as pltpu
from jax.sharding import PartitionSpec as P

MESH = pl.DeviceIdType.MESH

D = 768
HEADS = 12
HEAD = 64
FF = 3072
PATCH_IN = 3072
EMB = 512
CLASSES = 1000
LAYERS = 2
MICRO = 2
STEP = 10
SEQ = 50
ROWS_RAW = 22079


LN_EPS = 1e-05
NORM_EPS = 1e-06
LOGIT_SCALE = 50.0
SMOOTH = 0.1
CLIP_MAX = 0.02
BETA_ONE = 0.9
BETA_TWO = 0.98
ADAM_EPS = 1e-08
RATE = 0.02
DECAY = 0.1
OUTER_RATE = 0.7
OUTER_MOM = 0.9
GELU_SLOPE = 1.702
SPARE = 13
FIRST_SHARE = 0.6
LOOK_AHEAD = 3
PARCEL_STEP = 1
REDUCE_HEAD = [4, 6]
RELAY_LAG = 2
REDUCE_TAIL = [4]


def layout_rows():
    table_start = PATCH_IN
    layer_start = table_start + SEQ + 1
    block_size = 4 * D + 2 * FF
    norm_start = layer_start + LAYERS * block_size
    head_start = norm_start + 4 * LAYERS + 4
    return (table_start, layer_start, block_size, norm_start, head_start)


TOKENS = 56
CLASS_AT = 49
PAIR = 2 * TOKENS
BLOCK = 3072
TAIL_START = BLOCK + SEQ + 1 + SPARE + LAYERS * (4 * D + 2 * FF)
TAIL_ROWS = 544
HEAD_AT = 4 * LAYERS + 4
TABLE_ROWS = SEQ + 1 + SPARE
LOW_COLS = 2 * FF
FIRST_LAYER = BLOCK + TABLE_ROWS
DENSE_END = FIRST_LAYER + 4 * D + 2 * FF + 3 * D


def dot(first, second, first_dim=1, second_dim=0):
    return lax.dot_general(
        first,
        second,
        (((first_dim,), (second_dim,)), ((), ())),
        preferred_element_type=jnp.float32,
    )


def low(values):
    return values.astype(jnp.bfloat16)


def norm_parts(values):
    centred = values - jnp.mean(values, -1, keepdims=True)
    scale = lax.rsqrt(jnp.mean(centred * centred, -1, keepdims=True) + LN_EPS)
    return (centred * scale, scale)


def norm_back(values, gain, grad):
    unit, scale = norm_parts(values)
    weighted = grad * gain
    mean_one = jnp.mean(weighted, -1, keepdims=True)
    mean_two = jnp.mean(weighted * unit, -1, keepdims=True)
    return (scale * (weighted - mean_one - unit * mean_two), grad * unit)


def wide(values, rows):
    return jnp.concatenate(
        [values, jnp.zeros((rows - values.shape[0], values.shape[1]), values.dtype)], axis=0
    )


def head_mask(rows, lanes, first_head):
    row = lax.broadcasted_iota(jnp.int32, (rows, lanes), 0)
    lane = lax.broadcasted_iota(jnp.int32, (rows, lanes), 1)
    return (lane // HEAD + first_head) == row


def lane_pick(values, head):
    lane = lax.broadcasted_iota(jnp.int32, values.shape, 1)
    return jnp.where(lane // HEAD == head, values, jnp.zeros_like(values))


def stack_heads(values):
    return jnp.concatenate([lane_pick(values, head) for head in range(4)], axis=0)


def fold_heads(values):
    rows = values.shape[0] // 4
    total = lane_pick(values[:rows], 0)
    for head in range(1, 4):
        total = total + lane_pick(values[head * rows : (head + 1) * rows], head)
    return total


def soft(scores):
    scores = scores - jnp.max(scores, -1, keepdims=True)
    grown = jnp.exp(scores)
    return grown / jnp.sum(grown, -1, keepdims=True)


def pair_bias():
    row = lax.broadcasted_iota(jnp.int32, (PAIR, PAIR), 0)
    col = lax.broadcasted_iota(jnp.int32, (PAIR, PAIR), 1)
    fits = (row // TOKENS == col // TOKENS) & (col % TOKENS < SEQ)
    return jnp.where(fits, 0.0, -1e30)


def class_bias():
    row = lax.broadcasted_iota(jnp.int32, (32, PAIR), 0)
    col = lax.broadcasted_iota(jnp.int32, (32, PAIR), 1)
    fits = (row // 16 == col // TOKENS) & (col % TOKENS < SEQ)
    return jnp.where(fits, 0.0, -1e30)


def spread_heads(values):
    keep = head_mask(16, D, 0)
    rows = jnp.broadcast_to(values[:, None, :], (8, 16, D))
    return jnp.where(keep[None], rows, 0.0).reshape(128, D)


def unspread_heads(values):
    keep = head_mask(16, D, 0)
    return jnp.sum(jnp.where(keep[None], values.reshape(8, 16, D), 0.0), axis=1)


def tower_kernel(images, with_grads, carry, *refs):
    rows_all = images * TOKENS
    pairs = images // 2
    (w_hbm, pix_hbm, text_ref, note_ref), refs = refs[:4], refs[4:]
    if with_grads:
        (g_hbm, factor_ref, extra_ref), refs = refs[:3], refs[3:]
    else:
        carried, refs = refs[:carry], refs[carry:]
        (loss_ref,), refs = refs[:1], refs[1:]
        carried_out, refs = refs[:carry], refs[carry:]
    (wbuf, tail, table, pix, emb, hid0, mid0, hid1, acc, qkv, norm_a, norm_b, mixed, pre, act), refs = (
        refs[:15],
        refs[15:],
    )
    (norm_c, kv), refs = refs[:2], refs[2:]
    if with_grads:
        (dhid, dqkv, gb, dmix, stage, stage_sem), refs = refs[:6], refs[6:]
    elif carry:
        (hold, hold_sems), refs = refs[:2], refs[2:]
    (wsem, small_sem) = refs

    layer_at = [FIRST_LAYER + index * (4 * D + 2 * FF) for index in range(LAYERS)]
    order = [0]
    for start in layer_at:
        order += [start, start + 4 * D, start + 4 * D + FF]
    if with_grads:
        order += [layer_at[0] + 4 * D + FF, layer_at[0] + 4 * D, layer_at[0]]
    slot_of = [0, 1, 2, 0, 1, 2, 0, 0, 2, 1]

    def fetch(index):
        return pltpu.make_async_copy(
            w_hbm.at[pl.ds(order[index], BLOCK)], wbuf.at[slot_of[index]], wsem.at[slot_of[index]]
        )

    hops = []
    if carry:
        piece = hold.shape[1]
        for source, target in zip(carried, carried_out):
            for start in range(0, source.shape[0], piece):
                hops.append((source.at[pl.ds(start, piece)], target.at[pl.ds(start, piece)]))

    def hop_in(index):
        slot = index % 4
        return pltpu.make_async_copy(hops[index][0], hold.at[slot], hold_sems.at[0, slot])

    def hop_out(index):
        slot = index % 4
        return pltpu.make_async_copy(hold.at[slot], hops[index][1], hold_sems.at[1, slot])

    hopped = [0]

    def hop():
        index = hopped[0]
        if index < len(hops):
            hop_in(index).wait()
            hop_out(index).start()
            if index >= 2:
                hop_out(index - 2).wait()
            if 2 <= index and index + 2 < len(hops):
                hop_in(index + 2).start()
        hopped[0] = index + 1

    for index in range(min(4, len(hops))):
        hop_in(index).start()

    load_pix = pltpu.make_async_copy(pix_hbm, pix, small_sem.at[0])
    load_tail = pltpu.make_async_copy(
        w_hbm.at[pl.ds(TAIL_START, TAIL_ROWS)], tail, small_sem.at[1]
    )
    load_table = pltpu.make_async_copy(w_hbm.at[pl.ds(BLOCK, TABLE_ROWS)], table, small_sem.at[2])
    fetch(0).start()
    load_pix.start()
    load_table.start()
    load_tail.start()
    fetch(1).start()
    fetch(2).start()

    def chunks_of(count=rows_all // PAIR):
        return pl.loop(0, count)

    def rows_at(index):
        return pl.ds(pl.multiple_of(index * PAIR, PAIR), PAIR)

    def norm_row(index):
        return tail[0:16, :].astype(jnp.float32)[index : index + 1]

    def class_rows(ref):
        picked = [ref[TOKENS * i + CLASS_AT : TOKENS * i + CLASS_AT + 1, :] for i in range(images)]
        if images < 8:
            picked.append(jnp.zeros((8 - images, ref.shape[1]), ref.dtype))
        return jnp.concatenate(picked, axis=0)

    def add_class_rows(ref, values):
        for i in range(images):
            at = slice(TOKENS * i + CLASS_AT, TOKENS * i + CLASS_AT + 1)
            ref[at, :] = ref[at, :] + values[i : i + 1]

    def layer_norm_into(source, target, gain_row):
        gain, bias = norm_row(gain_row), norm_row(gain_row + 1)

        @chunks_of()
        def _(index):
            rows = rows_at(index)
            unit, _ = norm_parts(source[rows, :])
            target[rows, :] = (unit * gain + bias).astype(target.dtype)

    load_table.wait()
    load_tail.wait()
    load_pix.wait()
    fetch(0).wait()
    emb[...] = dot(pix[...], wbuf[0])
    hop()
    fetch(3).start()
    rows_table = table[...].astype(jnp.float32)
    added = pltpu.roll(rows_table, TABLE_ROWS - 2, 0)[:TOKENS]
    token = lax.broadcasted_iota(jnp.int32, (TOKENS, D), 0)
    added = jnp.where(token == CLASS_AT, rows_table[0:1] + rows_table[1:2], added)
    added = jnp.where(token < SEQ, added, 0.0)

    gain, bias = norm_row(0), norm_row(1)

    @chunks_of()
    def _(index):
        rows = rows_at(index)
        values = emb[rows, :] + jnp.concatenate([added, added], axis=0)
        emb[rows, :] = values
        unit, _ = norm_parts(values)
        hid0[rows, :] = unit * gain + bias

    layer_norm_into(hid0, norm_a, 2)
    hop()
    fetch(1).wait()

    @pl.loop(0, 3)
    def _(part):
        at = pl.ds(pl.multiple_of(part * D, D), D)
        qkv[:, at] = low(dot(norm_a[...], wbuf[1, at, :]))

    bias_pair = pair_bias()
    hop()

    def lanes(part, group):
        return slice(part * D + group * 256, part * D + (group + 1) * 256)

    def pair_soft(queries, keys):
        scores = dot(queries, keys, 1, 1) * HEAD ** (-0.5)
        scores = scores.reshape(4, PAIR, PAIR) + bias_pair[None]
        return soft(scores).reshape(4 * PAIR, PAIR)

    @pl.loop(0, pairs)
    def _(index):
        rows = rows_at(index)
        for group in range(3):
            queries = stack_heads(qkv[rows, lanes(0, group)])
            probs = low(pair_soft(queries, qkv[rows, lanes(1, group)]))
            out = dot(probs, qkv[rows, lanes(2, group)])
            mixed[rows, lanes(0, group)] = low(fold_heads(out))

    acc[...] = dot(mixed[...], wbuf[1, 3 * D : 4 * D, :])
    hop()
    fetch(4).start()
    gain2, bias2 = norm_row(4), norm_row(5)
    hop()

    @chunks_of()
    def _(index):
        rows = rows_at(index)
        values = hid0[rows, :] + acc[rows, :]
        mid0[rows, :] = values
        unit, _ = norm_parts(values)
        norm_b[rows, :] = low(unit * gain2 + bias2)

    fetch(2).wait()

    @pl.loop(0, 3)
    def _(part):
        at = pl.ds(pl.multiple_of(part * 1024, 1024), 1024)
        values = dot(norm_b[...], wbuf[2, at, :], 1, 1)
        if with_grads:
            pre[:, at] = low(values)
        act[:, at] = low(values * jax.nn.sigmoid(GELU_SLOPE * values))

    fetch(5).start()
    fetch(3).wait()
    hop()
    acc[...] = dot(act[...], wbuf[0])
    fetch(6).start()
    gain3, bias3 = norm_row(6), norm_row(7)
    hop()

    @chunks_of()
    def _(index):
        rows = rows_at(index)
        values = mid0[rows, :] + acc[rows, :]
        hid1[rows, :] = values
        unit, _ = norm_parts(values)
        norm_c[rows, :] = low(unit * gain3 + bias3)

    fetch(4).wait()

    @pl.loop(0, 2)
    def _(part):
        kv[:, pl.ds(pl.multiple_of(part * D, D), D)] = low(
            dot(norm_c[...], wbuf[1, pl.ds(pl.multiple_of(part * D + D, D), D), :])
        )

    class_hid = class_rows(hid1)
    hop()
    unit_one, _ = norm_parts(class_hid)
    class_a = low(wide(unit_one * gain3 + bias3, 16))
    class_q = low(dot(class_a, wbuf[1, 0:D, :]))
    spread_q = low(spread_heads(class_q[:8].astype(jnp.float32)))
    bias_class = class_bias()
    class_probs, outs = [], []
    for pair in range(pairs):
        rows = slice(pair * PAIR, (pair + 1) * PAIR)
        scores = dot(spread_q[32 * pair : 32 * pair + 32], kv[rows, 0:D], 1, 1)
        probs = soft(scores * HEAD ** (-0.5) + bias_class)
        class_probs.append(probs)
        outs.append(dot(low(probs), kv[rows, D : 2 * D]))
    for _ in range(4 - pairs):
        outs.append(jnp.zeros((32, D), jnp.float32))
    class_mix = low(wide(unspread_heads(jnp.concatenate(outs, axis=0)), 16))
    class_mid = class_hid + dot(class_mix, wbuf[1, 3 * D : 4 * D, :])[:8]
    hop()
    unit_two, _ = norm_parts(class_mid)
    gain4, bias4 = norm_row(8), norm_row(9)
    class_b = low(wide(unit_two * gain4 + bias4, 16))
    fetch(5).wait()
    class_pre = dot(class_b, wbuf[2], 1, 1)
    hop()
    gate = jax.nn.sigmoid(GELU_SLOPE * class_pre)
    class_act = low(class_pre * gate)
    fetch(6).wait()
    class_out = class_mid + dot(class_act, wbuf[0])[:8]
    hop()
    gain5, bias5 = norm_row(10), norm_row(11)
    unit_post, _ = norm_parts(class_out)
    pooled = low(wide(unit_post * gain5 + bias5, 16))

    hop()
    pooled_out = dot(pooled, tail[...], 1, 1)
    pooled_out = jnp.concatenate([pooled_out, jnp.zeros((16, 640 - TAIL_ROWS), jnp.float32)], axis=1)
    embedded = pltpu.roll(pooled_out, 640 - HEAD_AT, 1)[:8, :EMB]
    length = lax.rsqrt(jnp.sum(embedded * embedded, -1, keepdims=True) + NORM_EPS)
    unit_rows = embedded * length
    logits = LOGIT_SCALE * dot(low(wide(unit_rows, 16)), text_ref[...], 1, 1)[:8]
    top = jnp.max(logits, -1, keepdims=True)
    log_total = top + jnp.log(jnp.sum(jnp.exp(logits - top), -1, keepdims=True))
    log_probs = logits - log_total
    classes = lax.broadcasted_iota(jnp.int32, logits.shape, 1)
    label = note_ref[:, 0:1].astype(jnp.int32)
    target = jnp.where(classes == label, 1.0 - SMOOTH, 0.0) + SMOOTH / CLASSES
    live = note_ref[:, 1:2]
    losses = -live * jnp.sum(target * log_probs, -1, keepdims=True)
    if not with_grads:
        loss_ref[...] = jnp.broadcast_to(losses, loss_ref.shape)
        while hopped[0] < len(hops):
            hop()
        for index in range(max(0, len(hops) - 2), len(hops)):
            hop_out(index).wait()
        return

    grad_raw = low(wide(LOGIT_SCALE * ((jnp.exp(log_probs) - target) * live), 16))
    grad_unit = dot(grad_raw, text_ref[...])[:8]
    along = jnp.sum(grad_unit * embedded, -1, keepdims=True)
    grad_embed = grad_unit * length - embedded * (length * length * length * along)
    grad_embed = low(wide(grad_embed, 16))
    grad_tail = jnp.concatenate(
        [grad_embed.astype(jnp.float32), jnp.zeros((16, 640 - EMB), jnp.float32)], axis=1
    )
    grad_tail = low(pltpu.roll(grad_tail, HEAD_AT, 1)[:, :TAIL_ROWS])
    grad_pooled = dot(grad_tail, tail[...])[:8]

    def put_extra(row, values):
        extra_ref[row : row + 1, :] = values

    extra_ref[...] = jnp.zeros_like(extra_ref)
    lane = lax.broadcasted_iota(jnp.int32, (1, D), 1)
    put_extra(12, jnp.where(lane == 0, jnp.sum(losses), jnp.where(lane == 1, jnp.sum(live), 0.0)))

    def class_norm_back(values, gain_row, grad):
        result, terms = norm_back(values, norm_row(gain_row), grad)
        put_extra(gain_row, jnp.sum(terms, 0, keepdims=True))
        put_extra(gain_row + 1, jnp.sum(grad, 0, keepdims=True))
        return result

    grad_out = class_norm_back(class_out, 10, grad_pooled)

    grad_b = low(wide(grad_out, 16))
    grad_act = dot(grad_b, wbuf[0], 1, 1)
    grad_pre = low(grad_act * (gate + GELU_SLOPE * class_pre * gate * (1.0 - gate)))
    fetch(7).start()
    grad_mid = grad_out + class_norm_back(class_mid, 8, dot(grad_pre, wbuf[2])[:8])
    fetch(8).start()
    grad_proj = low(wide(grad_mid, 16))
    grad_mix = low(dot(grad_proj, wbuf[1, 3 * D : 4 * D, :], 1, 1))
    spread_g = low(spread_heads(grad_mix[:8].astype(jnp.float32)))
    grad_qs = []
    for pair in range(pairs):
        rows = slice(pair * PAIR, (pair + 1) * PAIR)
        some_g, some_q = spread_g[32 * pair : 32 * pair + 32], spread_q[32 * pair : 32 * pair + 32]
        probs = class_probs[pair]
        grad_probs = dot(some_g, kv[rows, D : 2 * D], 1, 1)
        dqkv[rows, 2 * D : 3 * D] = low(dot(low(probs), some_g, 0, 0))
        grad_scores = probs * (grad_probs - jnp.sum(grad_probs * probs, -1, keepdims=True))
        grad_scores = low(grad_scores)
        grad_qs.append(dot(grad_scores, kv[rows, 0:D]))
        dqkv[rows, D : 2 * D] = low(dot(grad_scores, some_q, 0, 0) * HEAD ** (-0.5))
    grad_q = low(wide(unspread_heads(jnp.concatenate(grad_qs, axis=0)) * HEAD ** (-0.5), 16))

    def pack(first, second, at, width):
        factor_ref[:, at : at + width] = low(
            jnp.concatenate([first[:8].astype(jnp.float32), second[:8].astype(jnp.float32)], axis=0)
        )

    pack(grad_pre, class_act, 0, FF)
    pack(class_a, class_mix, FF, D)
    pack(grad_q, grad_proj, FF + D, D)
    pack(class_b, grad_b, FF + 2 * D, D)
    embed_wide = jnp.concatenate(
        [grad_embed.astype(jnp.float32), jnp.zeros((16, D - EMB), jnp.float32)], axis=1
    )
    pack(embed_wide, pooled, FF + 3 * D, D)

    started = [0]

    def push(slot, at):
        return pltpu.make_async_copy(stage.at[slot], g_hbm.at[pl.ds(at, D)], stage_sem.at[slot])

    def weight_grad(left, left_at, right, right_at, at, count):
        base = started[0]

        def one(block):
            slot = lax.rem(base + block, 2)

            @pl.when(base + block >= 2)
            def _():
                push(slot, at).wait()

            from_lane = pl.multiple_of(left_at + block * D, D) if count > 1 else left_at
            stage[slot] = low(dot(left[:, pl.ds(from_lane, D)], right[:, right_at : right_at + D], 0, 0))
            push(slot, pl.multiple_of(at + block * D, 16)).start()

        if count > 1:
            pl.loop(0, count)(one)
        else:
            one(0)
        started[0] = base + count

    def norm_back_rows(values, gain_row, grad, finish):
        gain = norm_row(gain_row)
        extra_ref[gain_row : gain_row + 2, :] = jnp.zeros((2, D), jnp.float32)

        @chunks_of()
        def _(index):
            rows = rows_at(index)
            grad_rows = grad[rows, :]
            result, terms = norm_back(values[rows, :], gain, grad_rows)
            at = slice(gain_row, gain_row + 1)
            extra_ref[at, :] = extra_ref[at, :] + jnp.sum(terms, 0, keepdims=True)
            at = slice(gain_row + 1, gain_row + 2)
            extra_ref[at, :] = extra_ref[at, :] + jnp.sum(grad_rows, 0, keepdims=True)
            finish(rows, result)

    weight_grad(norm_c, 0, dqkv, D, layer_at[1] + D, 1)
    weight_grad(norm_c, 0, dqkv, 2 * D, layer_at[1] + 2 * D, 1)
    acc[...] = dot(dqkv[:, D : 2 * D], wbuf[1, D : 2 * D, :], 1, 1)
    acc[...] = acc[...] + dot(dqkv[:, 2 * D : 3 * D], wbuf[1, 2 * D : 3 * D, :], 1, 1)
    add_class_rows(acc, dot(grad_q, wbuf[1, 0:D, :], 1, 1))
    fetch(9).start()

    def finish_second(rows, result):
        dhid[rows, :] = result

    norm_back_rows(hid1, 6, acc, finish_second)
    add_class_rows(dhid, grad_mid)

    gb[...] = low(dhid[...])
    fetch(7).wait()
    weight_grad(act, 0, gb, 0, layer_at[0] + 4 * D + FF, FF // D)

    @pl.loop(0, 3)
    def _(part):
        at = pl.ds(pl.multiple_of(part * 1024, 1024), 1024)
        grad_rows = dot(gb[...], wbuf[0, at, :], 1, 1)
        values = pre[:, at].astype(jnp.float32)
        gates = jax.nn.sigmoid(GELU_SLOPE * values)
        pre[:, at] = low(grad_rows * (gates + GELU_SLOPE * values * gates * (1.0 - gates)))

    weight_grad(pre, 0, norm_b, 0, layer_at[0] + 4 * D, FF // D)
    fetch(8).wait()
    acc[...] = dot(pre[...], wbuf[2])

    def finish_mid(rows, result):
        total = dhid[rows, :] + result
        dhid[rows, :] = total
        gb[rows, :] = low(total)

    norm_back_rows(mid0, 4, acc, finish_mid)
    weight_grad(mixed, 0, gb, 0, layer_at[0] + 3 * D, 1)
    fetch(9).wait()
    dmix[...] = low(dot(gb[...], wbuf[1, 3 * D : 4 * D, :], 1, 1))

    @pl.loop(0, pairs)
    def _(index):
        rows = rows_at(index)
        for group in range(3):
            queries = stack_heads(qkv[rows, lanes(0, group)])
            keys = qkv[rows, lanes(1, group)]
            probs = pair_soft(queries, keys)
            some_g = stack_heads(dmix[rows, lanes(0, group)])
            grad_probs = dot(some_g, qkv[rows, lanes(2, group)], 1, 1)
            dqkv[rows, lanes(2, group)] = low(dot(low(probs), some_g, 0, 0))
            grad_scores = probs * (grad_probs - jnp.sum(grad_probs * probs, -1, keepdims=True))
            grad_scores = low(grad_scores)
            grad_queries = fold_heads(dot(grad_scores, keys))
            dqkv[rows, lanes(0, group)] = low(grad_queries * HEAD ** (-0.5))
            grad_keys = dot(grad_scores, queries, 0, 0)
            dqkv[rows, lanes(1, group)] = low(grad_keys * HEAD ** (-0.5))

    for part in range(3):
        weight_grad(norm_a, 0, dqkv, part * D, layer_at[0] + part * D, 1)
    acc[...] = dot(dqkv[:, 0:D], wbuf[1, 0:D, :], 1, 1)
    for part in (1, 2):
        at = slice(part * D, (part + 1) * D)
        acc[...] = acc[...] + dot(dqkv[:, at], wbuf[1, at, :], 1, 1)

    def finish_first(rows, result):
        dhid[rows, :] = dhid[rows, :] + result

    norm_back_rows(hid0, 2, acc, finish_first)

    def finish_embedding(rows, result):
        dhid[rows, :] = result
        gb[rows, :] = low(result)

    norm_back_rows(emb, 0, dhid, finish_embedding)
    weight_grad(pix, 0, gb, 0, 0, PATCH_IN // D)
    grad_tokens = dhid[0:TOKENS, :]
    for i in range(1, images):
        grad_tokens = grad_tokens + dhid[TOKENS * i : TOKENS * (i + 1), :]
    class_grad = grad_tokens[CLASS_AT : CLASS_AT + 1]
    grad_tokens = jnp.concatenate(
        [grad_tokens, jnp.zeros((TABLE_ROWS - TOKENS, D), jnp.float32)], axis=0
    )
    grad_table = pltpu.roll(grad_tokens, 2, 0)
    row = lax.broadcasted_iota(jnp.int32, (TABLE_ROWS, D), 0)
    grad_table = jnp.where(row < 2, class_grad, jnp.where(row < SEQ + 1, grad_table, 0.0))
    table[...] = low(grad_table)
    put_table = pltpu.make_async_copy(table, g_hbm.at[pl.ds(BLOCK, TABLE_ROWS)], small_sem.at[0])
    put_table.start()
    put_table.wait()
    for slot in range(2):
        push(slot, 0).wait()


def image_notes(label_row, live_mask):
    notes = jnp.stack([label_row.astype(jnp.float32), live_mask], axis=1)
    return jnp.pad(notes, ((0, 8 - notes.shape[0]), (0, 126)))


def run_tower(weights, pixel_rows, notes, text, with_grads, carried=()):
    rows_all = pixel_rows.shape[0]
    images = rows_all // TOKENS
    bf16, f32 = jnp.bfloat16, jnp.float32
    scratch = [
        pltpu.VMEM((3, BLOCK, D), bf16),
        pltpu.VMEM((TAIL_ROWS, D), bf16),
        pltpu.VMEM((TABLE_ROWS, D), bf16),
        pltpu.VMEM((rows_all, PATCH_IN), bf16),
        pltpu.VMEM((rows_all, D), f32),
        pltpu.VMEM((rows_all, D), f32),
        pltpu.VMEM((rows_all, D), f32),
        pltpu.VMEM((rows_all, D), f32),
        pltpu.VMEM((rows_all, D), f32),
        pltpu.VMEM((rows_all, 3 * D), bf16),
        pltpu.VMEM((rows_all, D), bf16),
        pltpu.VMEM((rows_all, D), bf16),
        pltpu.VMEM((rows_all, D), bf16),
        pltpu.VMEM((rows_all if with_grads else 16, FF), bf16),
        pltpu.VMEM((rows_all, FF), bf16),
        pltpu.VMEM((rows_all, D), bf16),
        pltpu.VMEM((rows_all, 2 * D), bf16),
    ]
    if with_grads:
        scratch += [
            pltpu.VMEM((rows_all, D), f32),
            pltpu.VMEM((rows_all, 3 * D), bf16),
            pltpu.VMEM((rows_all, D), bf16),
            pltpu.VMEM((rows_all, D), bf16),
            pltpu.VMEM((2, D, D), bf16),
            pltpu.SemaphoreType.DMA((2,)),
        ]
        out_shape = (
            jax.ShapeDtypeStruct((grad_rows_kept(weights.shape[0]), D), bf16),
            jax.ShapeDtypeStruct((16, LOW_COLS), bf16),
            jax.ShapeDtypeStruct((16, D), f32),
        )
        out_specs = (
            pl.BlockSpec(memory_space=pl.ANY),
            pl.BlockSpec(memory_space=pltpu.VMEM),
            pl.BlockSpec(memory_space=pltpu.VMEM),
        )
    else:
        out_shape = (jax.ShapeDtypeStruct((8, 128), f32),)
        out_shape += tuple(jax.ShapeDtypeStruct(array.shape, array.dtype) for array in carried)
        out_specs = (pl.BlockSpec(memory_space=pltpu.VMEM),)
        out_specs += (pl.BlockSpec(memory_space=pl.ANY),) * len(carried)
        if carried:
            scratch += [
                pltpu.VMEM((4, carried[0].shape[0] // 6, carried[0].shape[1]), carried[0].dtype),
                pltpu.SemaphoreType.DMA((2, 4)),
            ]
    scratch += [pltpu.SemaphoreType.DMA((3,)), pltpu.SemaphoreType.DMA((3,))]
    vmem = pl.BlockSpec(memory_space=pltpu.VMEM)
    hbm = pl.BlockSpec(memory_space=pl.ANY)
    return pl.pallas_call(
        functools.partial(tower_kernel, images, with_grads, len(carried)),
        out_shape=out_shape,
        in_specs=[hbm, hbm, vmem, vmem] + [hbm] * len(carried),
        out_specs=out_specs,
        scratch_shapes=scratch,
        compiler_params=pltpu.CompilerParams(vmem_limit_bytes=(52 if with_grads else 40) * 2**20),
        cost_estimate=None
        if with_grads
        else pl.CostEstimate(
            flops=2 * rows_all * weights.shape[0] * D,
            bytes_accessed=2 * weights.shape[0] * D,
            transcendentals=rows_all * 2 * FF,
        ),
        name="train" if with_grads else "evaluate",
    )(weights, pixel_rows, text, notes, *carried)


def grad_rows_kept(rows):
    if not on_grid():
        return DENSE_END
    plane_rows = rows // 4
    return (DENSE_END + plane_rows - 1) // plane_rows * plane_rows


def on_grid():
    return lax.axis_size("group") == 4 and lax.axis_size("dp") == 8


def place():
    worker = lax.axis_index("group")
    rank = lax.axis_index("dp")
    return (worker // 2, worker % 2, rank // 2, rank % 2)


def device_at(y, c, z, x):
    return (y * 2 + c, z * 2 + x)


def chunk_rows(total, share):
    units = total // 16
    sizes = [3, 4] + [6] * ((units - 15) // 6) + [4, 4 + (units - 15) % 6]
    chunks = []
    start = taken = 0
    for size in sizes:
        first = int(round((start + size) * share)) - taken
        taken += first
        chunks.append((start * 16, first * 16, (size - first) * 16))
        start += size
    return chunks


def image_device():
    y, c, z, x = place()
    return device_at((z + c) % 2, z // 2, 2 * c + y, x)


def image_source():
    y, c, z, x = place()
    return device_at(z % 2, z // 2, 2 * c + (y + z // 2) % 2, x)


def gather_kernel(chunks, images, *refs):
    if images:
        (part_ref, pixel_ref, note_ref, full_ref, moved_ref, moved_note_ref), refs = refs[:6], refs[6:]
        (local_sem, sends, recvs, pixel_sems) = refs
        count = pixel_ref.shape[0] // TOKENS
        parcels = [(note_ref, moved_note_ref)]
        for index in range(count):
            rows = pl.ds(index * TOKENS, TOKENS)
            parcels.append((pixel_ref.at[rows], moved_ref.at[rows]))
    else:
        (part_ref, full_ref, local_sem, sends, recvs) = refs
    half_cols = part_ref.shape[1]
    y, c, z, x = place()
    cols = pl.ds(pl.multiple_of(c * half_cols, half_cols), half_cols)
    over_x = device_at(y, c, z, 1 - x)
    over_y = device_at(1 - y, c, z, x)
    sibling = device_at(y, 1 - c, z, x)
    along_z = [device_at(y, c, (z + step) % 4, x) for step in (1, 2, 3)]
    target = image_device()
    stays = jnp.logical_and(target[0] == y * 2 + c, target[1] == z * 2 + x)
    barrier = pltpu.get_barrier_semaphore()
    for other in [over_x, over_y, sibling] + along_z:
        pl.semaphore_signal(barrier, inc=1, device_id=other, device_id_type=MESH)
    if images:

        @pl.when(jnp.logical_not(stays))
        def _():
            pl.semaphore_signal(barrier, inc=1, device_id=image_source(), device_id_type=MESH)

    def keep(index):
        start, first, second = chunks[index]
        rows = pl.ds(start, first + second)
        return pltpu.make_async_copy(
            part_ref.at[rows], full_ref.at[z, x, y, rows, cols], local_sem.at[index]
        )

    for index in range(len(chunks)):
        keep(index).start()
    pl.semaphore_wait(barrier, 6 + (jnp.where(stays, 0, 1) if images else 0))

    def send(piece, other, stage, index):
        pltpu.make_async_remote_copy(
            src_ref=piece,
            dst_ref=piece,
            send_sem=sends.at[stage, index],
            recv_sem=recvs.at[stage, index],
            device_id=other,
            device_id_type=MESH,
        ).start()

    def move_parcel(which):
        source, place_at = parcels[which]

        @pl.when(stays)
        def _():
            pltpu.make_async_copy(source, place_at, pixel_sems.at[0, which]).start()

        @pl.when(jnp.logical_not(stays))
        def _():
            pltpu.make_async_remote_copy(
                src_ref=source,
                dst_ref=place_at,
                send_sem=pixel_sems.at[1, which],
                recv_sem=pixel_sems.at[0, which],
                device_id=target,
                device_id_type=MESH,
            ).start()

    def arrived(piece, stage, index):
        pltpu.make_async_copy(piece, piece, recvs.at[stage, index]).wait()

    def sent(piece, stage, index):
        pltpu.make_async_copy(piece, piece, sends.at[stage, index]).wait()

    def pieces(index):
        start, first, second = chunks[index]
        rows = pl.ds(start, first + second)
        rows_a = pl.ds(start, first)
        rows_b = pl.ds(start + first, second)
        return {
            0: full_ref.at[pl.ds(0, 3), 0, 0, rows, cols],
            1: full_ref.at[:, x, y, rows_a, cols],
            2: full_ref.at[:, x, y, rows_b, cols],
            3: full_ref.at[:, x, :, rows_a, cols],
            4: full_ref.at[:, :, y, rows_b, cols],
            5: full_ref.at[:, :, :, rows, cols],
        }

    total = len(chunks)

    def send_along_z(index):
        start, first, second = chunks[index]
        rows = pl.ds(start, first + second)
        for other in along_z:
            pltpu.make_async_remote_copy(
                src_ref=part_ref.at[rows],
                dst_ref=full_ref.at[z, x, y, rows, cols],
                send_sem=sends.at[0, index],
                recv_sem=recvs.at[0, index],
                device_id=other,
                device_id_type=MESH,
            ).start()

    ahead = LOOK_AHEAD if images else 1
    for step in range(total + 3):
        for index in range(ahead) if step == 0 else [step + ahead - 1]:
            if index < total:
                send_along_z(index)
        if images and step % PARCEL_STEP == 0 and step // PARCEL_STEP < len(parcels):
            move_parcel(step // PARCEL_STEP)
        index = step - 1
        if 0 <= index < total:
            block = pieces(index)
            arrived(block[0], 0, index)
            keep(index).wait()
            send(block[1], over_y, 1, index)
            send(block[2], over_x, 2, index)
        index = step - 2
        if 0 <= index < total:
            block = pieces(index)
            arrived(block[1], 1, index)
            send(block[3], over_x, 3, index)
            arrived(block[2], 2, index)
            send(block[4], over_y, 4, index)
        index = step - 3
        if 0 <= index < total:
            block = pieces(index)
            arrived(block[3], 3, index)
            arrived(block[4], 4, index)
            send(block[5], sibling, 5, index)
    for index in range(total):
        block = pieces(index)
        arrived(block[5], 5, index)
        for stage in range(6):
            sent(block[stage], stage, index)
    if images:
        for which, (_, place_at) in enumerate(parcels):
            pltpu.make_async_copy(place_at, place_at, pixel_sems.at[0, which]).wait()

        @pl.when(jnp.logical_not(stays))
        def _():
            for which, (_, place_at) in enumerate(parcels):
                pltpu.make_async_copy(place_at, place_at, pixel_sems.at[1, which]).wait()


def gather_rows(part, shard_rows, pixel_rows=None, notes=None):
    images = pixel_rows is not None
    chunks = chunk_rows(part.shape[0], FIRST_SHARE if images else 0.5)
    hbm = pl.BlockSpec(memory_space=pl.ANY)
    width = 2 * part.shape[1]
    full_shape = jax.ShapeDtypeStruct((4, 2, 2, part.shape[0], width), part.dtype)
    semaphores = [
        pltpu.SemaphoreType.DMA((len(chunks),)),
        pltpu.SemaphoreType.DMA((6, len(chunks))),
        pltpu.SemaphoreType.DMA((6, len(chunks))),
    ]
    kernel = functools.partial(gather_kernel, chunks, images)
    if not images:
        full = pl.pallas_call(
            kernel,
            out_shape=full_shape,
            in_specs=[hbm],
            out_specs=hbm,
            scratch_shapes=semaphores,
            compiler_params=pltpu.CompilerParams(collective_id=0, has_side_effects=True),
            name="gather",
        )(part)
        return full.reshape(8 * shard_rows, width)
    full, moved, moved_notes = pl.pallas_call(
        kernel,
        out_shape=(
            full_shape,
            jax.ShapeDtypeStruct(pixel_rows.shape, pixel_rows.dtype),
            jax.ShapeDtypeStruct(notes.shape, notes.dtype),
        ),
        in_specs=[hbm, hbm, hbm],
        out_specs=[hbm, hbm, hbm],
        scratch_shapes=semaphores
        + [pltpu.SemaphoreType.DMA((2, 1 + pixel_rows.shape[0] // TOKENS))],
        compiler_params=pltpu.CompilerParams(collective_id=2, has_side_effects=True),
        name="gather_first",
    )(part, pixel_rows, notes)
    return (full.reshape(8 * shard_rows, width), moved, moved_notes)


def reduce_kernel(
    chunks,
    low_from,
    grad_ref,
    factor_ref,
    extra_ref,
    own_ref,
    factors_ref,
    extras_ref,
    squares_ref,
    mine,
    first_sum,
    sum_a,
    sum_b,
    last_sum,
    squares,
    passed_factor,
    passed_extra,
    relay,
    load_sems,
    sends,
    recvs,
    small_sends,
    small_recvs,
    pass_sends,
    pass_recvs,
):
    half_cols = first_sum.shape[-1]
    planes = grad_ref.shape[0]
    y, c, z, x = place()
    home_y, home_c = z % 2, z // 2
    at_home = jnp.logical_and(home_y == y, home_c == c)
    from_plane = 2 * c + y
    my_cols = pl.ds(pl.multiple_of(c * half_cols, half_cols), half_cols)
    other_cols = pl.ds(pl.multiple_of((1 - c) * half_cols, half_cols), half_cols)
    over_x = device_at(y, c, z, 1 - x)
    over_y = device_at(1 - y, c, z, x)
    sibling = device_at(y, 1 - c, z, x)
    barrier = pltpu.get_barrier_semaphore()
    for other in (over_x, over_y, sibling):
        pl.semaphore_signal(barrier, inc=1, device_id=other, device_id_type=MESH)
    for other in range(8):
        other_y, other_c, other_x = other // 4, other // 2 % 2, other % 2
        same = jnp.logical_and(y == other_y, jnp.logical_and(c == other_c, x == other_x))
        itself = jnp.logical_and(at_home, same)

        @pl.when(jnp.logical_not(itself))
        def _():
            pl.semaphore_signal(
                barrier,
                inc=1,
                device_id=device_at(other_y, other_c, from_plane, other_x),
                device_id_type=MESH,
            )

    through_self = z // 2 == c
    for other in range(4):
        from_z = 2 * c + other // 2
        itself = jnp.logical_and(z == from_z, c == other % 2)

        @pl.when(jnp.logical_not(itself))
        def _():
            pl.semaphore_signal(
                barrier, inc=1, device_id=device_at(y, other % 2, from_z, x), device_id_type=MESH
            )

    def spans(index):
        start, first, second = chunks[index]
        start_a = sum(chunk[1] for chunk in chunks[:index])
        start_b = sum(chunk[2] for chunk in chunks[:index])
        return (
            pl.ds(start, first + second),
            pl.ds(start, first),
            pl.ds(start + first, second),
            pl.ds(start_a, first),
            pl.ds(start_b, second),
        )

    def send(source, target, other, stage, index):
        pltpu.make_async_remote_copy(
            src_ref=source,
            dst_ref=target,
            send_sem=sends.at[stage, index],
            recv_sem=recvs.at[stage, index],
            device_id=other,
            device_id_type=MESH,
        ).start()

    def arrived(piece, stage, index):
        pltpu.make_async_copy(piece, piece, recvs.at[stage, index]).wait()

    def sent(piece, stage, index):
        pltpu.make_async_copy(piece, piece, sends.at[stage, index]).wait()

    def load(index):
        rows = spans(index)[0]
        return pltpu.make_async_copy(
            grad_ref.at[:, :, :, rows],
            mine.at[index % 2, :, :, :, pl.ds(0, rows.size)],
            load_sems.at[index % 2],
        )

    def send_core(index):
        rows = spans(index)[0]
        send(
            grad_ref.at[:, :, :, rows, other_cols],
            first_sum.at[:, :, :, rows],
            sibling,
            0,
            index,
        )

    def own_rows(half, rows):
        return pl.ds(pl.multiple_of(half * grad_ref.shape[3] + rows.start, 16), rows.size)

    def add(target, source):
        summed = target[...].astype(jnp.float32) + source[...].astype(jnp.float32)
        target[...] = summed.astype(target.dtype)

    total = len(chunks)
    load(0).start()
    pl.semaphore_wait(barrier, 3 + jnp.where(at_home, 7, 8) + jnp.where(through_self, 3, 4))
    send_core(0)
    send_core(1)
    def slot_of(from_y):
        return (from_y * 2 + c) * 2 + x

    def to_owners(source, target, which, first_z, way):
        for other in range(2 * first_z, 8):
            other_z, other_x = other // 2, other % 2
            itself = jnp.logical_and(at_home, jnp.logical_and(z == other_z, x == other_x))

            @pl.when(jnp.logical_not(itself))
            def _():
                pltpu.make_async_remote_copy(
                    src_ref=source,
                    dst_ref=target,
                    send_sem=small_sends.at[way, which],
                    recv_sem=small_recvs.at[which],
                    device_id=device_at(home_y, home_c, other_z, other_x),
                    device_id_type=MESH,
                ).start()

            @pl.when(itself)
            def _():
                pltpu.make_async_copy(source, target, small_recvs.at[which]).start()

    def passing(which):
        source, target = ((extra_ref, passed_extra), (factor_ref, passed_factor))[which]
        return pltpu.make_async_remote_copy(
            src_ref=source,
            dst_ref=target,
            send_sem=pass_sends.at[which],
            recv_sem=pass_recvs.at[which],
            device_id=over_y,
            device_id_type=MESH,
        )

    gives = y != home_y

    @pl.when(gives)
    def _():
        for which in range(2):
            passing(which).start()

    @pl.when(jnp.logical_not(gives))
    def _():
        to_owners(extra_ref, extras_ref.at[slot_of(y)], 0, 0, 0)
        to_owners(factor_ref, factors_ref.at[slot_of(y)], 1, low_from, 0)

    def pass_on():
        @pl.when(jnp.logical_not(gives))
        def _():
            for which in range(2):
                passing(which).wait_recv()
            to_owners(passed_extra, extras_ref.at[slot_of(1 - y)], 0, 0, 1)
            to_owners(passed_factor, factors_ref.at[slot_of(1 - y)], 1, low_from, 1)

    squares[...] = jnp.zeros_like(squares)
    half_rows = grad_ref.shape[3]
    last_layer = FIRST_LAYER + 4 * D + 2 * FF

    def add_squares(block, rows):
        values = last_sum[block, rows].astype(jnp.float32)
        row = ((block * 2 + x) * 2 + y) * half_rows + rows.start
        row = row + lax.broadcasted_iota(jnp.int32, values.shape, 0)
        values = jnp.where(dense_row(row), values * values, 0.0)
        values = jnp.sum(values.reshape(rows.size // 8, 8, half_cols), axis=0)
        for part in range(half_cols // 128):
            squares[...] += values[:, part * 128 : (part + 1) * 128]

    for step in range(total + 2 + RELAY_LAG):
        index = step
        if index < total:
            if index + 1 < total:
                load(index + 1).start()
            if index + 2 < total:
                send_core(index + 2)
            rows, rows_a, rows_b, in_a, in_b = spans(index)
            load(index).wait()
            arrived(first_sum.at[:, :, :, rows], 0, index)

            @pl.loop(0, 4 * planes)
            def _(block):
                zz, rest = block // 4, block % 4
                add(
                    first_sum.at[zz, rest // 2, rest % 2, rows],
                    mine.at[index % 2, zz, rest // 2, rest % 2, pl.ds(0, rows.size), my_cols],
                )

            if index == 1:
                pass_on()
            send(first_sum.at[:, 1 - x, :, rows_a], sum_a.at[:, :, in_a], over_x, 1, index)
            send(first_sum.at[:, :, 1 - y, rows_b], sum_b.at[:, :, in_b], over_y, 2, index)
        index = step - 1
        if 0 <= index < total:
            rows, rows_a, rows_b, in_a, in_b = spans(index)
            arrived(sum_a.at[:, :, in_a], 1, index)

            @pl.loop(0, 2 * planes)
            def _(block):
                add(
                    sum_a.at[block // 2, block % 2, in_a],
                    first_sum.at[block // 2, x, block % 2, rows_a],
                )

            send(sum_a.at[:, 1 - y, in_a], last_sum.at[:, rows_a], over_y, 3, index)
            arrived(sum_b.at[:, :, in_b], 2, index)

            @pl.loop(0, 2 * planes)
            def _(block):
                add(
                    sum_b.at[block // 2, block % 2, in_b],
                    first_sum.at[block // 2, block % 2, y, rows_b],
                )

            send(sum_b.at[:, 1 - x, in_b], last_sum.at[:, rows_b], over_x, 4, index)
        index = step - 2
        if 0 <= index < total:
            rows, rows_a, rows_b, in_a, in_b = spans(index)
            arrived(last_sum.at[:, rows_a], 3, index)
            arrived(last_sum.at[:, rows_b], 4, index)

            @pl.loop(0, planes)
            def _(block):
                add(last_sum.at[block, rows_a], sum_a.at[block, y, in_a])
                add(last_sum.at[block, rows_b], sum_b.at[block, x, in_b])
                add_squares(block, rows)

            on_home_y = y == home_y
            for to_z in range(planes):
                itself = jnp.logical_and(through_self, z == to_z)
                source = last_sum.at[to_z, rows]
                for direct in (True, False):
                    chosen = on_home_y if direct else jnp.logical_not(on_home_y)
                    target = own_ref.at[own_rows(y, rows), my_cols] if direct else relay.at[rows, my_cols]
                    way = 5 if direct else 6

                    @pl.when(jnp.logical_and(chosen, jnp.logical_not(itself)))
                    def _():
                        pltpu.make_async_remote_copy(
                            src_ref=source,
                            dst_ref=target,
                            send_sem=sends.at[5, index],
                            recv_sem=recvs.at[way, index],
                            device_id=device_at(y, home_c, to_z, x),
                            device_id_type=MESH,
                        ).start()

                    @pl.when(jnp.logical_and(chosen, itself))
                    def _():
                        pltpu.make_async_copy(source, target, recvs.at[way, index]).start()

        index = step - 2 - RELAY_LAG
        if 0 <= index < total:
            rows = spans(index)[0]

            @pl.when(z < planes)
            def _():
                arrived(relay.at[rows], 6, index)
                send(relay.at[rows], own_ref.at[own_rows(y, rows)], over_y, 7, index)

    to_owners(squares, squares_ref.at[slot_of(y)], 2, 0, 0)
    for index in range(total):
        rows, rows_a, rows_b, in_a, in_b = spans(index)

        @pl.when(z < planes)
        def _():
            arrived(own_ref.at[pl.ds(0, rows.size)], 5, index)
            arrived(own_ref.at[pl.ds(0, rows.size)], 7, index)
            sent(relay.at[rows], 7, index)

        sent(first_sum.at[:, :, :, rows], 0, index)
        sent(sum_a.at[:, :, in_a], 1, index)
        sent(sum_b.at[:, :, in_b], 2, index)
        sent(last_sum.at[:, rows_a], 3, index)
        sent(last_sum.at[:, rows_b], 4, index)

        kept = jnp.logical_and(through_self, z < planes)

        @pl.when(kept)
        def _():
            sent(last_sum.at[pl.ds(0, planes - 1), rows], 5, index)

        @pl.when(jnp.logical_not(kept))
        def _():
            sent(last_sum.at[:, rows], 5, index)

    def all_of(ref, count, sem):
        piece = ref.at[pl.ds(0, count)]
        pltpu.make_async_copy(piece, piece, sem).wait()

    all_of(extras_ref, 8, small_recvs.at[0])
    all_of(squares_ref, 8, small_recvs.at[2])

    @pl.when(z >= low_from)
    def _():
        all_of(factors_ref, 8, small_recvs.at[1])

    def sent_to_owners(ref, count, kept, which, way):
        @pl.when(kept)
        def _():
            all_of(ref, count - 1, small_sends.at[way, which])

        @pl.when(jnp.logical_not(kept))
        def _():
            all_of(ref, count, small_sends.at[way, which])

    sent_to_owners(squares_ref, 8, at_home, 2, 0)

    @pl.when(gives)
    def _():
        for which in range(2):
            passing(which).wait_send()

    @pl.when(jnp.logical_not(gives))
    def _():
        low_kept = jnp.logical_and(at_home, z >= low_from)
        for way in range(2):
            sent_to_owners(extras_ref, 8, at_home, 0, way)
            sent_to_owners(factors_ref, 2 * (4 - low_from), low_kept, 1, way)


def reduce_chunks(total, share):
    units = total // 16
    middle = units - sum(REDUCE_HEAD + REDUCE_TAIL)
    sizes = [8] * (middle // 8)
    sizes[-1] += middle % 8
    sizes = REDUCE_HEAD + sizes + REDUCE_TAIL
    chunks = []
    start = taken = 0
    for size in sizes:
        first = int(round((start + size) * share)) - taken
        taken += first
        chunks.append((start * 16, first * 16, (size - first) * 16))
        start += size
    return chunks


def low_plane(shard_rows):
    return (FIRST_LAYER + 4 * D + 2 * FF) // (2 * shard_rows)


def sum_on_plane(grad_rows, factors, extra, shard_rows):
    half_rows, width = shard_rows // 2, grad_rows.shape[1]
    planes = grad_rows.shape[0] // (2 * shard_rows)
    chunks = reduce_chunks(half_rows, 0.75)
    most = max(first + second for _, first, second in chunks)
    half_cols = width // 2
    dtype = grad_rows.dtype
    return pl.pallas_call(
        functools.partial(reduce_kernel, chunks, low_plane(shard_rows)),
        out_shape=(
            jax.ShapeDtypeStruct((shard_rows + 16, width), dtype),
            jax.ShapeDtypeStruct((8,) + factors.shape, factors.dtype),
            jax.ShapeDtypeStruct((8,) + extra.shape, extra.dtype),
            jax.ShapeDtypeStruct((8, 8, 128), jnp.float32),
        ),
        in_specs=[pl.BlockSpec(memory_space=pl.ANY)] * 3,
        out_specs=[pl.BlockSpec(memory_space=pl.ANY)] * 4,
        scratch_shapes=[
            pltpu.VMEM((2, planes, 2, 2, most, width), dtype),
            pltpu.VMEM((planes, 2, 2, half_rows, half_cols), dtype),
            pltpu.VMEM((planes, 2, sum(chunk[1] for chunk in chunks), half_cols), dtype),
            pltpu.VMEM((planes, 2, sum(chunk[2] for chunk in chunks), half_cols), dtype),
            pltpu.VMEM((planes, half_rows, half_cols), dtype),
            pltpu.VMEM((8, 128), jnp.float32),
            pltpu.VMEM(factors.shape, factors.dtype),
            pltpu.VMEM(extra.shape, extra.dtype),
            pltpu.VMEM((half_rows, width), dtype),
            pltpu.SemaphoreType.DMA((2,)),
            pltpu.SemaphoreType.DMA((8, len(chunks))),
            pltpu.SemaphoreType.DMA((8, len(chunks))),
            pltpu.SemaphoreType.DMA((2, 3)),
            pltpu.SemaphoreType.DMA((3,)),
            pltpu.SemaphoreType.DMA((2,)),
            pltpu.SemaphoreType.DMA((2,)),
        ],
        compiler_params=pltpu.CompilerParams(
            collective_id=1, has_side_effects=True, vmem_limit_bytes=56 * 2**20
        ),
        name="reduce",
    )(grad_rows.reshape(planes, 2, 2, half_rows, width), factors, extra)


def update_kernel(
    shape,
    own_hbm,
    rest_hbm,
    master_hbm,
    first_hbm,
    second_hbm,
    factors_ref,
    extras_ref,
    squares_ref,
    first_out,
    second_out,
    total_out,
    summary_ref,
    own,
    rest,
    weights,
    first,
    second,
    new_first,
    new_second,
    mine,
    other,
    core_in,
    y_out,
    y_in,
    load_sems,
    store_sems,
    sends,
    recvs,
    total_sem,
    low_squares_ref,
    low_sems,
):
    half_rows, piece, pieces, low_from = shape
    half_cols = mine.shape[-1]
    y, c, z, x = place()
    over_y = device_at(1 - y, c, z, x)
    sibling = device_at(y, 1 - c, z, x)
    barrier = pltpu.get_barrier_semaphore()
    for partner in (over_y, sibling):
        pl.semaphore_signal(barrier, inc=1, device_id=partner, device_id_type=MESH)
    has_factors = z >= low_from

    @pl.when(z < 4 - low_from)
    def _():
        pl.semaphore_signal(
            barrier, inc=1, device_id=device_at(y, c, z + low_from, x), device_id_type=MESH
        )

    def row_at(index):
        half = jnp.where(index < pieces, 1 - y, y)
        return pl.multiple_of(half * half_rows + index % pieces * piece, 16)

    def loads(index):
        slot = index % 2
        rows = pl.ds(row_at(index), piece)
        longer = pl.ds(row_at(index), piece + 16)
        return [
            pltpu.make_async_copy(own_hbm.at[longer], own.at[slot], load_sems.at[0, slot]),
            pltpu.make_async_copy(rest_hbm.at[rows], rest.at[slot], load_sems.at[1, slot]),
            pltpu.make_async_copy(master_hbm.at[rows], weights.at[slot], load_sems.at[2, slot]),
            pltpu.make_async_copy(first_hbm.at[rows], first.at[slot], load_sems.at[3, slot]),
            pltpu.make_async_copy(second_hbm.at[rows], second.at[slot], load_sems.at[4, slot]),
        ]

    def stores(index):
        slot = index % 2
        rows = pl.ds(row_at(index), piece)
        return [
            pltpu.make_async_copy(new_first.at[slot], first_out.at[rows], store_sems.at[0, slot]),
            pltpu.make_async_copy(new_second.at[slot], second_out.at[rows], store_sems.at[1, slot]),
        ]

    for copy in loads(0):
        copy.start()

    def gram(at, width):
        values = factors_ref[:, :, at : at + width].reshape(128, width)
        return dot(values, values, 1, 1)

    row = lax.broadcasted_iota(jnp.int32, (128, 128), 0) % 16
    col = lax.broadcasted_iota(jnp.int32, (128, 128), 1) % 16
    head = gram(FF + 3 * D, D)
    shifted_head = pltpu.roll(pltpu.roll(head, 120, 0), 120, 1)
    products = gram(0, FF) * gram(FF + 2 * D, D) + gram(FF, D) * gram(FF + D, D)
    low_squares = jnp.where(row // 8 == col // 8, products, 0.0)
    low_squares = low_squares + jnp.where((row < 8) & (col < 8), head * shifted_head, 0.0)
    pl.semaphore_wait(barrier, 2 + jnp.where(has_factors, 1, 0))
    to_low = pltpu.make_async_remote_copy(
        src_ref=low_squares_ref,
        dst_ref=low_squares_ref,
        send_sem=low_sems.at[0],
        recv_sem=low_sems.at[1],
        device_id=device_at(y, c, z - low_from, x),
        device_id_type=MESH,
    )

    @pl.when(has_factors)
    def _():
        low_squares_ref[...] = jnp.sum(low_squares.reshape(16, 8, 128), axis=0)
        to_low.start()

    @pl.when(jnp.logical_not(has_factors))
    def _():
        to_low.wait_recv()

    extra = jnp.sum(extras_ref[...], axis=0)
    norm_squares = extra[:HEAD_AT] * extra[:HEAD_AT]
    square_all = jnp.sum(squares_ref[...]) + jnp.sum(low_squares_ref[...]) + jnp.sum(norm_squares)
    count_all = extra[12:13, 1:2]
    grad_norm = jnp.sqrt(jnp.zeros((1, 1), jnp.float32) + square_all) / count_all
    factor = CLIP_MAX / jnp.maximum(grad_norm, CLIP_MAX) / count_all
    summary_ref[...] = extra
    summary_ref[10:12, :] = extra[10:12] * factor
    summary_ref[13:14, :] = jnp.broadcast_to(grad_norm, (1, D))

    flat_start = (z * 2 + x) * (2 * half_rows)
    layer_start = BLOCK + SEQ + 1

    def step(index):
        slot = index % 2
        for copy in loads(index):
            copy.wait()

        @pl.loop(0, piece // 16)
        def _(block):
            at = pl.multiple_of(block * 16, 16)
            rows = pl.ds(at, 16)
            longer = own[slot, pl.ds(at, 32), :].astype(jnp.float32)
            flat = flat_start + row_at(index) + at + lax.broadcasted_iota(jnp.int32, (16, D), 0)
            grads = jnp.where(flat < layer_start, longer[:16], longer[SPARE : SPARE + 16])
            spared = jnp.where(flat < layer_start, flat, flat + SPARE)
            grads = jnp.where(dense_row(spared), grads, rest[slot, rows, :].astype(jnp.float32))
            clipped = grads * factor
            moment_one = BETA_ONE * first[slot, rows, :] + (1.0 - BETA_ONE) * clipped
            moment_two = BETA_TWO * second[slot, rows, :] + (1.0 - BETA_TWO) * clipped * clipped
            new_first[slot, rows, :] = moment_one
            new_second[slot, rows, :] = moment_two
            corrected_one = moment_one * (1.0 / (1.0 - BETA_ONE**STEP))
            corrected_two = moment_two * (1.0 / (1.0 - BETA_TWO**STEP))
            change = corrected_one / (jnp.sqrt(corrected_two) + ADAM_EPS) + DECAY * weights[slot, rows, :]
            change = low(RATE * change)
            left, right = change[:, :half_cols], change[:, half_cols:]
            mine[index, rows, :] = jnp.where(c == 0, left, right)
            other[index, rows, :] = jnp.where(c == 0, right, left)

        for copy in stores(index):
            copy.start()
        pltpu.make_async_remote_copy(
            src_ref=other.at[index],
            dst_ref=core_in.at[index],
            send_sem=sends.at[index],
            recv_sem=recvs.at[index],
            device_id=sibling,
            device_id_type=MESH,
        ).start()

    def fold(index):
        pltpu.make_async_copy(core_in.at[index], core_in.at[index], recvs.at[index]).wait()
        total = mine[index].astype(jnp.float32) + core_in[index].astype(jnp.float32)
        if index < pieces:
            y_out[index] = low(total)
            pltpu.make_async_remote_copy(
                src_ref=y_out.at[index],
                dst_ref=y_in.at[index],
                send_sem=sends.at[2 * pieces + index],
                recv_sem=recvs.at[2 * pieces + index],
                device_id=over_y,
                device_id_type=MESH,
            ).start()
        else:
            mine[index] = low(total)

    steps = 2 * pieces
    for index in range(steps):
        if index + 1 < steps:
            if index >= 1:
                for copy in stores(index - 1):
                    copy.wait()
            for copy in loads(index + 1):
                copy.start()
        step(index)
        if index >= 1:
            fold(index - 1)
    fold(steps - 1)

    def hand_over(index):
        rows = pl.ds(index * piece, piece)
        return pltpu.make_async_copy(mine.at[pieces + index], total_out.at[rows], total_sem.at[index])

    for index in range(pieces):
        at = 2 * pieces + index
        pltpu.make_async_copy(y_in.at[index], y_in.at[index], recvs.at[at]).wait()
        total = mine[pieces + index].astype(jnp.float32) + y_in[index].astype(jnp.float32)
        mine[pieces + index] = low(total)
        hand_over(index).start()
    for index in range(steps - 2, steps):
        for copy in stores(index):
            copy.wait()
    for index in range(steps):
        pltpu.make_async_copy(other.at[index], other.at[index], sends.at[index]).wait()
    for index in range(pieces):
        pltpu.make_async_copy(y_out.at[index], y_out.at[index], sends.at[steps + index]).wait()
        hand_over(index).wait()

    @pl.when(has_factors)
    def _():
        to_low.wait_send()


def update_rows(own, rest, master, first, second, factors, extras, squares):
    rows, width = master.shape
    half_rows, half_cols = rows // 2, width // 2
    pieces = 3
    piece = half_rows // pieces
    f32, bf16 = jnp.float32, jnp.bfloat16
    hbm = pl.BlockSpec(memory_space=pl.ANY)
    vmem = pl.BlockSpec(memory_space=pltpu.VMEM)
    return pl.pallas_call(
        functools.partial(update_kernel, (half_rows, piece, pieces, low_plane(rows))),
        out_shape=(
            jax.ShapeDtypeStruct((rows, width), f32),
            jax.ShapeDtypeStruct((rows, width), f32),
            jax.ShapeDtypeStruct((half_rows, half_cols), bf16),
            jax.ShapeDtypeStruct((16, width), f32),
        ),
        in_specs=[hbm] * 5 + [vmem] * 3,
        out_specs=[hbm] * 3 + [vmem],
        scratch_shapes=[
            pltpu.VMEM((2, piece + 16, width), bf16),
            pltpu.VMEM((2, piece, width), bf16),
            pltpu.VMEM((2, piece, width), f32),
            pltpu.VMEM((2, piece, width), f32),
            pltpu.VMEM((2, piece, width), f32),
            pltpu.VMEM((2, piece, width), f32),
            pltpu.VMEM((2, piece, width), f32),
            pltpu.VMEM((2 * pieces, piece, half_cols), bf16),
            pltpu.VMEM((2 * pieces, piece, half_cols), bf16),
            pltpu.VMEM((2 * pieces, piece, half_cols), bf16),
            pltpu.VMEM((pieces, piece, half_cols), bf16),
            pltpu.VMEM((pieces, piece, half_cols), bf16),
            pltpu.SemaphoreType.DMA((5, 2)),
            pltpu.SemaphoreType.DMA((2, 2)),
            pltpu.SemaphoreType.DMA((3 * pieces,)),
            pltpu.SemaphoreType.DMA((3 * pieces,)),
            pltpu.SemaphoreType.DMA((pieces,)),
            pltpu.VMEM((8, 128), f32),
            pltpu.SemaphoreType.DMA((2,)),
        ],
        compiler_params=pltpu.CompilerParams(
            collective_id=3, has_side_effects=True, vmem_limit_bytes=48 * 2**20
        ),
        name="update",
    )(own, rest, master, first, second, factors, extras, squares)


def pairs_of(partner):
    pairs = []
    for source in range(32):
        y, c, z, x = source // 16, source // 8 % 2, source // 2 % 4, source % 2
        target = partner(y, c, z, x)
        if target is not None:
            pairs.append((source, (target[0] * 2 + target[1]) * 8 + target[2] * 2 + target[3]))
    return pairs


def next_half(y, c, z, x):
    place_in_row = (z * 2 + x) * 2 + y + 1
    if place_in_row == 16:
        return None
    return (place_in_row % 2, c, place_in_row // 4, place_in_row // 2 % 2)


def on_grid_step(grad_rows, factors, extra, master, outer_momentum, first, second):
    rows, width = master.shape
    half_rows, half_cols = rows // 2, width // 2
    y, c, z, x = place()
    rank = lax.axis_index("dp")
    own, factors, extras, squares = sum_on_plane(grad_rows, factors, extra, rows)
    following = lax.ppermute(own[:16], "dp", [(source, source - 1) for source in range(1, 8)])
    own = lax.dynamic_update_slice(own, following, (rows, 0))
    rest = low_rank_rows(factors, jnp.sum(extras, axis=0), rank * rows + SPARE, rows)
    first, second, total, summary = update_rows(
        own, rest.astype(jnp.bfloat16), master, first, second, factors, extras, squares
    )
    groups = lax.axis_size("group")
    at = (y * half_rows, c * half_cols)
    quarter = [lax.dynamic_slice(whole, at, (half_rows, half_cols)) for whole in (master, outer_momentum)]
    part, _ = nesterov(*quarter, total.astype(jnp.float32) / groups)
    before = lax.ppermute(part[-16:], ("group", "dp"), pairs_of(next_half))
    moved = jnp.concatenate([before, part], axis=0)[16 - SPARE :][:half_rows]
    flat_row = rank * rows + y * half_rows + lax.broadcasted_iota(jnp.int32, (half_rows, 1), 0)
    part = jnp.where(flat_row < layout_rows()[1], part, moved).astype(jnp.bfloat16)
    soup_rows = gather_rows(part, rows)
    total, soup_rows = lax.optimization_barrier((total, soup_rows))
    over_y = lax.ppermute(total, ("group", "dp"), pairs_of(lambda y, c, z, x: (1 - y, c, z, x)))

    def finish(over_y):
        column = jnp.where(y == 0, jnp.stack([total, over_y]), jnp.stack([over_y, total]))
        column = column.reshape(rows, half_cols)
        sibling = lax.ppermute(
            column, ("group", "dp"), pairs_of(lambda y, c, z, x: (y, 1 - c, z, x))
        )
        whole = jnp.where(
            c == 0,
            jnp.concatenate([column, sibling], axis=1),
            jnp.concatenate([sibling, column], axis=1),
        )
        return nesterov(master, outer_momentum, whole.astype(jnp.float32) / groups)

    return (over_y, finish, first, second, summary, soup_rows)


def fetch_weights(params, pixel_rows=None, notes=None):
    rows, width = params.shape
    ranks, rank = lax.axis_size("dp"), lax.axis_index("dp")
    before = lax.ppermute(params[-16:], "dp", [(source, source + 1) for source in range(ranks - 1)])
    longer = jnp.concatenate([before, params], axis=0)
    in_place = lax.broadcasted_iota(jnp.int32, (rows, 1), 0) + rank * rows < layout_rows()[1]
    if not on_grid():
        moved = jnp.where(in_place, params, longer[16 - SPARE :][:rows])
        full = lax.all_gather(moved.astype(jnp.bfloat16), "dp", axis=0, tiled=True)
        return full if pixel_rows is None else (full, pixel_rows, notes)
    y, c, _, _ = place()
    half, half_cols = rows // 2, width // 2
    part = lax.dynamic_slice(params, (y * half, c * half_cols), (half, half_cols))
    moved = lax.dynamic_slice(longer, (y * half + 16 - SPARE, c * half_cols), (half, half_cols))
    in_place = lax.dynamic_slice(in_place, (y * half, 0), (half, 1))
    return gather_rows(jnp.where(in_place, part, moved).astype(jnp.bfloat16), rows, pixel_rows, notes)


def low_rank_rows(factors, extra, first_row, count):
    last_layer = FIRST_LAYER + 4 * D + 2 * FF
    devices = factors.shape[0]

    def half(at, width, which):
        piece = factors[:, 8 * which : 8 * which + 8, at : at + width]
        return piece.reshape(devices * 8, width)

    norms = extra[:16].astype(jnp.bfloat16)
    sections = [
        (last_layer, half(FF, D, 0), half(FF + D, D, 0)),
        (last_layer + 3 * D, half(FF, D, 1), half(FF + D, D, 1)),
        (last_layer + 4 * D, half(0, FF, 0), half(FF + 2 * D, D, 0)),
        (last_layer + 4 * D + FF, half(0, FF, 1), half(FF + 2 * D, D, 1)),
        (TAIL_START, jnp.eye(16, HEAD_AT, dtype=jnp.bfloat16), norms),
        (TAIL_START + HEAD_AT, half(FF + 3 * D, EMB, 0), half(FF + 3 * D, D, 1)),
    ]
    row = first_row + jnp.arange(count)
    lefts, rights = [], []
    for start, left, right in sections:
        width = left.shape[1]
        padded = jnp.pad(left, ((0, 0), (count, count)))
        at = jnp.clip(first_row - start + count, 0, width + count)
        window = lax.dynamic_slice(padded, (0, at), (left.shape[0], count))
        inside = (row >= start) & (row < start + width)
        lefts.append(jnp.where(inside[None], window, jnp.zeros_like(window)))
        rights.append(right)
    return lax.dot_general(
        jnp.concatenate(lefts, axis=0),
        jnp.concatenate(rights, axis=0),
        (((0,), (0,)), ((), ())),
        preferred_element_type=jnp.float32,
    )


def reduce_rows(grad_rows, factors, extra, count):
    ranks, rank = lax.axis_size("dp"), lax.axis_index("dp")
    flat_row = rank * count + lax.broadcasted_iota(jnp.int32, (count, 1), 0)
    rest = low_rank_rows(factors[None], extra, 0, ranks * count).astype(jnp.bfloat16)
    whole = jnp.where(dense_row(jnp.arange(DENSE_END))[:, None], grad_rows, rest[:DENSE_END])
    whole = jnp.concatenate([whole, rest[DENSE_END:]], axis=0)
    shard = lax.psum_scatter(whole, "dp", scatter_dimension=0, tiled=True)
    following = lax.ppermute(shard[:16], "dp", [(source, source - 1) for source in range(1, ranks)])
    shifted = jnp.concatenate([shard[SPARE:], following[:SPARE]], axis=0)
    summed = jnp.where(flat_row < layout_rows()[1], shard, shifted).astype(jnp.float32)
    return (summed, lax.psum(extra, "dp"))


def any_grid_step(grad_rows, factors, extra, master, outer_momentum, first, second):
    reduced, extra = reduce_rows(grad_rows, factors, extra, master.shape[0])
    count_all = extra[12, 1]
    grad_norm = jnp.sqrt(lax.psum(jnp.sum(reduced * reduced), "dp")) / count_all
    factor = CLIP_MAX / jnp.maximum(grad_norm, CLIP_MAX) / count_all
    params, first, second = adam_update(master, first, second, reduced * factor, STEP)
    delta = (master - params).astype(jnp.bfloat16)
    mean_delta = lax.psum(delta, "group").astype(jnp.float32) / lax.axis_size("group")
    outer = nesterov(master, outer_momentum, mean_delta)
    summary = jnp.concatenate(
        [extra[:10], extra[10:12] * factor, extra[12:13], jnp.full((3, D), grad_norm)], axis=0
    )
    return (outer, lambda done: done, first, second, summary, fetch_weights(outer[0]))


def dense_row(row):
    last_layer = FIRST_LAYER + 4 * D + 2 * FF
    return (row < last_layer) | ((row >= last_layer + D) & (row < DENSE_END))


def adam_update(params, moment_one, moment_two, clipped, step_number):
    moment_one = BETA_ONE * moment_one + (1.0 - BETA_ONE) * clipped
    moment_two = BETA_TWO * moment_two + (1.0 - BETA_TWO) * clipped * clipped
    corrected_one = moment_one / (1.0 - BETA_ONE**step_number)
    corrected_two = moment_two / (1.0 - BETA_TWO**step_number)
    params = params - RATE * (corrected_one / (jnp.sqrt(corrected_two) + ADAM_EPS) + DECAY * params)
    return (params, moment_one, moment_two)


def nesterov(master_rows, momentum_rows, mean_delta):
    momentum_next = OUTER_MOM * momentum_rows + mean_delta
    return (master_rows - OUTER_RATE * (mean_delta + OUTER_MOM * momentum_next), momentum_next)


def token_rows(pixel_block):
    images, patches, _ = pixel_block.shape
    padded = jnp.pad(pixel_block, ((0, 0), (0, TOKENS - patches), (0, 0)))
    return padded.reshape(images * TOKENS, PATCH_IN)


def per_device(
    pixels,
    counts,
    labels,
    text,
    master,
    outer_momentum,
    first_moment,
    second_moment,
    eval_pixels,
    eval_counts,
    eval_labels,
):
    slots = pixels.shape[2]
    live = (jnp.arange(slots)[None, :] < counts[0]).astype(jnp.float32).reshape(-1)
    step_labels = labels[0].reshape(-1)
    step_pixels = token_rows(pixels[0].reshape((-1,) + pixels.shape[3:]))
    notes = image_notes(step_labels, live)
    weights, step_pixels, notes = fetch_weights(master, step_pixels, notes)
    grad_rows, factors, extra = run_tower(weights, step_pixels, notes, text, True)
    step = on_grid_step if on_grid() else any_grid_step
    waiting, finish, moment_one, moment_two, summary, soup_rows = step(
        grad_rows, factors, extra, master, outer_momentum, first_moment[0], second_moment[0]
    )
    eval_live = (jnp.arange(eval_pixels.shape[0]) < eval_counts[0]).astype(jnp.float32)
    eval_notes = image_notes(eval_labels, eval_live)
    carried = (moment_one, moment_two) if on_grid() else ()
    eval_tile, *carried = run_tower(
        soup_rows, token_rows(eval_pixels), eval_notes, text, False, carried
    )
    if on_grid():
        moment_one, moment_two = carried
    eval_tile, waiting = lax.optimization_barrier((eval_tile, waiting))
    new_master, new_outer = finish(waiting)
    eval_losses = eval_tile[: eval_labels.shape[0], 0]
    return (
        new_master,
        new_outer,
        moment_one[None],
        moment_two[None],
        summary[13:14, :1],
        summary[12:13, :1],
        summary[12:13, 1:2],
        summary[10:12][None, None],
        eval_losses,
    )


def solution(mesh):
    return jax.shard_map(
        per_device,
        mesh=mesh,
        in_specs=(
            P(None, None, ("group", "dp"), None, None),
            P(None, None, ("group", "dp")),
            P(None, None, ("group", "dp")),
            P(),
            P("dp", None),
            P("dp", None),
            P("group", "dp", None),
            P("group", "dp", None),
            P(("group", "dp"), None, None),
            P(("group", "dp")),
            P(("group", "dp")),
        ),
        out_specs=(
            P("dp", None),
            P("dp", None),
            P("group", "dp", None),
            P("group", "dp", None),
            P("group", None),
            P("group", None),
            P("group", None),
            P("group", None, None, None),
            P(("group", "dp")),
        ),
        check_vma=False,
    )
```

```python
import functools

import jax
import jax.numpy as jnp
from jax import lax
from jax.experimental import pallas as pl
from jax.experimental.pallas import tpu as pltpu
from jax.sharding import PartitionSpec as P

MESH = pl.DeviceIdType.MESH

D = 768
HEADS = 12
HEAD = 64
FF = 3072
PATCH_IN = 3072
EMB = 512
CLASSES = 1000
LAYERS = 2
MICRO = 2
STEP = 10
SEQ = 50
ROWS_RAW = 22079


LN_EPS = 1e-05
NORM_EPS = 1e-06
LOGIT_SCALE = 50.0
SMOOTH = 0.1
CLIP_MAX = 0.02
BETA_ONE = 0.9
BETA_TWO = 0.98
ADAM_EPS = 1e-08
RATE = 0.02
DECAY = 0.1
OUTER_RATE = 0.7
OUTER_MOM = 0.9
GELU_SLOPE = 1.702
SPARE = 13
FIRST_SHARE = 0.6
LOOK_AHEAD = 3
PARCEL_STEP = 1
REDUCE_HEAD = [4, 6]
RELAY_LAG = 1
REDUCE_TAIL = [4]


def layout_rows():
    table_start = PATCH_IN
    layer_start = table_start + SEQ + 1
    block_size = 4 * D + 2 * FF
    norm_start = layer_start + LAYERS * block_size
    head_start = norm_start + 4 * LAYERS + 4
    return (table_start, layer_start, block_size, norm_start, head_start)


TOKENS = 56
CLASS_AT = 49
PAIR = 2 * TOKENS
BLOCK = 3072
TAIL_START = BLOCK + SEQ + 1 + SPARE + LAYERS * (4 * D + 2 * FF)
TAIL_ROWS = 544
HEAD_AT = 4 * LAYERS + 4
TABLE_ROWS = SEQ + 1 + SPARE
LOW_COLS = 2 * FF
FIRST_LAYER = BLOCK + TABLE_ROWS
DENSE_END = FIRST_LAYER + 4 * D + 2 * FF + 3 * D


def dot(first, second, first_dim=1, second_dim=0):
    return lax.dot_general(
        first,
        second,
        (((first_dim,), (second_dim,)), ((), ())),
        preferred_element_type=jnp.float32,
    )


def low(values):
    return values.astype(jnp.bfloat16)


def norm_parts(values):
    centred = values - jnp.mean(values, -1, keepdims=True)
    scale = lax.rsqrt(jnp.mean(centred * centred, -1, keepdims=True) + LN_EPS)
    return (centred * scale, scale)


def norm_back(values, gain, grad):
    unit, scale = norm_parts(values)
    weighted = grad * gain
    mean_one = jnp.mean(weighted, -1, keepdims=True)
    mean_two = jnp.mean(weighted * unit, -1, keepdims=True)
    return (scale * (weighted - mean_one - unit * mean_two), grad * unit)


def wide(values, rows):
    return jnp.concatenate(
        [values, jnp.zeros((rows - values.shape[0], values.shape[1]), values.dtype)], axis=0
    )


def head_mask(rows, lanes, first_head):
    row = lax.broadcasted_iota(jnp.int32, (rows, lanes), 0)
    lane = lax.broadcasted_iota(jnp.int32, (rows, lanes), 1)
    return (lane // HEAD + first_head) == row


def lane_pick(values, head):
    lane = lax.broadcasted_iota(jnp.int32, values.shape, 1)
    return jnp.where(lane // HEAD == head, values, jnp.zeros_like(values))


def stack_heads(values):
    return jnp.concatenate([lane_pick(values, head) for head in range(4)], axis=0)


def fold_heads(values):
    rows = values.shape[0] // 4
    total = lane_pick(values[:rows], 0)
    for head in range(1, 4):
        total = total + lane_pick(values[head * rows : (head + 1) * rows], head)
    return total


def soft(scores):
    scores = scores - jnp.max(scores, -1, keepdims=True)
    grown = jnp.exp(scores)
    return grown / jnp.sum(grown, -1, keepdims=True)


def pair_bias():
    row = lax.broadcasted_iota(jnp.int32, (PAIR, PAIR), 0)
    col = lax.broadcasted_iota(jnp.int32, (PAIR, PAIR), 1)
    fits = (row // TOKENS == col // TOKENS) & (col % TOKENS < SEQ)
    return jnp.where(fits, 0.0, -1e30)


def class_bias():
    row = lax.broadcasted_iota(jnp.int32, (32, PAIR), 0)
    col = lax.broadcasted_iota(jnp.int32, (32, PAIR), 1)
    fits = (row // 16 == col // TOKENS) & (col % TOKENS < SEQ)
    return jnp.where(fits, 0.0, -1e30)


def spread_heads(values):
    keep = head_mask(16, D, 0)
    rows = jnp.broadcast_to(values[:, None, :], (8, 16, D))
    return jnp.where(keep[None], rows, 0.0).reshape(128, D)


def unspread_heads(values):
    keep = head_mask(16, D, 0)
    return jnp.sum(jnp.where(keep[None], values.reshape(8, 16, D), 0.0), axis=1)


def tower_kernel(images, with_grads, carry, *refs):
    rows_all = images * TOKENS
    pairs = images // 2
    (w_hbm, pix_hbm, text_ref, note_ref), refs = refs[:4], refs[4:]
    if with_grads:
        (g_hbm, factor_ref, extra_ref), refs = refs[:3], refs[3:]
    else:
        carried, refs = refs[:carry], refs[carry:]
        (loss_ref,), refs = refs[:1], refs[1:]
        carried_out, refs = refs[:carry], refs[carry:]
    (wbuf, tail, table, pix, emb, hid0, mid0, hid1, acc, qkv, norm_a, norm_b, mixed, pre, act), refs = (
        refs[:15],
        refs[15:],
    )
    (norm_c, kv), refs = refs[:2], refs[2:]
    if with_grads:
        (dhid, dqkv, gb, dmix, stage, stage_sem), refs = refs[:6], refs[6:]
    elif carry:
        (hold, hold_sems), refs = refs[:2], refs[2:]
    (wsem, small_sem) = refs

    layer_at = [FIRST_LAYER + index * (4 * D + 2 * FF) for index in range(LAYERS)]
    order = [0]
    for start in layer_at:
        order += [start, start + 4 * D, start + 4 * D + FF]
    if with_grads:
        order += [layer_at[0] + 4 * D + FF, layer_at[0] + 4 * D, layer_at[0]]
    slot_of = [0, 1, 2, 0, 1, 2, 0, 0, 2, 1]

    def fetch(index):
        return pltpu.make_async_copy(
            w_hbm.at[pl.ds(order[index], BLOCK)], wbuf.at[slot_of[index]], wsem.at[slot_of[index]]
        )

    hops = []
    if carry:
        piece = hold.shape[1]
        for source, target in zip(carried, carried_out):
            for start in range(0, source.shape[0], piece):
                hops.append((source.at[pl.ds(start, piece)], target.at[pl.ds(start, piece)]))

    def hop_in(index):
        slot = index % 4
        return pltpu.make_async_copy(hops[index][0], hold.at[slot], hold_sems.at[0, slot])

    def hop_out(index):
        slot = index % 4
        return pltpu.make_async_copy(hold.at[slot], hops[index][1], hold_sems.at[1, slot])

    hopped = [0]

    def hop():
        index = hopped[0]
        if index < len(hops):
            hop_in(index).wait()
            hop_out(index).start()
            if index >= 2:
                hop_out(index - 2).wait()
            if 2 <= index and index + 2 < len(hops):
                hop_in(index + 2).start()
        hopped[0] = index + 1

    for index in range(min(4, len(hops))):
        hop_in(index).start()

    load_pix = pltpu.make_async_copy(pix_hbm, pix, small_sem.at[0])
    load_tail = pltpu.make_async_copy(
        w_hbm.at[pl.ds(TAIL_START, TAIL_ROWS)], tail, small_sem.at[1]
    )
    load_table = pltpu.make_async_copy(w_hbm.at[pl.ds(BLOCK, TABLE_ROWS)], table, small_sem.at[2])
    fetch(0).start()
    load_pix.start()
    load_table.start()
    load_tail.start()
    fetch(1).start()
    fetch(2).start()

    def chunks_of(count=rows_all // PAIR):
        return pl.loop(0, count)

    def rows_at(index):
        return pl.ds(pl.multiple_of(index * PAIR, PAIR), PAIR)

    def norm_row(index):
        return tail[0:16, :].astype(jnp.float32)[index : index + 1]

    def class_rows(ref):
        picked = [ref[TOKENS * i + CLASS_AT : TOKENS * i + CLASS_AT + 1, :] for i in range(images)]
        if images < 8:
            picked.append(jnp.zeros((8 - images, ref.shape[1]), ref.dtype))
        return jnp.concatenate(picked, axis=0)

    def add_class_rows(ref, values):
        for i in range(images):
            at = slice(TOKENS * i + CLASS_AT, TOKENS * i + CLASS_AT + 1)
            ref[at, :] = ref[at, :] + values[i : i + 1]

    def layer_norm_into(source, target, gain_row):
        gain, bias = norm_row(gain_row), norm_row(gain_row + 1)

        @chunks_of()
        def _(index):
            rows = rows_at(index)
            unit, _ = norm_parts(source[rows, :])
            target[rows, :] = (unit * gain + bias).astype(target.dtype)

    load_table.wait()
    load_tail.wait()
    load_pix.wait()
    fetch(0).wait()
    emb[...] = dot(pix[...], wbuf[0])
    hop()
    fetch(3).start()
    rows_table = table[...].astype(jnp.float32)
    added = pltpu.roll(rows_table, TABLE_ROWS - 2, 0)[:TOKENS]
    token = lax.broadcasted_iota(jnp.int32, (TOKENS, D), 0)
    added = jnp.where(token == CLASS_AT, rows_table[0:1] + rows_table[1:2], added)
    added = jnp.where(token < SEQ, added, 0.0)

    gain, bias = norm_row(0), norm_row(1)

    @chunks_of()
    def _(index):
        rows = rows_at(index)
        values = emb[rows, :] + jnp.concatenate([added, added], axis=0)
        emb[rows, :] = values
        unit, _ = norm_parts(values)
        hid0[rows, :] = unit * gain + bias

    layer_norm_into(hid0, norm_a, 2)
    hop()
    fetch(1).wait()

    @pl.loop(0, 3)
    def _(part):
        at = pl.ds(pl.multiple_of(part * D, D), D)
        qkv[:, at] = low(dot(norm_a[...], wbuf[1, at, :]))

    bias_pair = pair_bias()
    hop()

    def lanes(part, group):
        return slice(part * D + group * 256, part * D + (group + 1) * 256)

    def pair_soft(queries, keys):
        scores = dot(queries, keys, 1, 1) * HEAD ** (-0.5)
        scores = scores.reshape(4, PAIR, PAIR) + bias_pair[None]
        return soft(scores).reshape(4 * PAIR, PAIR)

    @pl.loop(0, pairs)
    def _(index):
        rows = rows_at(index)
        for group in range(3):
            queries = stack_heads(qkv[rows, lanes(0, group)])
            probs = low(pair_soft(queries, qkv[rows, lanes(1, group)]))
            out = dot(probs, qkv[rows, lanes(2, group)])
            mixed[rows, lanes(0, group)] = low(fold_heads(out))

    acc[...] = dot(mixed[...], wbuf[1, 3 * D : 4 * D, :])
    hop()
    fetch(4).start()
    gain2, bias2 = norm_row(4), norm_row(5)
    hop()

    @chunks_of()
    def _(index):
        rows = rows_at(index)
        values = hid0[rows, :] + acc[rows, :]
        mid0[rows, :] = values
        unit, _ = norm_parts(values)
        norm_b[rows, :] = low(unit * gain2 + bias2)

    fetch(2).wait()

    @pl.loop(0, 3)
    def _(part):
        at = pl.ds(pl.multiple_of(part * 1024, 1024), 1024)
        values = dot(norm_b[...], wbuf[2, at, :], 1, 1)
        if with_grads:
            pre[:, at] = low(values)
        act[:, at] = low(values * jax.nn.sigmoid(GELU_SLOPE * values))

    fetch(5).start()
    fetch(3).wait()
    hop()
    acc[...] = dot(act[...], wbuf[0])
    fetch(6).start()
    gain3, bias3 = norm_row(6), norm_row(7)
    hop()

    @chunks_of()
    def _(index):
        rows = rows_at(index)
        values = mid0[rows, :] + acc[rows, :]
        hid1[rows, :] = values
        unit, _ = norm_parts(values)
        norm_c[rows, :] = low(unit * gain3 + bias3)

    fetch(4).wait()

    @pl.loop(0, 2)
    def _(part):
        kv[:, pl.ds(pl.multiple_of(part * D, D), D)] = low(
            dot(norm_c[...], wbuf[1, pl.ds(pl.multiple_of(part * D + D, D), D), :])
        )

    class_hid = class_rows(hid1)
    hop()
    unit_one, _ = norm_parts(class_hid)
    class_a = low(wide(unit_one * gain3 + bias3, 16))
    class_q = low(dot(class_a, wbuf[1, 0:D, :]))
    spread_q = low(spread_heads(class_q[:8].astype(jnp.float32)))
    bias_class = class_bias()
    class_probs, outs = [], []
    for pair in range(pairs):
        rows = slice(pair * PAIR, (pair + 1) * PAIR)
        scores = dot(spread_q[32 * pair : 32 * pair + 32], kv[rows, 0:D], 1, 1)
        probs = soft(scores * HEAD ** (-0.5) + bias_class)
        class_probs.append(probs)
        outs.append(dot(low(probs), kv[rows, D : 2 * D]))
    for _ in range(4 - pairs):
        outs.append(jnp.zeros((32, D), jnp.float32))
    class_mix = low(wide(unspread_heads(jnp.concatenate(outs, axis=0)), 16))
    class_mid = class_hid + dot(class_mix, wbuf[1, 3 * D : 4 * D, :])[:8]
    hop()
    unit_two, _ = norm_parts(class_mid)
    gain4, bias4 = norm_row(8), norm_row(9)
    class_b = low(wide(unit_two * gain4 + bias4, 16))
    fetch(5).wait()
    class_pre = dot(class_b, wbuf[2], 1, 1)
    hop()
    gate = jax.nn.sigmoid(GELU_SLOPE * class_pre)
    class_act = low(class_pre * gate)
    fetch(6).wait()
    class_out = class_mid + dot(class_act, wbuf[0])[:8]
    hop()
    gain5, bias5 = norm_row(10), norm_row(11)
    unit_post, _ = norm_parts(class_out)
    pooled = low(wide(unit_post * gain5 + bias5, 16))

    hop()
    pooled_out = dot(pooled, tail[...], 1, 1)
    pooled_out = jnp.concatenate([pooled_out, jnp.zeros((16, 640 - TAIL_ROWS), jnp.float32)], axis=1)
    embedded = pltpu.roll(pooled_out, 640 - HEAD_AT, 1)[:8, :EMB]
    length = lax.rsqrt(jnp.sum(embedded * embedded, -1, keepdims=True) + NORM_EPS)
    unit_rows = embedded * length
    logits = LOGIT_SCALE * dot(low(wide(unit_rows, 16)), text_ref[...], 1, 1)[:8]
    top = jnp.max(logits, -1, keepdims=True)
    log_total = top + jnp.log(jnp.sum(jnp.exp(logits - top), -1, keepdims=True))
    log_probs = logits - log_total
    classes = lax.broadcasted_iota(jnp.int32, logits.shape, 1)
    label = note_ref[:, 0:1].astype(jnp.int32)
    target = jnp.where(classes == label, 1.0 - SMOOTH, 0.0) + SMOOTH / CLASSES
    live = note_ref[:, 1:2]
    losses = -live * jnp.sum(target * log_probs, -1, keepdims=True)
    if not with_grads:
        loss_ref[...] = jnp.broadcast_to(losses, loss_ref.shape)
        while hopped[0] < len(hops):
            hop()
        for index in range(max(0, len(hops) - 2), len(hops)):
            hop_out(index).wait()
        return

    grad_raw = low(wide(LOGIT_SCALE * ((jnp.exp(log_probs) - target) * live), 16))
    grad_unit = dot(grad_raw, text_ref[...])[:8]
    along = jnp.sum(grad_unit * embedded, -1, keepdims=True)
    grad_embed = grad_unit * length - embedded * (length * length * length * along)
    grad_embed = low(wide(grad_embed, 16))
    grad_tail = jnp.concatenate(
        [grad_embed.astype(jnp.float32), jnp.zeros((16, 640 - EMB), jnp.float32)], axis=1
    )
    grad_tail = low(pltpu.roll(grad_tail, HEAD_AT, 1)[:, :TAIL_ROWS])
    grad_pooled = dot(grad_tail, tail[...])[:8]

    def put_extra(row, values):
        extra_ref[row : row + 1, :] = values

    extra_ref[...] = jnp.zeros_like(extra_ref)
    lane = lax.broadcasted_iota(jnp.int32, (1, D), 1)
    put_extra(12, jnp.where(lane == 0, jnp.sum(losses), jnp.where(lane == 1, jnp.sum(live), 0.0)))

    def class_norm_back(values, gain_row, grad):
        result, terms = norm_back(values, norm_row(gain_row), grad)
        put_extra(gain_row, jnp.sum(terms, 0, keepdims=True))
        put_extra(gain_row + 1, jnp.sum(grad, 0, keepdims=True))
        return result

    grad_out = class_norm_back(class_out, 10, grad_pooled)

    grad_b = low(wide(grad_out, 16))
    grad_act = dot(grad_b, wbuf[0], 1, 1)
    grad_pre = low(grad_act * (gate + GELU_SLOPE * class_pre * gate * (1.0 - gate)))
    fetch(7).start()
    grad_mid = grad_out + class_norm_back(class_mid, 8, dot(grad_pre, wbuf[2])[:8])
    fetch(8).start()
    grad_proj = low(wide(grad_mid, 16))
    grad_mix = low(dot(grad_proj, wbuf[1, 3 * D : 4 * D, :], 1, 1))
    spread_g = low(spread_heads(grad_mix[:8].astype(jnp.float32)))
    grad_qs = []
    for pair in range(pairs):
        rows = slice(pair * PAIR, (pair + 1) * PAIR)
        some_g, some_q = spread_g[32 * pair : 32 * pair + 32], spread_q[32 * pair : 32 * pair + 32]
        probs = class_probs[pair]
        grad_probs = dot(some_g, kv[rows, D : 2 * D], 1, 1)
        dqkv[rows, 2 * D : 3 * D] = low(dot(low(probs), some_g, 0, 0))
        grad_scores = probs * (grad_probs - jnp.sum(grad_probs * probs, -1, keepdims=True))
        grad_scores = low(grad_scores)
        grad_qs.append(dot(grad_scores, kv[rows, 0:D]))
        dqkv[rows, D : 2 * D] = low(dot(grad_scores, some_q, 0, 0) * HEAD ** (-0.5))
    grad_q = low(wide(unspread_heads(jnp.concatenate(grad_qs, axis=0)) * HEAD ** (-0.5), 16))

    def pack(first, second, at, width):
        factor_ref[:, at : at + width] = low(
            jnp.concatenate([first[:8].astype(jnp.float32), second[:8].astype(jnp.float32)], axis=0)
        )

    pack(grad_pre, class_act, 0, FF)
    pack(class_a, class_mix, FF, D)
    pack(grad_q, grad_proj, FF + D, D)
    pack(class_b, grad_b, FF + 2 * D, D)
    embed_wide = jnp.concatenate(
        [grad_embed.astype(jnp.float32), jnp.zeros((16, D - EMB), jnp.float32)], axis=1
    )
    pack(embed_wide, pooled, FF + 3 * D, D)

    started = [0]

    def push(slot, at):
        return pltpu.make_async_copy(stage.at[slot], g_hbm.at[pl.ds(at, D)], stage_sem.at[slot])

    def weight_grad(left, left_at, right, right_at, at, count):
        base = started[0]

        def one(block):
            slot = lax.rem(base + block, 2)

            @pl.when(base + block >= 2)
            def _():
                push(slot, at).wait()

            from_lane = pl.multiple_of(left_at + block * D, D) if count > 1 else left_at
            stage[slot] = low(dot(left[:, pl.ds(from_lane, D)], right[:, right_at : right_at + D], 0, 0))
            push(slot, pl.multiple_of(at + block * D, 16)).start()

        if count > 1:
            pl.loop(0, count)(one)
        else:
            one(0)
        started[0] = base + count

    def norm_back_rows(values, gain_row, grad, finish):
        gain = norm_row(gain_row)
        extra_ref[gain_row : gain_row + 2, :] = jnp.zeros((2, D), jnp.float32)

        @chunks_of()
        def _(index):
            rows = rows_at(index)
            grad_rows = grad[rows, :]
            result, terms = norm_back(values[rows, :], gain, grad_rows)
            at = slice(gain_row, gain_row + 1)
            extra_ref[at, :] = extra_ref[at, :] + jnp.sum(terms, 0, keepdims=True)
            at = slice(gain_row + 1, gain_row + 2)
            extra_ref[at, :] = extra_ref[at, :] + jnp.sum(grad_rows, 0, keepdims=True)
            finish(rows, result)

    weight_grad(norm_c, 0, dqkv, D, layer_at[1] + D, 1)
    weight_grad(norm_c, 0, dqkv, 2 * D, layer_at[1] + 2 * D, 1)
    acc[...] = dot(dqkv[:, D : 2 * D], wbuf[1, D : 2 * D, :], 1, 1)
    acc[...] = acc[...] + dot(dqkv[:, 2 * D : 3 * D], wbuf[1, 2 * D : 3 * D, :], 1, 1)
    add_class_rows(acc, dot(grad_q, wbuf[1, 0:D, :], 1, 1))
    fetch(9).start()

    def finish_second(rows, result):
        dhid[rows, :] = result

    norm_back_rows(hid1, 6, acc, finish_second)
    add_class_rows(dhid, grad_mid)

    gb[...] = low(dhid[...])
    fetch(7).wait()
    weight_grad(act, 0, gb, 0, layer_at[0] + 4 * D + FF, FF // D)

    @pl.loop(0, 3)
    def _(part):
        at = pl.ds(pl.multiple_of(part * 1024, 1024), 1024)
        grad_rows = dot(gb[...], wbuf[0, at, :], 1, 1)
        values = pre[:, at].astype(jnp.float32)
        gates = jax.nn.sigmoid(GELU_SLOPE * values)
        pre[:, at] = low(grad_rows * (gates + GELU_SLOPE * values * gates * (1.0 - gates)))

    weight_grad(pre, 0, norm_b, 0, layer_at[0] + 4 * D, FF // D)
    fetch(8).wait()
    acc[...] = dot(pre[...], wbuf[2])

    def finish_mid(rows, result):
        total = dhid[rows, :] + result
        dhid[rows, :] = total
        gb[rows, :] = low(total)

    norm_back_rows(mid0, 4, acc, finish_mid)
    weight_grad(mixed, 0, gb, 0, layer_at[0] + 3 * D, 1)
    fetch(9).wait()
    dmix[...] = low(dot(gb[...], wbuf[1, 3 * D : 4 * D, :], 1, 1))

    @pl.loop(0, pairs)
    def _(index):
        rows = rows_at(index)
        for group in range(3):
            queries = stack_heads(qkv[rows, lanes(0, group)])
            keys = qkv[rows, lanes(1, group)]
            probs = pair_soft(queries, keys)
            some_g = stack_heads(dmix[rows, lanes(0, group)])
            grad_probs = dot(some_g, qkv[rows, lanes(2, group)], 1, 1)
            dqkv[rows, lanes(2, group)] = low(dot(low(probs), some_g, 0, 0))
            grad_scores = probs * (grad_probs - jnp.sum(grad_probs * probs, -1, keepdims=True))
            grad_scores = low(grad_scores)
            grad_queries = fold_heads(dot(grad_scores, keys))
            dqkv[rows, lanes(0, group)] = low(grad_queries * HEAD ** (-0.5))
            grad_keys = dot(grad_scores, queries, 0, 0)
            dqkv[rows, lanes(1, group)] = low(grad_keys * HEAD ** (-0.5))

    for part in range(3):
        weight_grad(norm_a, 0, dqkv, part * D, layer_at[0] + part * D, 1)
    acc[...] = dot(dqkv[:, 0:D], wbuf[1, 0:D, :], 1, 1)
    for part in (1, 2):
        at = slice(part * D, (part + 1) * D)
        acc[...] = acc[...] + dot(dqkv[:, at], wbuf[1, at, :], 1, 1)

    def finish_first(rows, result):
        dhid[rows, :] = dhid[rows, :] + result

    norm_back_rows(hid0, 2, acc, finish_first)

    def finish_embedding(rows, result):
        dhid[rows, :] = result
        gb[rows, :] = low(result)

    norm_back_rows(emb, 0, dhid, finish_embedding)
    weight_grad(pix, 0, gb, 0, 0, PATCH_IN // D)
    grad_tokens = dhid[0:TOKENS, :]
    for i in range(1, images):
        grad_tokens = grad_tokens + dhid[TOKENS * i : TOKENS * (i + 1), :]
    class_grad = grad_tokens[CLASS_AT : CLASS_AT + 1]
    grad_tokens = jnp.concatenate(
        [grad_tokens, jnp.zeros((TABLE_ROWS - TOKENS, D), jnp.float32)], axis=0
    )
    grad_table = pltpu.roll(grad_tokens, 2, 0)
    row = lax.broadcasted_iota(jnp.int32, (TABLE_ROWS, D), 0)
    grad_table = jnp.where(row < 2, class_grad, jnp.where(row < SEQ + 1, grad_table, 0.0))
    table[...] = low(grad_table)
    put_table = pltpu.make_async_copy(table, g_hbm.at[pl.ds(BLOCK, TABLE_ROWS)], small_sem.at[0])
    put_table.start()
    put_table.wait()
    for slot in range(2):
        push(slot, 0).wait()


def image_notes(label_row, live_mask):
    notes = jnp.stack([label_row.astype(jnp.float32), live_mask], axis=1)
    return jnp.pad(notes, ((0, 8 - notes.shape[0]), (0, 126)))


def run_tower(weights, pixel_rows, notes, text, with_grads, carried=()):
    rows_all = pixel_rows.shape[0]
    images = rows_all // TOKENS
    bf16, f32 = jnp.bfloat16, jnp.float32
    scratch = [
        pltpu.VMEM((3, BLOCK, D), bf16),
        pltpu.VMEM((TAIL_ROWS, D), bf16),
        pltpu.VMEM((TABLE_ROWS, D), bf16),
        pltpu.VMEM((rows_all, PATCH_IN), bf16),
        pltpu.VMEM((rows_all, D), f32),
        pltpu.VMEM((rows_all, D), f32),
        pltpu.VMEM((rows_all, D), f32),
        pltpu.VMEM((rows_all, D), f32),
        pltpu.VMEM((rows_all, D), f32),
        pltpu.VMEM((rows_all, 3 * D), bf16),
        pltpu.VMEM((rows_all, D), bf16),
        pltpu.VMEM((rows_all, D), bf16),
        pltpu.VMEM((rows_all, D), bf16),
        pltpu.VMEM((rows_all if with_grads else 16, FF), bf16),
        pltpu.VMEM((rows_all, FF), bf16),
        pltpu.VMEM((rows_all, D), bf16),
        pltpu.VMEM((rows_all, 2 * D), bf16),
    ]
    if with_grads:
        scratch += [
            pltpu.VMEM((rows_all, D), f32),
            pltpu.VMEM((rows_all, 3 * D), bf16),
            pltpu.VMEM((rows_all, D), bf16),
            pltpu.VMEM((rows_all, D), bf16),
            pltpu.VMEM((2, D, D), bf16),
            pltpu.SemaphoreType.DMA((2,)),
        ]
        out_shape = (
            jax.ShapeDtypeStruct((grad_rows_kept(weights.shape[0]), D), bf16),
            jax.ShapeDtypeStruct((16, LOW_COLS), bf16),
            jax.ShapeDtypeStruct((16, D), f32),
        )
        out_specs = (
            pl.BlockSpec(memory_space=pl.ANY),
            pl.BlockSpec(memory_space=pltpu.VMEM),
            pl.BlockSpec(memory_space=pltpu.VMEM),
        )
    else:
        out_shape = (jax.ShapeDtypeStruct((8, 128), f32),)
        out_shape += tuple(jax.ShapeDtypeStruct(array.shape, array.dtype) for array in carried)
        out_specs = (pl.BlockSpec(memory_space=pltpu.VMEM),)
        out_specs += (pl.BlockSpec(memory_space=pl.ANY),) * len(carried)
        if carried:
            scratch += [
                pltpu.VMEM((4, carried[0].shape[0] // 6, carried[0].shape[1]), carried[0].dtype),
                pltpu.SemaphoreType.DMA((2, 4)),
            ]
    scratch += [pltpu.SemaphoreType.DMA((3,)), pltpu.SemaphoreType.DMA((3,))]
    vmem = pl.BlockSpec(memory_space=pltpu.VMEM)
    hbm = pl.BlockSpec(memory_space=pl.ANY)
    return pl.pallas_call(
        functools.partial(tower_kernel, images, with_grads, len(carried)),
        out_shape=out_shape,
        in_specs=[hbm, hbm, vmem, vmem] + [hbm] * len(carried),
        out_specs=out_specs,
        scratch_shapes=scratch,
        compiler_params=pltpu.CompilerParams(vmem_limit_bytes=(52 if with_grads else 40) * 2**20),
        cost_estimate=None
        if with_grads
        else pl.CostEstimate(
            flops=2 * rows_all * weights.shape[0] * D,
            bytes_accessed=2 * weights.shape[0] * D,
            transcendentals=rows_all * 2 * FF,
        ),
        name="train" if with_grads else "evaluate",
    )(weights, pixel_rows, text, notes, *carried)


def grad_rows_kept(rows):
    if not on_grid():
        return DENSE_END
    plane_rows = rows // 4
    return (DENSE_END + plane_rows - 1) // plane_rows * plane_rows


def on_grid():
    return lax.axis_size("group") == 4 and lax.axis_size("dp") == 8


def place():
    worker = lax.axis_index("group")
    rank = lax.axis_index("dp")
    return (worker // 2, worker % 2, rank // 2, rank % 2)


def device_at(y, c, z, x):
    return (y * 2 + c, z * 2 + x)


def chunk_rows(total, share):
    units = total // 16
    sizes = [3, 4] + [6] * ((units - 15) // 6) + [4, 4 + (units - 15) % 6]
    chunks = []
    start = taken = 0
    for size in sizes:
        first = int(round((start + size) * share)) - taken
        taken += first
        chunks.append((start * 16, first * 16, (size - first) * 16))
        start += size
    return chunks


def image_device():
    y, c, z, x = place()
    return device_at((z + c) % 2, z // 2, 2 * c + y, x)


def image_source():
    y, c, z, x = place()
    return device_at(z % 2, z // 2, 2 * c + (y + z // 2) % 2, x)


def gather_kernel(chunks, images, *refs):
    if images:
        (part_ref, pixel_ref, note_ref, full_ref, moved_ref, moved_note_ref), refs = refs[:6], refs[6:]
        (local_sem, sends, recvs, pixel_sems) = refs
        count = pixel_ref.shape[0] // TOKENS
        parcels = [(note_ref, moved_note_ref)]
        for index in range(count):
            rows = pl.ds(index * TOKENS, TOKENS)
            parcels.append((pixel_ref.at[rows], moved_ref.at[rows]))
    else:
        (part_ref, full_ref, local_sem, sends, recvs) = refs
    half_cols = part_ref.shape[1]
    y, c, z, x = place()
    cols = pl.ds(pl.multiple_of(c * half_cols, half_cols), half_cols)
    over_x = device_at(y, c, z, 1 - x)
    over_y = device_at(1 - y, c, z, x)
    sibling = device_at(y, 1 - c, z, x)
    along_z = [device_at(y, c, (z + step) % 4, x) for step in (1, 2, 3)]
    target = image_device()
    stays = jnp.logical_and(target[0] == y * 2 + c, target[1] == z * 2 + x)
    barrier = pltpu.get_barrier_semaphore()
    for other in [over_x, over_y, sibling] + along_z:
        pl.semaphore_signal(barrier, inc=1, device_id=other, device_id_type=MESH)
    if images:

        @pl.when(jnp.logical_not(stays))
        def _():
            pl.semaphore_signal(barrier, inc=1, device_id=image_source(), device_id_type=MESH)

    def keep(index):
        start, first, second = chunks[index]
        rows = pl.ds(start, first + second)
        return pltpu.make_async_copy(
            part_ref.at[rows], full_ref.at[z, x, y, rows, cols], local_sem.at[index]
        )

    for index in range(len(chunks)):
        keep(index).start()
    pl.semaphore_wait(barrier, 6 + (jnp.where(stays, 0, 1) if images else 0))

    def send(piece, other, stage, index):
        pltpu.make_async_remote_copy(
            src_ref=piece,
            dst_ref=piece,
            send_sem=sends.at[stage, index],
            recv_sem=recvs.at[stage, index],
            device_id=other,
            device_id_type=MESH,
        ).start()

    def move_parcel(which):
        source, place_at = parcels[which]

        @pl.when(stays)
        def _():
            pltpu.make_async_copy(source, place_at, pixel_sems.at[0, which]).start()

        @pl.when(jnp.logical_not(stays))
        def _():
            pltpu.make_async_remote_copy(
                src_ref=source,
                dst_ref=place_at,
                send_sem=pixel_sems.at[1, which],
                recv_sem=pixel_sems.at[0, which],
                device_id=target,
                device_id_type=MESH,
            ).start()

    def arrived(piece, stage, index):
        pltpu.make_async_copy(piece, piece, recvs.at[stage, index]).wait()

    def sent(piece, stage, index):
        pltpu.make_async_copy(piece, piece, sends.at[stage, index]).wait()

    def pieces(index):
        start, first, second = chunks[index]
        rows = pl.ds(start, first + second)
        rows_a = pl.ds(start, first)
        rows_b = pl.ds(start + first, second)
        return {
            0: full_ref.at[pl.ds(0, 3), 0, 0, rows, cols],
            1: full_ref.at[:, x, y, rows_a, cols],
            2: full_ref.at[:, x, y, rows_b, cols],
            3: full_ref.at[:, x, :, rows_a, cols],
            4: full_ref.at[:, :, y, rows_b, cols],
            5: full_ref.at[:, :, :, rows, cols],
        }

    total = len(chunks)

    def send_along_z(index):
        start, first, second = chunks[index]
        rows = pl.ds(start, first + second)
        for other in along_z:
            pltpu.make_async_remote_copy(
                src_ref=part_ref.at[rows],
                dst_ref=full_ref.at[z, x, y, rows, cols],
                send_sem=sends.at[0, index],
                recv_sem=recvs.at[0, index],
                device_id=other,
                device_id_type=MESH,
            ).start()

    ahead = LOOK_AHEAD if images else 1
    for step in range(total + 3):
        for index in range(ahead) if step == 0 else [step + ahead - 1]:
            if index < total:
                send_along_z(index)
        if images and step % PARCEL_STEP == 0 and step // PARCEL_STEP < len(parcels):
            move_parcel(step // PARCEL_STEP)
        index = step - 1
        if 0 <= index < total:
            block = pieces(index)
            arrived(block[0], 0, index)
            keep(index).wait()
            send(block[1], over_y, 1, index)
            send(block[2], over_x, 2, index)
        index = step - 2
        if 0 <= index < total:
            block = pieces(index)
            arrived(block[1], 1, index)
            send(block[3], over_x, 3, index)
            arrived(block[2], 2, index)
            send(block[4], over_y, 4, index)
        index = step - 3
        if 0 <= index < total:
            block = pieces(index)
            arrived(block[3], 3, index)
            arrived(block[4], 4, index)
            send(block[5], sibling, 5, index)
    for index in range(total):
        block = pieces(index)
        arrived(block[5], 5, index)
        for stage in range(6):
            sent(block[stage], stage, index)
    if images:
        for which, (_, place_at) in enumerate(parcels):
            pltpu.make_async_copy(place_at, place_at, pixel_sems.at[0, which]).wait()

        @pl.when(jnp.logical_not(stays))
        def _():
            for which, (_, place_at) in enumerate(parcels):
                pltpu.make_async_copy(place_at, place_at, pixel_sems.at[1, which]).wait()


def gather_rows(part, shard_rows, pixel_rows=None, notes=None):
    images = pixel_rows is not None
    chunks = chunk_rows(part.shape[0], FIRST_SHARE if images else 0.5)
    hbm = pl.BlockSpec(memory_space=pl.ANY)
    width = 2 * part.shape[1]
    full_shape = jax.ShapeDtypeStruct((4, 2, 2, part.shape[0], width), part.dtype)
    semaphores = [
        pltpu.SemaphoreType.DMA((len(chunks),)),
        pltpu.SemaphoreType.DMA((6, len(chunks))),
        pltpu.SemaphoreType.DMA((6, len(chunks))),
    ]
    kernel = functools.partial(gather_kernel, chunks, images)
    if not images:
        full = pl.pallas_call(
            kernel,
            out_shape=full_shape,
            in_specs=[hbm],
            out_specs=hbm,
            scratch_shapes=semaphores,
            compiler_params=pltpu.CompilerParams(collective_id=0, has_side_effects=True),
            name="gather",
        )(part)
        return full.reshape(8 * shard_rows, width)
    full, moved, moved_notes = pl.pallas_call(
        kernel,
        out_shape=(
            full_shape,
            jax.ShapeDtypeStruct(pixel_rows.shape, pixel_rows.dtype),
            jax.ShapeDtypeStruct(notes.shape, notes.dtype),
        ),
        in_specs=[hbm, hbm, hbm],
        out_specs=[hbm, hbm, hbm],
        scratch_shapes=semaphores
        + [pltpu.SemaphoreType.DMA((2, 1 + pixel_rows.shape[0] // TOKENS))],
        compiler_params=pltpu.CompilerParams(collective_id=2, has_side_effects=True),
        name="gather_first",
    )(part, pixel_rows, notes)
    return (full.reshape(8 * shard_rows, width), moved, moved_notes)


def reduce_kernel(
    chunks,
    low_from,
    grad_ref,
    factor_ref,
    extra_ref,
    own_ref,
    factors_ref,
    extras_ref,
    squares_ref,
    mine,
    first_sum,
    sum_a,
    sum_b,
    last_sum,
    squares,
    passed_factor,
    passed_extra,
    relay,
    load_sems,
    sends,
    recvs,
    small_sends,
    small_recvs,
    pass_sends,
    pass_recvs,
):
    half_cols = first_sum.shape[-1]
    planes = grad_ref.shape[0]
    y, c, z, x = place()
    home_y, home_c = z % 2, z // 2
    at_home = jnp.logical_and(home_y == y, home_c == c)
    from_plane = 2 * c + y
    my_cols = pl.ds(pl.multiple_of(c * half_cols, half_cols), half_cols)
    other_cols = pl.ds(pl.multiple_of((1 - c) * half_cols, half_cols), half_cols)
    over_x = device_at(y, c, z, 1 - x)
    over_y = device_at(1 - y, c, z, x)
    sibling = device_at(y, 1 - c, z, x)
    barrier = pltpu.get_barrier_semaphore()
    for other in (over_x, over_y, sibling):
        pl.semaphore_signal(barrier, inc=1, device_id=other, device_id_type=MESH)
    for other in range(8):
        other_y, other_c, other_x = other // 4, other // 2 % 2, other % 2
        same = jnp.logical_and(y == other_y, jnp.logical_and(c == other_c, x == other_x))
        itself = jnp.logical_and(at_home, same)

        @pl.when(jnp.logical_not(itself))
        def _():
            pl.semaphore_signal(
                barrier,
                inc=1,
                device_id=device_at(other_y, other_c, from_plane, other_x),
                device_id_type=MESH,
            )

    through_self = z // 2 == c
    for other in range(4):
        from_z = 2 * c + other // 2
        itself = jnp.logical_and(z == from_z, c == other % 2)

        @pl.when(jnp.logical_not(itself))
        def _():
            pl.semaphore_signal(
                barrier, inc=1, device_id=device_at(y, other % 2, from_z, x), device_id_type=MESH
            )

    def spans(index):
        start, first, second = chunks[index]
        start_a = sum(chunk[1] for chunk in chunks[:index])
        start_b = sum(chunk[2] for chunk in chunks[:index])
        return (
            pl.ds(start, first + second),
            pl.ds(start, first),
            pl.ds(start + first, second),
            pl.ds(start_a, first),
            pl.ds(start_b, second),
        )

    def send(source, target, other, stage, index):
        pltpu.make_async_remote_copy(
            src_ref=source,
            dst_ref=target,
            send_sem=sends.at[stage, index],
            recv_sem=recvs.at[stage, index],
            device_id=other,
            device_id_type=MESH,
        ).start()

    def arrived(piece, stage, index):
        pltpu.make_async_copy(piece, piece, recvs.at[stage, index]).wait()

    def sent(piece, stage, index):
        pltpu.make_async_copy(piece, piece, sends.at[stage, index]).wait()

    def load(index):
        rows = spans(index)[0]
        return pltpu.make_async_copy(
            grad_ref.at[:, :, :, rows],
            mine.at[index % 2, :, :, :, pl.ds(0, rows.size)],
            load_sems.at[index % 2],
        )

    def send_core(index):
        rows = spans(index)[0]
        send(
            grad_ref.at[:, :, :, rows, other_cols],
            first_sum.at[:, :, :, rows],
            sibling,
            0,
            index,
        )

    def own_rows(half, rows):
        return pl.ds(pl.multiple_of(half * grad_ref.shape[3] + rows.start, 16), rows.size)

    def add(target, source):
        summed = target[...].astype(jnp.float32) + source[...].astype(jnp.float32)
        target[...] = summed.astype(target.dtype)

    total = len(chunks)
    load(0).start()
    pl.semaphore_wait(barrier, 3 + jnp.where(at_home, 7, 8) + jnp.where(through_self, 3, 4))
    send_core(0)
    send_core(1)
    def slot_of(from_y):
        return (from_y * 2 + c) * 2 + x

    def to_owners(source, target, which, first_z, way):
        for other in range(2 * first_z, 8):
            other_z, other_x = other // 2, other % 2
            itself = jnp.logical_and(at_home, jnp.logical_and(z == other_z, x == other_x))

            @pl.when(jnp.logical_not(itself))
            def _():
                pltpu.make_async_remote_copy(
                    src_ref=source,
                    dst_ref=target,
                    send_sem=small_sends.at[way, which],
                    recv_sem=small_recvs.at[which],
                    device_id=device_at(home_y, home_c, other_z, other_x),
                    device_id_type=MESH,
                ).start()

            @pl.when(itself)
            def _():
                pltpu.make_async_copy(source, target, small_recvs.at[which]).start()

    def passing(which):
        source, target = ((extra_ref, passed_extra), (factor_ref, passed_factor))[which]
        return pltpu.make_async_remote_copy(
            src_ref=source,
            dst_ref=target,
            send_sem=pass_sends.at[which],
            recv_sem=pass_recvs.at[which],
            device_id=over_y,
            device_id_type=MESH,
        )

    gives = y != home_y

    @pl.when(gives)
    def _():
        for which in range(2):
            passing(which).start()

    @pl.when(jnp.logical_not(gives))
    def _():
        to_owners(extra_ref, extras_ref.at[slot_of(y)], 0, 0, 0)
        to_owners(factor_ref, factors_ref.at[slot_of(y)], 1, low_from, 0)

    def pass_on():
        @pl.when(jnp.logical_not(gives))
        def _():
            for which in range(2):
                passing(which).wait_recv()
            to_owners(passed_extra, extras_ref.at[slot_of(1 - y)], 0, 0, 1)
            to_owners(passed_factor, factors_ref.at[slot_of(1 - y)], 1, low_from, 1)

    squares[...] = jnp.zeros_like(squares)
    half_rows = grad_ref.shape[3]
    last_layer = FIRST_LAYER + 4 * D + 2 * FF

    def add_squares(block, rows):
        values = last_sum[block, rows].astype(jnp.float32)
        row = ((block * 2 + x) * 2 + y) * half_rows + rows.start
        row = row + lax.broadcasted_iota(jnp.int32, values.shape, 0)
        values = jnp.where(dense_row(row), values * values, 0.0)
        values = jnp.sum(values.reshape(rows.size // 8, 8, half_cols), axis=0)
        for part in range(half_cols // 128):
            squares[...] += values[:, part * 128 : (part + 1) * 128]

    for step in range(total + 2 + RELAY_LAG):
        index = step
        if index < total:
            if index + 1 < total:
                load(index + 1).start()
            if index + 2 < total:
                send_core(index + 2)
            rows, rows_a, rows_b, in_a, in_b = spans(index)
            load(index).wait()
            arrived(first_sum.at[:, :, :, rows], 0, index)

            @pl.loop(0, 4 * planes)
            def _(block):
                zz, rest = block // 4, block % 4
                add(
                    first_sum.at[zz, rest // 2, rest % 2, rows],
                    mine.at[index % 2, zz, rest // 2, rest % 2, pl.ds(0, rows.size), my_cols],
                )

            if index == 1:
                pass_on()
            send(first_sum.at[:, 1 - x, :, rows_a], sum_a.at[:, :, in_a], over_x, 1, index)
            send(first_sum.at[:, :, 1 - y, rows_b], sum_b.at[:, :, in_b], over_y, 2, index)
        index = step - 1
        if 0 <= index < total:
            rows, rows_a, rows_b, in_a, in_b = spans(index)
            arrived(sum_a.at[:, :, in_a], 1, index)

            @pl.loop(0, 2 * planes)
            def _(block):
                add(
                    sum_a.at[block // 2, block % 2, in_a],
                    first_sum.at[block // 2, x, block % 2, rows_a],
                )

            send(sum_a.at[:, 1 - y, in_a], last_sum.at[:, rows_a], over_y, 3, index)
            arrived(sum_b.at[:, :, in_b], 2, index)

            @pl.loop(0, 2 * planes)
            def _(block):
                add(
                    sum_b.at[block // 2, block % 2, in_b],
                    first_sum.at[block // 2, block % 2, y, rows_b],
                )

            send(sum_b.at[:, 1 - x, in_b], last_sum.at[:, rows_b], over_x, 4, index)
        index = step - 2
        if 0 <= index < total:
            rows, rows_a, rows_b, in_a, in_b = spans(index)
            arrived(last_sum.at[:, rows_a], 3, index)
            arrived(last_sum.at[:, rows_b], 4, index)

            @pl.loop(0, planes)
            def _(block):
                add(last_sum.at[block, rows_a], sum_a.at[block, y, in_a])
                add(last_sum.at[block, rows_b], sum_b.at[block, x, in_b])
                add_squares(block, rows)

            on_home_y = y == home_y
            for to_z in range(planes):
                itself = jnp.logical_and(through_self, z == to_z)
                source = last_sum.at[to_z, rows]
                for direct in (True, False):
                    chosen = on_home_y if direct else jnp.logical_not(on_home_y)
                    target = own_ref.at[own_rows(y, rows), my_cols] if direct else relay.at[rows, my_cols]
                    way = 5 if direct else 6

                    @pl.when(jnp.logical_and(chosen, jnp.logical_not(itself)))
                    def _():
                        pltpu.make_async_remote_copy(
                            src_ref=source,
                            dst_ref=target,
                            send_sem=sends.at[5, index],
                            recv_sem=recvs.at[way, index],
                            device_id=device_at(y, home_c, to_z, x),
                            device_id_type=MESH,
                        ).start()

                    @pl.when(jnp.logical_and(chosen, itself))
                    def _():
                        pltpu.make_async_copy(source, target, recvs.at[way, index]).start()

        index = step - 2 - RELAY_LAG
        if 0 <= index < total:
            rows = spans(index)[0]

            @pl.when(z < planes)
            def _():
                arrived(relay.at[rows], 6, index)
                send(relay.at[rows], own_ref.at[own_rows(y, rows)], over_y, 7, index)

    to_owners(squares, squares_ref.at[slot_of(y)], 2, 0, 0)
    for index in range(total):
        rows, rows_a, rows_b, in_a, in_b = spans(index)

        @pl.when(z < planes)
        def _():
            arrived(own_ref.at[pl.ds(0, rows.size)], 5, index)
            arrived(own_ref.at[pl.ds(0, rows.size)], 7, index)
            sent(relay.at[rows], 7, index)

        sent(first_sum.at[:, :, :, rows], 0, index)
        sent(sum_a.at[:, :, in_a], 1, index)
        sent(sum_b.at[:, :, in_b], 2, index)
        sent(last_sum.at[:, rows_a], 3, index)
        sent(last_sum.at[:, rows_b], 4, index)

        kept = jnp.logical_and(through_self, z < planes)

        @pl.when(kept)
        def _():
            sent(last_sum.at[pl.ds(0, planes - 1), rows], 5, index)

        @pl.when(jnp.logical_not(kept))
        def _():
            sent(last_sum.at[:, rows], 5, index)

    def all_of(ref, count, sem):
        piece = ref.at[pl.ds(0, count)]
        pltpu.make_async_copy(piece, piece, sem).wait()

    all_of(extras_ref, 8, small_recvs.at[0])
    all_of(squares_ref, 8, small_recvs.at[2])

    @pl.when(z >= low_from)
    def _():
        all_of(factors_ref, 8, small_recvs.at[1])

    def sent_to_owners(ref, count, kept, which, way):
        @pl.when(kept)
        def _():
            all_of(ref, count - 1, small_sends.at[way, which])

        @pl.when(jnp.logical_not(kept))
        def _():
            all_of(ref, count, small_sends.at[way, which])

    sent_to_owners(squares_ref, 8, at_home, 2, 0)

    @pl.when(gives)
    def _():
        for which in range(2):
            passing(which).wait_send()

    @pl.when(jnp.logical_not(gives))
    def _():
        low_kept = jnp.logical_and(at_home, z >= low_from)
        for way in range(2):
            sent_to_owners(extras_ref, 8, at_home, 0, way)
            sent_to_owners(factors_ref, 2 * (4 - low_from), low_kept, 1, way)


def reduce_chunks(total, share):
    units = total // 16
    middle = units - sum(REDUCE_HEAD + REDUCE_TAIL)
    sizes = [8] * (middle // 8)
    sizes[-1] += middle % 8
    sizes = REDUCE_HEAD + sizes + REDUCE_TAIL
    chunks = []
    start = taken = 0
    for size in sizes:
        first = int(round((start + size) * share)) - taken
        taken += first
        chunks.append((start * 16, first * 16, (size - first) * 16))
        start += size
    return chunks


def low_plane(shard_rows):
    return (FIRST_LAYER + 4 * D + 2 * FF) // (2 * shard_rows)


def sum_on_plane(grad_rows, factors, extra, shard_rows):
    half_rows, width = shard_rows // 2, grad_rows.shape[1]
    planes = grad_rows.shape[0] // (2 * shard_rows)
    chunks = reduce_chunks(half_rows, 0.65)
    most = max(first + second for _, first, second in chunks)
    half_cols = width // 2
    dtype = grad_rows.dtype
    return pl.pallas_call(
        functools.partial(reduce_kernel, chunks, low_plane(shard_rows)),
        out_shape=(
            jax.ShapeDtypeStruct((shard_rows + 16, width), dtype),
            jax.ShapeDtypeStruct((8,) + factors.shape, factors.dtype),
            jax.ShapeDtypeStruct((8,) + extra.shape, extra.dtype),
            jax.ShapeDtypeStruct((8, 8, 128), jnp.float32),
        ),
        in_specs=[pl.BlockSpec(memory_space=pl.ANY)] * 3,
        out_specs=[pl.BlockSpec(memory_space=pl.ANY)] * 4,
        scratch_shapes=[
            pltpu.VMEM((2, planes, 2, 2, most, width), dtype),
            pltpu.VMEM((planes, 2, 2, half_rows, half_cols), dtype),
            pltpu.VMEM((planes, 2, sum(chunk[1] for chunk in chunks), half_cols), dtype),
            pltpu.VMEM((planes, 2, sum(chunk[2] for chunk in chunks), half_cols), dtype),
            pltpu.VMEM((planes, half_rows, half_cols), dtype),
            pltpu.VMEM((8, 128), jnp.float32),
            pltpu.VMEM(factors.shape, factors.dtype),
            pltpu.VMEM(extra.shape, extra.dtype),
            pltpu.VMEM((half_rows, width), dtype),
            pltpu.SemaphoreType.DMA((2,)),
            pltpu.SemaphoreType.DMA((8, len(chunks))),
            pltpu.SemaphoreType.DMA((8, len(chunks))),
            pltpu.SemaphoreType.DMA((2, 3)),
            pltpu.SemaphoreType.DMA((3,)),
            pltpu.SemaphoreType.DMA((2,)),
            pltpu.SemaphoreType.DMA((2,)),
        ],
        compiler_params=pltpu.CompilerParams(
            collective_id=1, has_side_effects=True, vmem_limit_bytes=56 * 2**20
        ),
        name="reduce",
    )(grad_rows.reshape(planes, 2, 2, half_rows, width), factors, extra)


def update_kernel(
    shape,
    own_hbm,
    rest_hbm,
    master_hbm,
    first_hbm,
    second_hbm,
    factors_ref,
    extras_ref,
    squares_ref,
    first_out,
    second_out,
    total_out,
    summary_ref,
    own,
    rest,
    weights,
    first,
    second,
    new_first,
    new_second,
    mine,
    other,
    core_in,
    y_out,
    y_in,
    load_sems,
    store_sems,
    sends,
    recvs,
    total_sem,
    low_squares_ref,
    low_sems,
):
    half_rows, piece, pieces, low_from = shape
    half_cols = mine.shape[-1]
    y, c, z, x = place()
    over_y = device_at(1 - y, c, z, x)
    sibling = device_at(y, 1 - c, z, x)
    barrier = pltpu.get_barrier_semaphore()
    for partner in (over_y, sibling):
        pl.semaphore_signal(barrier, inc=1, device_id=partner, device_id_type=MESH)
    has_factors = z >= low_from

    @pl.when(z < 4 - low_from)
    def _():
        pl.semaphore_signal(
            barrier, inc=1, device_id=device_at(y, c, z + low_from, x), device_id_type=MESH
        )

    def row_at(index):
        half = jnp.where(index < pieces, 1 - y, y)
        return pl.multiple_of(half * half_rows + index % pieces * piece, 16)

    def loads(index):
        slot = index % 2
        rows = pl.ds(row_at(index), piece)
        longer = pl.ds(row_at(index), piece + 16)
        return [
            pltpu.make_async_copy(own_hbm.at[longer], own.at[slot], load_sems.at[0, slot]),
            pltpu.make_async_copy(rest_hbm.at[rows], rest.at[slot], load_sems.at[1, slot]),
            pltpu.make_async_copy(master_hbm.at[rows], weights.at[slot], load_sems.at[2, slot]),
            pltpu.make_async_copy(first_hbm.at[rows], first.at[slot], load_sems.at[3, slot]),
            pltpu.make_async_copy(second_hbm.at[rows], second.at[slot], load_sems.at[4, slot]),
        ]

    def stores(index):
        slot = index % 2
        rows = pl.ds(row_at(index), piece)
        return [
            pltpu.make_async_copy(new_first.at[slot], first_out.at[rows], store_sems.at[0, slot]),
            pltpu.make_async_copy(new_second.at[slot], second_out.at[rows], store_sems.at[1, slot]),
        ]

    for copy in loads(0):
        copy.start()

    def gram(at, width):
        values = factors_ref[:, :, at : at + width].reshape(128, width)
        return dot(values, values, 1, 1)

    row = lax.broadcasted_iota(jnp.int32, (128, 128), 0) % 16
    col = lax.broadcasted_iota(jnp.int32, (128, 128), 1) % 16
    head = gram(FF + 3 * D, D)
    shifted_head = pltpu.roll(pltpu.roll(head, 120, 0), 120, 1)
    products = gram(0, FF) * gram(FF + 2 * D, D) + gram(FF, D) * gram(FF + D, D)
    low_squares = jnp.where(row // 8 == col // 8, products, 0.0)
    low_squares = low_squares + jnp.where((row < 8) & (col < 8), head * shifted_head, 0.0)
    pl.semaphore_wait(barrier, 2 + jnp.where(has_factors, 1, 0))
    to_low = pltpu.make_async_remote_copy(
        src_ref=low_squares_ref,
        dst_ref=low_squares_ref,
        send_sem=low_sems.at[0],
        recv_sem=low_sems.at[1],
        device_id=device_at(y, c, z - low_from, x),
        device_id_type=MESH,
    )

    @pl.when(has_factors)
    def _():
        low_squares_ref[...] = jnp.sum(low_squares.reshape(16, 8, 128), axis=0)
        to_low.start()

    @pl.when(jnp.logical_not(has_factors))
    def _():
        to_low.wait_recv()

    extra = jnp.sum(extras_ref[...], axis=0)
    norm_squares = extra[:HEAD_AT] * extra[:HEAD_AT]
    square_all = jnp.sum(squares_ref[...]) + jnp.sum(low_squares_ref[...]) + jnp.sum(norm_squares)
    count_all = extra[12:13, 1:2]
    grad_norm = jnp.sqrt(jnp.zeros((1, 1), jnp.float32) + square_all) / count_all
    factor = CLIP_MAX / jnp.maximum(grad_norm, CLIP_MAX) / count_all
    summary_ref[...] = extra
    summary_ref[10:12, :] = extra[10:12] * factor
    summary_ref[13:14, :] = jnp.broadcast_to(grad_norm, (1, D))

    flat_start = (z * 2 + x) * (2 * half_rows)
    layer_start = BLOCK + SEQ + 1

    def step(index):
        slot = index % 2
        for copy in loads(index):
            copy.wait()

        @pl.loop(0, piece // 16)
        def _(block):
            at = pl.multiple_of(block * 16, 16)
            rows = pl.ds(at, 16)
            longer = own[slot, pl.ds(at, 32), :].astype(jnp.float32)
            flat = flat_start + row_at(index) + at + lax.broadcasted_iota(jnp.int32, (16, D), 0)
            grads = jnp.where(flat < layer_start, longer[:16], longer[SPARE : SPARE + 16])
            spared = jnp.where(flat < layer_start, flat, flat + SPARE)
            grads = jnp.where(dense_row(spared), grads, rest[slot, rows, :].astype(jnp.float32))
            clipped = grads * factor
            moment_one = BETA_ONE * first[slot, rows, :] + (1.0 - BETA_ONE) * clipped
            moment_two = BETA_TWO * second[slot, rows, :] + (1.0 - BETA_TWO) * clipped * clipped
            new_first[slot, rows, :] = moment_one
            new_second[slot, rows, :] = moment_two
            corrected_one = moment_one * (1.0 / (1.0 - BETA_ONE**STEP))
            corrected_two = moment_two * (1.0 / (1.0 - BETA_TWO**STEP))
            change = corrected_one / (jnp.sqrt(corrected_two) + ADAM_EPS) + DECAY * weights[slot, rows, :]
            change = low(RATE * change)
            left, right = change[:, :half_cols], change[:, half_cols:]
            mine[index, rows, :] = jnp.where(c == 0, left, right)
            other[index, rows, :] = jnp.where(c == 0, right, left)

        for copy in stores(index):
            copy.start()
        pltpu.make_async_remote_copy(
            src_ref=other.at[index],
            dst_ref=core_in.at[index],
            send_sem=sends.at[index],
            recv_sem=recvs.at[index],
            device_id=sibling,
            device_id_type=MESH,
        ).start()

    def fold(index):
        pltpu.make_async_copy(core_in.at[index], core_in.at[index], recvs.at[index]).wait()
        total = mine[index].astype(jnp.float32) + core_in[index].astype(jnp.float32)
        if index < pieces:
            y_out[index] = low(total)
            pltpu.make_async_remote_copy(
                src_ref=y_out.at[index],
                dst_ref=y_in.at[index],
                send_sem=sends.at[2 * pieces + index],
                recv_sem=recvs.at[2 * pieces + index],
                device_id=over_y,
                device_id_type=MESH,
            ).start()
        else:
            mine[index] = low(total)

    steps = 2 * pieces
    for index in range(steps):
        if index + 1 < steps:
            if index >= 1:
                for copy in stores(index - 1):
                    copy.wait()
            for copy in loads(index + 1):
                copy.start()
        if index >= 1:
            fold(index - 1)
        step(index)
    fold(steps - 1)

    def hand_over(index):
        rows = pl.ds(index * piece, piece)
        return pltpu.make_async_copy(mine.at[pieces + index], total_out.at[rows], total_sem.at[index])

    for index in range(pieces):
        at = 2 * pieces + index
        pltpu.make_async_copy(y_in.at[index], y_in.at[index], recvs.at[at]).wait()
        total = mine[pieces + index].astype(jnp.float32) + y_in[index].astype(jnp.float32)
        mine[pieces + index] = low(total)
        hand_over(index).start()
    for index in range(steps - 2, steps):
        for copy in stores(index):
            copy.wait()
    for index in range(steps):
        pltpu.make_async_copy(other.at[index], other.at[index], sends.at[index]).wait()
    for index in range(pieces):
        pltpu.make_async_copy(y_out.at[index], y_out.at[index], sends.at[steps + index]).wait()
        hand_over(index).wait()

    @pl.when(has_factors)
    def _():
        to_low.wait_send()


def update_rows(own, rest, master, first, second, factors, extras, squares):
    rows, width = master.shape
    half_rows, half_cols = rows // 2, width // 2
    pieces = 3
    piece = half_rows // pieces
    f32, bf16 = jnp.float32, jnp.bfloat16
    hbm = pl.BlockSpec(memory_space=pl.ANY)
    vmem = pl.BlockSpec(memory_space=pltpu.VMEM)
    return pl.pallas_call(
        functools.partial(update_kernel, (half_rows, piece, pieces, low_plane(rows))),
        out_shape=(
            jax.ShapeDtypeStruct((rows, width), f32),
            jax.ShapeDtypeStruct((rows, width), f32),
            jax.ShapeDtypeStruct((half_rows, half_cols), bf16),
            jax.ShapeDtypeStruct((16, width), f32),
        ),
        in_specs=[hbm] * 5 + [vmem] * 3,
        out_specs=[hbm] * 3 + [vmem],
        scratch_shapes=[
            pltpu.VMEM((2, piece + 16, width), bf16),
            pltpu.VMEM((2, piece, width), bf16),
            pltpu.VMEM((2, piece, width), f32),
            pltpu.VMEM((2, piece, width), f32),
            pltpu.VMEM((2, piece, width), f32),
            pltpu.VMEM((2, piece, width), f32),
            pltpu.VMEM((2, piece, width), f32),
            pltpu.VMEM((2 * pieces, piece, half_cols), bf16),
            pltpu.VMEM((2 * pieces, piece, half_cols), bf16),
            pltpu.VMEM((2 * pieces, piece, half_cols), bf16),
            pltpu.VMEM((pieces, piece, half_cols), bf16),
            pltpu.VMEM((pieces, piece, half_cols), bf16),
            pltpu.SemaphoreType.DMA((5, 2)),
            pltpu.SemaphoreType.DMA((2, 2)),
            pltpu.SemaphoreType.DMA((3 * pieces,)),
            pltpu.SemaphoreType.DMA((3 * pieces,)),
            pltpu.SemaphoreType.DMA((pieces,)),
            pltpu.VMEM((8, 128), f32),
            pltpu.SemaphoreType.DMA((2,)),
        ],
        compiler_params=pltpu.CompilerParams(
            collective_id=3, has_side_effects=True, vmem_limit_bytes=48 * 2**20
        ),
        name="update",
    )(own, rest, master, first, second, factors, extras, squares)


def pairs_of(partner):
    pairs = []
    for source in range(32):
        y, c, z, x = source // 16, source // 8 % 2, source // 2 % 4, source % 2
        target = partner(y, c, z, x)
        if target is not None:
            pairs.append((source, (target[0] * 2 + target[1]) * 8 + target[2] * 2 + target[3]))
    return pairs


def next_half(y, c, z, x):
    place_in_row = (z * 2 + x) * 2 + y + 1
    if place_in_row == 16:
        return None
    return (place_in_row % 2, c, place_in_row // 4, place_in_row // 2 % 2)


def on_grid_step(grad_rows, factors, extra, master, outer_momentum, first, second):
    rows, width = master.shape
    half_rows, half_cols = rows // 2, width // 2
    y, c, z, x = place()
    rank = lax.axis_index("dp")
    own, factors, extras, squares = sum_on_plane(grad_rows, factors, extra, rows)
    following = lax.ppermute(own[:16], "dp", [(source, source - 1) for source in range(1, 8)])
    own = lax.dynamic_update_slice(own, following, (rows, 0))
    rest = low_rank_rows(factors, jnp.sum(extras, axis=0), rank * rows + SPARE, rows)
    first, second, total, summary = update_rows(
        own, rest.astype(jnp.bfloat16), master, first, second, factors, extras, squares
    )
    groups = lax.axis_size("group")
    at = (y * half_rows, c * half_cols)
    quarter = [lax.dynamic_slice(whole, at, (half_rows, half_cols)) for whole in (master, outer_momentum)]
    part, _ = nesterov(*quarter, total.astype(jnp.float32) / groups)
    before = lax.ppermute(part[-16:], ("group", "dp"), pairs_of(next_half))
    moved = jnp.concatenate([before, part], axis=0)[16 - SPARE :][:half_rows]
    flat_row = rank * rows + y * half_rows + lax.broadcasted_iota(jnp.int32, (half_rows, 1), 0)
    part = jnp.where(flat_row < layout_rows()[1], part, moved).astype(jnp.bfloat16)
    soup_rows = gather_rows(part, rows)
    total, soup_rows = lax.optimization_barrier((total, soup_rows))
    over_y = lax.ppermute(total, ("group", "dp"), pairs_of(lambda y, c, z, x: (1 - y, c, z, x)))

    def finish(over_y):
        column = jnp.where(y == 0, jnp.stack([total, over_y]), jnp.stack([over_y, total]))
        column = column.reshape(rows, half_cols)
        sibling = lax.ppermute(
            column, ("group", "dp"), pairs_of(lambda y, c, z, x: (y, 1 - c, z, x))
        )
        whole = jnp.where(
            c == 0,
            jnp.concatenate([column, sibling], axis=1),
            jnp.concatenate([sibling, column], axis=1),
        )
        return nesterov(master, outer_momentum, whole.astype(jnp.float32) / groups)

    return (over_y, finish, first, second, summary, soup_rows)


def fetch_weights(params, pixel_rows=None, notes=None):
    rows, width = params.shape
    ranks, rank = lax.axis_size("dp"), lax.axis_index("dp")
    before = lax.ppermute(params[-16:], "dp", [(source, source + 1) for source in range(ranks - 1)])
    longer = jnp.concatenate([before, params], axis=0)
    in_place = lax.broadcasted_iota(jnp.int32, (rows, 1), 0) + rank * rows < layout_rows()[1]
    if not on_grid():
        moved = jnp.where(in_place, params, longer[16 - SPARE :][:rows])
        full = lax.all_gather(moved.astype(jnp.bfloat16), "dp", axis=0, tiled=True)
        return full if pixel_rows is None else (full, pixel_rows, notes)
    y, c, _, _ = place()
    half, half_cols = rows // 2, width // 2
    part = lax.dynamic_slice(params, (y * half, c * half_cols), (half, half_cols))
    moved = lax.dynamic_slice(longer, (y * half + 16 - SPARE, c * half_cols), (half, half_cols))
    in_place = lax.dynamic_slice(in_place, (y * half, 0), (half, 1))
    return gather_rows(jnp.where(in_place, part, moved).astype(jnp.bfloat16), rows, pixel_rows, notes)


def low_rank_rows(factors, extra, first_row, count):
    last_layer = FIRST_LAYER + 4 * D + 2 * FF
    devices = factors.shape[0]

    def half(at, width, which):
        piece = factors[:, 8 * which : 8 * which + 8, at : at + width]
        return piece.reshape(devices * 8, width)

    norms = extra[:16].astype(jnp.bfloat16)
    sections = [
        (last_layer, half(FF, D, 0), half(FF + D, D, 0)),
        (last_layer + 3 * D, half(FF, D, 1), half(FF + D, D, 1)),
        (last_layer + 4 * D, half(0, FF, 0), half(FF + 2 * D, D, 0)),
        (last_layer + 4 * D + FF, half(0, FF, 1), half(FF + 2 * D, D, 1)),
        (TAIL_START, jnp.eye(16, HEAD_AT, dtype=jnp.bfloat16), norms),
        (TAIL_START + HEAD_AT, half(FF + 3 * D, EMB, 0), half(FF + 3 * D, D, 1)),
    ]
    row = first_row + jnp.arange(count)
    lefts, rights = [], []
    for start, left, right in sections:
        width = left.shape[1]
        padded = jnp.pad(left, ((0, 0), (count, count)))
        at = jnp.clip(first_row - start + count, 0, width + count)
        window = lax.dynamic_slice(padded, (0, at), (left.shape[0], count))
        inside = (row >= start) & (row < start + width)
        lefts.append(jnp.where(inside[None], window, jnp.zeros_like(window)))
        rights.append(right)
    return lax.dot_general(
        jnp.concatenate(lefts, axis=0),
        jnp.concatenate(rights, axis=0),
        (((0,), (0,)), ((), ())),
        preferred_element_type=jnp.float32,
    )


def reduce_rows(grad_rows, factors, extra, count):
    ranks, rank = lax.axis_size("dp"), lax.axis_index("dp")
    flat_row = rank * count + lax.broadcasted_iota(jnp.int32, (count, 1), 0)
    rest = low_rank_rows(factors[None], extra, 0, ranks * count).astype(jnp.bfloat16)
    whole = jnp.where(dense_row(jnp.arange(DENSE_END))[:, None], grad_rows, rest[:DENSE_END])
    whole = jnp.concatenate([whole, rest[DENSE_END:]], axis=0)
    shard = lax.psum_scatter(whole, "dp", scatter_dimension=0, tiled=True)
    following = lax.ppermute(shard[:16], "dp", [(source, source - 1) for source in range(1, ranks)])
    shifted = jnp.concatenate([shard[SPARE:], following[:SPARE]], axis=0)
    summed = jnp.where(flat_row < layout_rows()[1], shard, shifted).astype(jnp.float32)
    return (summed, lax.psum(extra, "dp"))


def any_grid_step(grad_rows, factors, extra, master, outer_momentum, first, second):
    reduced, extra = reduce_rows(grad_rows, factors, extra, master.shape[0])
    count_all = extra[12, 1]
    grad_norm = jnp.sqrt(lax.psum(jnp.sum(reduced * reduced), "dp")) / count_all
    factor = CLIP_MAX / jnp.maximum(grad_norm, CLIP_MAX) / count_all
    params, first, second = adam_update(master, first, second, reduced * factor, STEP)
    delta = (master - params).astype(jnp.bfloat16)
    mean_delta = lax.psum(delta, "group").astype(jnp.float32) / lax.axis_size("group")
    outer = nesterov(master, outer_momentum, mean_delta)
    summary = jnp.concatenate(
        [extra[:10], extra[10:12] * factor, extra[12:13], jnp.full((3, D), grad_norm)], axis=0
    )
    return (outer, lambda done: done, first, second, summary, fetch_weights(outer[0]))


def dense_row(row):
    last_layer = FIRST_LAYER + 4 * D + 2 * FF
    return (row < last_layer) | ((row >= last_layer + D) & (row < DENSE_END))


def adam_update(params, moment_one, moment_two, clipped, step_number):
    moment_one = BETA_ONE * moment_one + (1.0 - BETA_ONE) * clipped
    moment_two = BETA_TWO * moment_two + (1.0 - BETA_TWO) * clipped * clipped
    corrected_one = moment_one / (1.0 - BETA_ONE**step_number)
    corrected_two = moment_two / (1.0 - BETA_TWO**step_number)
    params = params - RATE * (corrected_one / (jnp.sqrt(corrected_two) + ADAM_EPS) + DECAY * params)
    return (params, moment_one, moment_two)


def nesterov(master_rows, momentum_rows, mean_delta):
    momentum_next = OUTER_MOM * momentum_rows + mean_delta
    return (master_rows - OUTER_RATE * (mean_delta + OUTER_MOM * momentum_next), momentum_next)


def token_rows(pixel_block):
    images, patches, _ = pixel_block.shape
    padded = jnp.pad(pixel_block, ((0, 0), (0, TOKENS - patches), (0, 0)))
    return padded.reshape(images * TOKENS, PATCH_IN)


def per_device(
    pixels,
    counts,
    labels,
    text,
    master,
    outer_momentum,
    first_moment,
    second_moment,
    eval_pixels,
    eval_counts,
    eval_labels,
):
    slots = pixels.shape[2]
    live = (jnp.arange(slots)[None, :] < counts[0]).astype(jnp.float32).reshape(-1)
    step_labels = labels[0].reshape(-1)
    step_pixels = token_rows(pixels[0].reshape((-1,) + pixels.shape[3:]))
    notes = image_notes(step_labels, live)
    weights, step_pixels, notes = fetch_weights(master, step_pixels, notes)
    grad_rows, factors, extra = run_tower(weights, step_pixels, notes, text, True)
    step = on_grid_step if on_grid() else any_grid_step
    waiting, finish, moment_one, moment_two, summary, soup_rows = step(
        grad_rows, factors, extra, master, outer_momentum, first_moment[0], second_moment[0]
    )
    eval_live = (jnp.arange(eval_pixels.shape[0]) < eval_counts[0]).astype(jnp.float32)
    eval_notes = image_notes(eval_labels, eval_live)
    carried = (moment_one, moment_two) if on_grid() else ()
    eval_tile, *carried = run_tower(
        soup_rows, token_rows(eval_pixels), eval_notes, text, False, carried
    )
    if on_grid():
        moment_one, moment_two = carried
    eval_tile, waiting = lax.optimization_barrier((eval_tile, waiting))
    new_master, new_outer = finish(waiting)
    eval_losses = eval_tile[: eval_labels.shape[0], 0]
    return (
        new_master,
        new_outer,
        moment_one[None],
        moment_two[None],
        summary[13:14, :1],
        summary[12:13, :1],
        summary[12:13, 1:2],
        summary[10:12][None, None],
        eval_losses,
    )


def solution(mesh):
    return jax.shard_map(
        per_device,
        mesh=mesh,
        in_specs=(
            P(None, None, ("group", "dp"), None, None),
            P(None, None, ("group", "dp")),
            P(None, None, ("group", "dp")),
            P(),
            P("dp", None),
            P("dp", None),
            P("group", "dp", None),
            P("group", "dp", None),
            P(("group", "dp"), None, None),
            P(("group", "dp")),
            P(("group", "dp")),
        ),
        out_specs=(
            P("dp", None),
            P("dp", None),
            P("group", "dp", None),
            P("group", "dp", None),
            P("group", None),
            P("group", None),
            P("group", None),
            P("group", None, None, None),
            P(("group", "dp")),
        ),
        check_vma=False,
    )
```
